32 devices in a mesh: wide: 16 (over z, y, x), narrow: 2 (over core).
Axes of the slice: x: 2, y: 2, z: 4, core: 2. Of those that a mesh axis runs over, the one named last changes fastest.
Arguments:
- tokens: bfloat16 [8192, 1024], P(('wide', 'narrow')), may hold values from -6 to 6
- seq_lens: int32 [16, 1], P('wide'), may hold values from 1 to 512, as said below
- decay_rate: float32 [8], replicated, may hold values from 0.0001 to 0.03
- w_query: bfloat16 [1024, 1024], replicated, may hold values from -0.1875 to 0.1875
- w_key: bfloat16 [1024, 1024], replicated, may hold values from -0.1875 to 0.1875
- w_value: bfloat16 [1024, 1024], replicated, may hold values from -0.1875 to 0.1875
- w_gate_u: bfloat16 [1024, 1024], replicated, may hold values from -0.1875 to 0.1875
- w_out: bfloat16 [1024, 1024], replicated, may hold values from -0.1875 to 0.1875
- w_left: bfloat16 [1024, 2816], P(None, 'narrow'), may hold values from -0.1875 to 0.1875
- w_right: bfloat16 [1024, 2816], P(None, 'narrow'), may hold values from -0.1875 to 0.1875
- w_down: bfloat16 [2816, 1024], P('narrow'), may hold values from -0.109375 to 0.109375
- cotangent: bfloat16 [8192, 1024], P(('wide', 'narrow')), may hold values from -6 to 6
Outputs:
- mixed: bfloat16 [8192, 1024], P(('wide', 'narrow'))
- input_grad: float32 [8192, 1024], P(('wide', 'narrow'))
- grad_query: float32 [1024, 1024], P('wide')
- grad_key: float32 [1024, 1024], P('wide')
- grad_value: float32 [1024, 1024], P('wide')
- grad_gate_u: float32 [1024, 1024], P('wide')
- grad_out: float32 [1024, 1024], P('wide')
- grad_left: float32 [1024, 2816], P('wide', 'narrow')
- grad_right: float32 [1024, 2816], P('wide', 'narrow')
- grad_down: float32 [2816, 1024], P('narrow', 'wide')
The draws below stay inside these ranges and needn't reach their ends.
Inputs may be any that keep to these rules, and one draw needn't show every extreme that they name: `seq_lens`: row g holds the lengths of the 1 sequence of group g; padded to whole blocks of 256 rows they add up to at most 512.
All inputs are finite; a program needn't handle non-finite values.
Results may differ from the reference program's by a relative error of at most 0.013.
Values may be sent and summed in bfloat16 or wider, within the bound.
No kernel may reach another device: no remote copies, remote signals or barrier semaphores. Data moves between devices by JAX's collectives and lax.ppermute only.
A program may use at most 192 MiB of HBM per device.

```python
import math
import jax
import jax.numpy as jnp
from jax import lax

D = 1024
HEADS = 8
HEAD_DIM = 128
FF = 2816
BLOCK = 256
BLK_DEV = 1
SEQ_GRP = 1
ROWS = 256
TOKENS = 8192
N_WIDE = 16
N_NARROW = 2


def draw_seq_lens(key, part):
    key = jax.random.fold_in(key, 11)
    key_short, key_long, key_pick, key_slot = jax.random.split(key, 4)
    shortest = jax.random.randint(key_short, (N_WIDE, SEQ_GRP), 1, BLOCK + 1)
    least_long = BLK_DEV * BLOCK + 1
    most_long = (2 * BLK_DEV - SEQ_GRP + 1) * BLOCK
    longest = jax.random.randint(key_long, (N_WIDE,), least_long, most_long + 1)
    chosen = jax.random.randint(key_pick, (), 0, N_WIDE)
    longest = jnp.where(jnp.arange(N_WIDE) == chosen, most_long, longest)
    slot = jax.random.randint(key_slot, (N_WIDE,), 0, SEQ_GRP)
    lengths = jnp.where(jnp.arange(SEQ_GRP)[None, :] == slot[:, None], longest[:, None], shortest)
    return lengths.astype(jnp.int32)


def raised(values, stream_key, source, target, blocks, factor):
    def block_of(dim):
        return (jnp.arange(values.shape[dim]) // (values.shape[dim] // blocks)).reshape((-1,) + (1,) * (values.ndim - 1 - dim))

    near = jax.random.permutation(stream_key, blocks)[block_of(target)]
    second = (block_of(target) + blocks // 2) % blocks
    return jnp.where((block_of(source) == near) | (block_of(source) == second), factor * values, values)


def shard_levels(key, dims, pieces, least, high):
    def one(axis_at, parts):
        steps = jax.random.uniform(jax.random.fold_in(jax.random.fold_in(key, 6), axis_at), (parts,), jnp.float32, least / len(pieces), high / len(pieces))
        return jnp.repeat(jnp.exp(steps), dims[axis_at] // parts).reshape((-1,) + (1,) * (len(dims) - axis_at - 1))

    loudness = one(*pieces[0])
    for cut in pieces[1:]:
        loudness = loudness * one(*cut)
    return loudness


def bell_draw(key, shape, width, reach, pieces=(), kind=jnp.bfloat16):
    gain = shard_levels(key, shape, pieces, -0.22, 0.18) if pieces else 1.0
    array = jax.random.normal(key, shape, jnp.float32) * width * gain
    return jnp.minimum(jnp.maximum(array, -reach), reach).astype(kind)


def bell_draw_with(rng, dims, deviation, limit, cuts, heavy, kind=jnp.bfloat16):
    drawn = deviation * jax.random.normal(rng, dims, jnp.float32)
    if cuts:
        drawn = drawn * shard_levels(rng, dims, cuts, -0.22, 0.18)
    return jnp.clip(raised(drawn, jax.random.fold_in(rng, 3), *heavy), -limit, limit).astype(kind)


def setup_inputs(seed: int = 0) -> dict:
    splits = jax.random.split(jax.random.key(seed), 13)
    return {
        "tokens": bell_draw_with(splits[0], (TOKENS, D), 1.0, 6.0, ((0, 32),), (0, 1, 32, 2.75)),
        "seq_lens": draw_seq_lens(jax.random.fold_in(splits[12], 71), 0),
        "decay_rate": jnp.clip(jnp.exp(jax.random.uniform(splits[2], (HEADS,), jnp.float32, math.log(0.0001), math.log(0.03))), 0.0001, 0.03),
        "w_query": bell_draw(splits[3], (D, D), D ** -0.5, 0.1875),
        "w_key": bell_draw(splits[4], (D, D), D ** -0.5, 0.1875),
        "w_value": bell_draw(splits[5], (D, D), D ** -0.5, 0.1875),
        "w_gate_u": bell_draw(splits[6], (D, D), D ** -0.5, 0.1875),
        "w_out": bell_draw(splits[7], (D, D), D ** -0.5, 0.1875),
        "w_left": bell_draw(splits[8], (D, FF), D ** -0.5, 0.1875, ((1, 2),)),
        "w_right": bell_draw(splits[9], (D, FF), D ** -0.5, 0.1875, ((1, 2),)),
        "w_down": bell_draw(splits[10], (FF, D), FF ** -0.5, 0.109375, ((0, 2),)),
        "cotangent": bell_draw(splits[11], (TOKENS, D), 1.0, 6.0, ((0, 32),)),
    }


EPSILON = 1e-06

@jax.custom_vjp
def low(v):
    return lax.optimization_barrier(v.astype(jnp.bfloat16)).astype(jnp.float32)

@jax.custom_vjp
def low_back(v):
    return v

def low_keep(v):
    return (low(v), None)

def low_pass(kept, grad):
    return (grad,)

def back_keep(v):
    return (v, None)

def back_low(kept, grad):
    return (low(grad),)
low.defvjp(low_keep, low_pass)
low_back.defvjp(back_keep, back_low)

def matmul(left_side, right_side):
    return jnp.dot(left_side, right_side, precision=lax.Precision.HIGHEST)

def rms_scaled(values):
    return values * lax.rsqrt(lax.optimization_barrier(jnp.mean(values * values, axis=-1, keepdims=True)) + EPSILON)

def layout(lengths, first_row, row_count, block_rows):
    padded = (lengths + block_rows - 1) // block_rows * block_rows
    ends = jnp.cumsum(padded).astype(jnp.int32)
    starts = (ends - padded).astype(jnp.int32)
    positions = (first_row + jnp.arange(row_count, dtype=jnp.int32)).astype(jnp.int32)
    sequence = lax.optimization_barrier(jnp.sum((positions[:, None] >= ends[None, :]).astype(jnp.int32), axis=1)).astype(jnp.int32)
    slots = jnp.arange(lengths.shape[0], dtype=jnp.int32)
    member = (sequence[:, None] == slots[None, :]).astype(jnp.int32)
    row_start = lax.optimization_barrier(jnp.sum(member * starts[None, :], axis=1)).astype(jnp.int32)
    row_length = lax.optimization_barrier(jnp.sum(member * lengths[None, :], axis=1)).astype(jnp.int32)
    offset = positions - row_start
    inside = sequence < lengths.shape[0]
    usable = jnp.logical_and(inside, offset < row_length)
    fresh = jnp.logical_not(jnp.logical_and(inside, offset > 0))
    return (usable, fresh, sequence)

def attend(queries, keys, values, decay_rate, fresh_blocks):
    group_rows = queries.shape[0]
    block_count = group_rows // BLOCK
    block_shape = (block_count, BLOCK, HEADS, HEAD_DIM)
    query_blocks = queries.reshape(block_shape)
    key_blocks = keys.reshape(block_shape)
    value_blocks = values.reshape(block_shape)
    steps = jnp.arange(BLOCK).astype(queries.dtype)
    spacing = steps[:, None] - steps[None, :]
    decay_mask = jnp.where(spacing[None] >= 0, jnp.exp(-decay_rate[:, None, None] * jnp.maximum(spacing, 0.0)[None]), 0.0)
    scores = jnp.einsum('nihe,njhe->nhij', query_blocks, key_blocks, precision=lax.Precision.HIGHEST)
    weighted = low(low_back(scores) * decay_mask[None])
    within = jnp.einsum('nhij,njhe->nihe', weighted, value_blocks, precision=lax.Precision.HIGHEST)
    query_decay = jnp.exp(-decay_rate[None, :] * (steps[:, None] + 1.0))
    key_decay = jnp.exp(-decay_rate[None, :] * (BLOCK - 1.0 - steps[:, None]))
    block_states = jnp.einsum('njhe,njhf->nhef', key_blocks * key_decay[None, :, :, None], value_blocks, precision=lax.Precision.HIGHEST)
    carry_rate = jnp.exp(-decay_rate * BLOCK)

    def advance(state, item):
        block_state, reset = item
        prior = jnp.where(reset, 0.0, state)
        return (carry_rate[:, None, None] * prior + block_state, prior)
    _, priors = lax.scan(advance, jnp.zeros_like(block_states[0]), (block_states, fresh_blocks))
    across = jnp.einsum('nihe,nhef->nihf', query_blocks * query_decay[None, :, :, None], priors, precision=lax.Precision.HIGHEST)
    return (within + across).reshape(group_rows, D)

def group_forward(inputs, w_query, w_key, w_value, w_gate_u, w_out, w_left, w_right, w_down, decay_rate, valid, fresh_blocks):
    normed_in = low(rms_scaled(inputs))
    query_pre = low_back(matmul(normed_in, w_query))
    key_pre = low_back(matmul(normed_in, w_key))
    value_pre = low_back(matmul(normed_in, w_value))
    gate_pre = low_back(matmul(normed_in, w_gate_u))
    queries = low(jax.nn.silu(query_pre))
    keys = low(jax.nn.silu(key_pre) * valid)
    values = low(value_pre * valid)
    gate_u = jax.nn.silu(gate_pre)
    attended = low_back(attend(queries, keys, values, decay_rate, fresh_blocks))
    gated = low(rms_scaled(attended) * gate_u)
    branch = low_back(matmul(gated, w_out))
    hidden_res = inputs + valid * branch
    normed_mid = low(rms_scaled(hidden_res))
    left_part = low_back(matmul(normed_mid, w_left))
    right_part = low_back(matmul(normed_mid, w_right))
    joined = low(left_part * right_part)
    ffn_out = low_back(matmul(joined, w_down))
    return hidden_res + valid * ffn_out

def reference(tokens, seq_lens, decay_rate, w_query, w_key, w_value, w_gate_u, w_out, w_left, w_right, w_down, cotangent):
    group_rows = ROWS * N_NARROW
    weights = (w_query.astype(jnp.float32), w_key.astype(jnp.float32), w_value.astype(jnp.float32), w_gate_u.astype(jnp.float32), w_out.astype(jnp.float32), w_left.astype(jnp.float32), w_right.astype(jnp.float32), w_down.astype(jnp.float32))
    inputs_all = tokens.astype(jnp.float32).reshape(N_WIDE, group_rows, D)
    upstream_all = cotangent.astype(jnp.float32).reshape(N_WIDE, group_rows, D)

    def one_group(totals, item):
        inputs, upstream, lengths = item
        usable, fresh, sequence = layout(lengths, 0, group_rows, BLOCK)
        valid = usable.astype(inputs.dtype)[:, None]
        fresh_blocks = fresh.reshape(group_rows // BLOCK, BLOCK)[:, 0]

        def forward(inputs, wq_f, wk_f, wv_f, wu_f, wo_f, wl_f, wr_f, wd_f):
            return group_forward(inputs, wq_f, wk_f, wv_f, wu_f, wo_f, wl_f, wr_f, wd_f, decay_rate, valid, fresh_blocks)
        output, pullback = jax.vjp(forward, inputs, *weights)
        grads = pullback(upstream)
        updated = tuple((total + grad for total, grad in zip(totals, grads[1:])))
        return (updated, (output.astype(jnp.bfloat16), grads[0]))
    initial = tuple((jnp.zeros_like(weight) for weight in weights))
    totals, (outputs, input_grads) = lax.scan(one_group, initial, (inputs_all, upstream_all, seq_lens))
    return (outputs.reshape(TOKENS, D), input_grads.reshape(TOKENS, D), totals[0], totals[1], totals[2], totals[3], totals[4], totals[5], totals[6], totals[7])
```

```python
import functools

import jax
import jax.numpy as jnp
from jax import lax
from jax.experimental import pallas as pl
from jax.experimental.pallas import tpu as pltpu
from jax.sharding import PartitionSpec as P

BLOCK = 256
EPSILON = 1e-06
F32 = jnp.float32
BF16 = jnp.bfloat16


def plain(a, b):
    return jnp.dot(a, b, preferred_element_type=F32)


def against(a, b):
    return lax.dot_general(a, b, (((1,), (1,)), ((), ())), preferred_element_type=F32)


def outer(a, b):
    return lax.dot_general(a, b, (((0,), (0,)), ((), ())), preferred_element_type=F32)


def column_tiles(count, tile, body):
    whole = count // tile

    if whole:

        @pl.loop(0, whole)
        def _(i):
            body(pl.multiple_of(i * tile, tile), tile)

    if count - whole * tile:
        body(whole * tile, count - whole * tile)


def row_mean(v):
    return jnp.mean(v, axis=-1, keepdims=True)


def valid_rows(scalars, half, rows):
    c, length = scalars[0], scalars[2]
    first = rows * (c if half == 0 else 1 - c)
    return (first + lax.broadcasted_iota(jnp.int32, (rows, 1), 0) < length).astype(F32)


def decays(rate, n):
    i = lax.broadcasted_iota(jnp.int32, (n, n), 0)
    j = lax.broadcasted_iota(jnp.int32, (n, n), 1)
    gap = (i - j).astype(F32)
    mask = jnp.where(gap >= 0, jnp.exp(-rate * jnp.maximum(gap, 0.0)), 0.0)
    step = lax.broadcasted_iota(jnp.int32, (n, 1), 0).astype(F32)
    return mask, jnp.exp(-rate * (step + 1.0)), jnp.exp(-rate * (n - 1.0 - step))


def attention_forward(
    scalars, rates, tok_own, tok_other, w_query, w_key, w_value, w_gate,
    nin, q_out, k_out, v_out, dq_out, dk_out, gu_out, dg_out, att_out, u_out, prior_out,
    gate_buf,
):
    rows = tok_own.shape[0]
    cols = q_out.shape[1]
    c = scalars[0]
    valid = []
    for half, tok in enumerate((tok_own, tok_other)):
        x = tok[...].astype(F32)
        nin[half * rows : (half + 1) * rows, :] = (
            x * lax.rsqrt(row_mean(x * x) + EPSILON)
        ).astype(BF16)
        valid.append(valid_rows(scalars, half, rows))
    for half in (0, 1):
        part = slice(half * rows, (half + 1) * rows)
        ok = valid[half]
        for start in range(0, cols, BLOCK):
            at = slice(start, start + BLOCK)
            normed = nin[part, :]
            pre = plain(normed, w_query[:, at])
            sig = jax.nn.sigmoid(pre)
            act = pre * sig
            q_out[part, at] = act.astype(BF16)
            dq_out[part, at] = (sig + act * (1.0 - sig)).astype(BF16)
            pre = plain(normed, w_key[:, at])
            sig = jax.nn.sigmoid(pre)
            act = pre * sig
            k_out[part, at] = (act * ok).astype(BF16)
            dk_out[part, at] = ((sig + act * (1.0 - sig)) * ok).astype(BF16)
            v_out[part, at] = (plain(normed, w_value[:, at]) * ok).astype(BF16)
            pre = plain(normed, w_gate[:, at])
            sig = jax.nn.sigmoid(pre)
            act = pre * sig
            gate_buf[part, at] = act
            gu_out[part, at] = act.astype(BF16)
            dg_out[part, at] = (sig + act * (1.0 - sig)).astype(BF16)
    size = prior_out.shape[1]
    heads = prior_out.shape[0]
    carried = (scalars[2] > rows).astype(F32)
    first = pl.ds(pl.multiple_of(c * rows, rows), rows)
    second = pl.ds(pl.multiple_of((1 - c) * rows, rows), rows)
    squares = [jnp.zeros((rows, 1), F32), jnp.zeros((rows, 1), F32)]
    for h in range(heads):
        at = slice(h * size, (h + 1) * size)
        mask, query_decay, key_decay = decays(rates[c * heads + h], rows)
        wide = (k_out[first, at].astype(F32) * key_decay).astype(BF16)
        prior = (outer(wide, v_out[first, at]) * carried).astype(BF16)
        prior_out[h] = prior
        for b, part in enumerate((first, second)):
            q = q_out[part, at]
            weighted = (against(q, k_out[part, at]) * mask).astype(BF16)
            att = plain(weighted, v_out[part, at])
            if b == 1:
                att = att + plain(q, prior) * query_decay
            att_out[part, at] = att.astype(BF16)
            u_out[part, at] = (att * gate_buf[part, at]).astype(BF16)
            squares[b] = squares[b] + jnp.sum(att * att, axis=-1, keepdims=True)
    lane = lax.broadcasted_iota(jnp.int32, (rows, 128), 1)
    for b, part in enumerate((first, second)):
        high = squares[b].astype(BF16).astype(F32)
        low = squares[b] - high
        u_out[part, cols:] = jnp.where(lane < 64, high, low).astype(BF16)


def feed_forward(
    scalars, tok_own, tok_other, u_own, u_other, w_out, w_left, w_right, w_down, cot_own, cot_other,
    nm, joined, d_left, d_right, d_ffn, branch_out, scale_out,
):
    rows, width = tok_own.shape
    cols = u_own.shape[1] - 128
    c = scalars[0]
    own = pl.ds(pl.multiple_of(c * cols, cols), cols)
    other = pl.ds(pl.multiple_of((1 - c) * cols, cols), cols)
    for half in (0, 1):
        part = slice(half * rows, (half + 1) * rows)
        swap = slice((1 - half) * rows, (2 - half) * rows)
        total = jnp.zeros((rows, 1), F32)
        for lane in (0, 64):
            total = total + u_own[part, cols + lane : cols + lane + 1].astype(F32)
            total = total + u_other[swap, cols + lane : cols + lane + 1].astype(F32)
        scale = lax.rsqrt(total / width + EPSILON)
        scale_out[part, :] = jnp.broadcast_to(scale, (rows, 128))
        branch = scale * (
            plain(u_own[part, :cols], w_out[own, :]) + plain(u_other[swap, :cols], w_out[other, :])
        )
        branch_out[part, :] = branch.astype(BF16)
        ok = valid_rows(scalars, half, rows)
        hidden = (tok_own, tok_other)[half][...].astype(F32) + ok * branch
        nm[part, :] = (hidden * lax.rsqrt(row_mean(hidden * hidden) + EPSILON)).astype(BF16)
        cot = (cot_own, cot_other)[half][...].astype(F32)
        d_ffn[part, :] = (cot * ok).astype(BF16)

    def body(start, count):
        at = pl.ds(start, count)
        left = plain(nm[...], w_left[:, at])
        right = plain(nm[...], w_right[:, at])
        joined[:, at] = (left * right).astype(BF16)
        d_joined = against(d_ffn[...], w_down[at, :])
        d_left[:, at] = (d_joined * right).astype(BF16)
        d_right[:, at] = (d_joined * left).astype(BF16)

    column_tiles(w_left.shape[1], 256, body)


def place_rows(wide, dims, pos, count):
    mask = 0
    for k, d in enumerate(dims):
        if pos >> (len(dims) - 1 - k) & 1:
            mask |= 1 << d
    return wide ^ mask


def transposed_rows(scalars, source, target, dims, first=0):
    n = 1 << len(dims)
    rows = target.shape[0] // n
    for pos in range(n):
        block = place_rows(scalars[1], dims, pos, n)
        target[pos * rows : (pos + 1) * rows, :] = source[
            pl.ds(pl.multiple_of(block * rows, rows), rows), :
        ]


def outer_products(orders, scalars, *refs):
    count = len(orders)
    lefts, rights = refs[:count], refs[count : 2 * count]
    outs, (flat, placed) = refs[2 * count : 4 * count], refs[4 * count :]
    done = None
    for k, (dims, left) in enumerate(orders):
        if left != done:
            for at in range(0, flat.shape[0], 128):
                flat[at : at + 128, :] = lefts[k][:, at : at + 128].T
            done = left
        transposed_rows(scalars, flat, placed, dims)
        half = flat.shape[0] // 2
        stays, goes, right = outs[2 * k], outs[2 * k + 1], rights[k]

        def body(start, size):
            at = pl.ds(start, size)
            stays[:, at] = plain(placed[:half, :], right[:, at]).astype(BF16)
            goes[:, at] = plain(placed[half:, :], right[:, at]).astype(BF16)

        column_tiles(right.shape[1], 256, body)


def mid_gradient(d_left, d_right, w_left, w_right, out):
    def body(start, count):
        at = pl.ds(start, count)
        total = against(d_left[...], w_left[at, :]) + against(d_right[...], w_right[at, :])
        out[:, at] = total.astype(BF16)

    column_tiles(out.shape[1], 256, body)


def down_projection(joined, w_down, stays, goes):
    rows = stays.shape[0]

    def body(start, count):
        at = pl.ds(start, count)
        total = plain(joined[...], w_down[:, at])
        stays[:, at] = total[:rows]
        goes[:, at] = total[rows:].astype(BF16)

    column_tiles(stays.shape[1], 256, body)


def attention_backward(
    scalars, rates, tok_own, tok_other, cot_own, cot_other, nm, branch, mid_own, mid_other,
    scale_ref, w_out, u_own, u_other, q_ref, k_ref, v_ref, dq_ref, dk_ref, gu_ref, dg_ref, att_ref, prior_ref,
    dpre_q, dpre_k, dpre_v, dpre_g, d_branch, gated, hidden_out,
    d_att,
):
    rows, width = tok_own.shape
    cols = q_ref.shape[1]
    c = scalars[0]
    own = pl.ds(pl.multiple_of(c * cols, cols), cols)
    other = pl.ds(pl.multiple_of((1 - c) * cols, cols), cols)
    for half in (0, 1):
        part = slice(half * rows, (half + 1) * rows)
        swap = slice((1 - half) * rows, (2 - half) * rows)
        ok = valid_rows(scalars, half, rows)
        lined = branch[part, :].astype(F32)
        hidden = (tok_own, tok_other)[half][...].astype(F32) + ok * lined
        mid_scale = lax.rsqrt(row_mean(hidden * hidden) + EPSILON)
        normed = hidden * mid_scale
        d_mid = mid_own[part, :].astype(F32) + mid_other[swap, :].astype(F32)
        d_hidden = (cot_own, cot_other)[half][...].astype(F32) + mid_scale * (
            d_mid - normed * row_mean(d_mid * normed)
        )
        if half == 0:
            hidden_out[...] = d_hidden
        d_out = (ok * d_hidden).astype(BF16)
        d_branch[part, :] = d_out
        inner = row_mean(d_out.astype(F32) * lined)
        scale = scale_ref[part, :1]
        d_gated = against(d_out, w_out[own, :])
        normed = att_ref[part, :].astype(F32) * scale
        dpre_g[part, :] = (d_gated * normed * dg_ref[part, :].astype(F32)).astype(BF16)
        d_att[part, :] = (scale * (d_gated * gu_ref[part, :].astype(F32) - normed * inner)).astype(
            BF16
        )
        gated[part, own] = (u_own[part, :cols].astype(F32) * scale).astype(BF16)
        gated[part, other] = (u_other[swap, :cols].astype(F32) * scale).astype(BF16)
    heads, size = prior_ref.shape[:2]
    carried = (scalars[2] > rows).astype(F32)
    first = pl.ds(pl.multiple_of(c * rows, rows), rows)
    second = pl.ds(pl.multiple_of((1 - c) * rows, rows), rows)
    for h in range(heads):
        at = slice(h * size, (h + 1) * size)
        mask, query_decay, key_decay = decays(rates[c * heads + h], rows)
        prior = prior_ref[h]
        wide = (q_ref[second, at].astype(F32) * query_decay).astype(BF16)
        state = (outer(wide, d_att[second, at]) * carried).astype(BF16)
        for b, part in enumerate((first, second)):
            q, k, v, d_o = q_ref[part, at], k_ref[part, at], v_ref[part, at], d_att[part, at]
            weighted = (against(q, k) * mask).astype(BF16)
            d_scores = (against(d_o, v) * mask).astype(BF16)
            d_q = plain(d_scores, k)
            d_k = outer(d_scores, q)
            d_v = outer(weighted, d_o)
            if b == 1:
                d_q = d_q + against(d_o, prior) * query_decay
            else:
                d_k = d_k + against(v, state) * key_decay
                d_v = d_v + plain(k, state) * key_decay
            ok = jnp.where(
                b * rows + lax.broadcasted_iota(jnp.int32, (rows, 1), 0) < scalars[2], 1.0, 0.0
            )
            dpre_q[part, at] = (d_q * dq_ref[part, at].astype(F32)).astype(BF16)
            dpre_k[part, at] = (d_k * dk_ref[part, at].astype(F32)).astype(BF16)
            dpre_v[part, at] = (d_v * ok).astype(BF16)


def input_gradient(
    dpre_q, dpre_k, dpre_v, dpre_g, w_query, w_key, w_value, w_gate, stays, goes
):
    rows = stays.shape[0]

    def body(start, count):
        at = pl.ds(start, count)
        total = against(dpre_q[...], w_query[at, :]) + against(dpre_k[...], w_key[at, :])
        total += against(dpre_v[...], w_value[at, :]) + against(dpre_g[...], w_gate[at, :])
        stays[:, at] = total[:rows]
        goes[:, at] = total[rows:].astype(BF16)

    column_tiles(stays.shape[1], 256, body)


def finish_input(tok, d_hidden, stays, came, out):
    x = tok[...].astype(F32)
    scale = lax.rsqrt(row_mean(x * x) + EPSILON)
    normed = x * scale
    d_in = stays[...] + came[...].astype(F32)
    out[...] = d_hidden[...] + scale * (d_in - normed * row_mean(d_in * normed))


WHOLE = pl.BlockSpec(memory_space=pltpu.VMEM)
SCALAR = pl.BlockSpec(memory_space=pltpu.SMEM)


def call(body, outs, args, specs=None, scratch=(), scalars=None, name=None):
    specs = specs or {}

    def whole(shape):
        return pl.BlockSpec(shape, lambda i, s: (0,) * len(shape))

    in_specs = [specs.get(i, whole(a.shape)) for i, a in enumerate(args)]
    nbytes = sum(a.size * a.dtype.itemsize for a in args)
    return pl.pallas_call(
        body,
        grid_spec=pltpu.PrefetchScalarGridSpec(
            num_scalar_prefetch=1,
            grid=(1,),
            in_specs=in_specs,
            out_specs=[whole(o.shape) for o in outs],
            scratch_shapes=list(scratch),
        ),
        out_shape=outs,
        name=name,
        compiler_params=pltpu.CompilerParams(vmem_limit_bytes=60 * 1024 * 1024),
    )(scalars, *args)


def arr(shape, dtype=BF16):
    return jax.ShapeDtypeStruct(shape, dtype)


def flipped(n, bit):
    return [(i, i ^ (1 << bit)) for i in range(n)]


def halve(stays, goes, n, bit, last=False):
    came = lax.ppermute(goes, "wide", flipped(n, bit))
    total = stays.astype(F32) + came.astype(F32)
    if last:
        return total
    half = total.shape[0] // 2
    return total[:half].astype(BF16), total[half:].astype(BF16)


def scatter_sums(pairs, orders, n):
    pairs = list(pairs)
    for phase in range(len(orders[0])):
        last = phase == len(orders[0]) - 1
        pairs = [halve(*p, n, dims[phase], last) for p, dims in zip(pairs, orders)]
    return pairs


def on_device(
    tokens,
    seq_lens,
    decay_rate,
    w_query,
    w_key,
    w_value,
    w_gate_u,
    w_out,
    w_left,
    w_right,
    w_down,
    cotangent,
):
    n_wide = lax.axis_size("wide")
    bits = n_wide.bit_length() - 1
    order_x = [0, 1] + list(range(2, bits))
    order_y = [1, 0] + list(range(2, bits))
    order_z = [2, 0, 1] + list(range(3, bits))
    rows, width = tokens.shape
    hidden = w_left.shape[1]
    heads = decay_rate.shape[0] // 2
    size = width // decay_rate.shape[0]
    cols = width // 2
    c = lax.axis_index("narrow")
    wide = lax.axis_index("wide")
    scalars = jnp.stack([c, wide, seq_lens[0, 0]]).astype(jnp.int32)
    swap = [(0, 1), (1, 0)]

    def other(v):
        return lax.ppermute(v, "narrow", swap)

    run = functools.partial(call, scalars=scalars)
    tok_other = other(tokens)
    cot_other = other(cotangent)
    half_cols = pl.BlockSpec((width, cols), lambda i, s: (0, s[0]))
    nin, q, k, v, dq, dk, gu, dg, att, u, prior = run(
        attention_forward,
        [arr((2 * rows, width))]
        + [arr((2 * rows, cols))] * 8
        + [arr((2 * rows, cols + 128)), arr((heads, size, size))],
        (decay_rate, tokens, tok_other, w_query, w_key, w_value, w_gate_u),
        specs={0: SCALAR, 3: half_cols, 4: half_cols, 5: half_cols, 6: half_cols},
        scratch=[pltpu.VMEM((2 * rows, cols), F32)],
        name="attention_forward",
    )
    u_other = other(u)
    nm, joined, d_left, d_right, d_ffn, branch, scale = run(
        feed_forward,
        [arr((2 * rows, width))]
        + [arr((2 * rows, hidden))] * 3
        + [arr((2 * rows, width))] * 2
        + [arr((2 * rows, 128), F32)],
        (tokens, tok_other, u, u_other, w_out, w_left, w_right, w_down, cotangent, cot_other),
        name="feed_forward",
    )

    def products(lefts, rights, which, orders, name):
        half = arr((width // 2, rights[0].shape[1]))
        flat = run(
            functools.partial(outer_products, list(zip(orders, which))),
            [half] * (2 * len(rights)),
            tuple(lefts[i] for i in which) + tuple(rights),
            scratch=[pltpu.VMEM((width, 2 * rows), BF16)] * 2,
            name=name,
        )
        return list(zip(flat[0::2], flat[1::2]))

    pairs = products([d_ffn], [joined], [0], [order_z], "grad_down")
    pairs += products([nm], [d_left, d_right], [0, 0], [order_x, order_y], "grad_left_right")
    grad_down, grad_left, grad_right = scatter_sums(pairs, [order_z, order_x, order_y], n_wide)
    (mid,) = run(
        lambda s, *r: mid_gradient(*r),
        [arr((2 * rows, width))],
        (d_left, d_right, w_left, w_right),
        name="mid_gradient",
    )
    mid_other = other(mid)
    ffn_stays, ffn_goes = run(
        lambda s, *r: down_projection(*r),
        [arr((rows, width), F32), arr((rows, width))],
        (joined, w_down),
        name="down_projection",
    )
    ffn_came = other(ffn_goes)
    dpre_q, dpre_k, dpre_v, dpre_g, d_branch, gated, d_hidden = run(
        attention_backward,
        [arr((2 * rows, cols))] * 4 + [arr((2 * rows, width))] * 2 + [arr((rows, width), F32)],
        (decay_rate, tokens, tok_other, cotangent, cot_other, nm, branch, mid, mid_other)
        + (scale, w_out, u, u_other, q, k, v, dq, dk, gu, dg, att, prior),
        specs={0: SCALAR},
        scratch=[pltpu.VMEM((2 * rows, cols), BF16)],
        name="attention_backward",
    )
    pairs = products(
        [nin],
        [dpre_q, dpre_k, dpre_v, dpre_g],
        [0] * 4,
        [order_x, order_x, order_y, order_y],
        "grad_attention",
    )
    d_mine = lax.dynamic_slice_in_dim(d_branch, c * cols, cols, 1)
    pairs += products([gated], [d_mine], [0], [order_z], "grad_out")
    sums = scatter_sums(pairs, [order_x, order_x, order_y, order_y, order_z], n_wide)
    in_stays, in_goes = run(
        lambda s, *r: input_gradient(*r),
        [arr((rows, width), F32), arr((rows, width))],
        (dpre_q, dpre_k, dpre_v, dpre_g, w_query, w_key, w_value, w_gate_u),
        specs={4: half_cols, 5: half_cols, 6: half_cols, 7: half_cols},
        name="input_gradient",
    )
    (input_grad,) = run(
        lambda s, *r: finish_input(*r),
        [arr((rows, width), F32)],
        (tokens, d_hidden, in_stays, other(in_goes)),
        name="finish_input",
    )
    valid = (c * rows + jnp.arange(rows) < seq_lens[0, 0]).astype(F32)[:, None]
    mixed = (
        tokens.astype(F32)
        + valid * (branch[:rows].astype(F32) + ffn_stays + ffn_came.astype(F32))
    ).astype(BF16)
    stacked = jnp.stack(sums)
    theirs = other(stacked)
    both = jnp.where(
        c == 0,
        jnp.concatenate([stacked, theirs], axis=2),
        jnp.concatenate([theirs, stacked], axis=2),
    )
    return (
        mixed,
        input_grad,
        both[0],
        both[1],
        both[2],
        both[3],
        both[4],
        grad_left,
        grad_right,
        grad_down.T,
    )


def solution(mesh):
    placed = (
        P(("wide", "narrow"), None),
        P("wide", None),
        P(),
        P(),
        P(),
        P(),
        P(),
        P(),
        P(None, "narrow"),
        P(None, "narrow"),
        P("narrow", None),
        P(("wide", "narrow"), None),
    )
    return jax.shard_map(
        on_device,
        mesh=mesh,
        in_specs=placed,
        out_specs=(
            P(("wide", "narrow"), None),
            P(("wide", "narrow"), None),
            P("wide", None),
            P("wide", None),
            P("wide", None),
            P("wide", None),
            P("wide", None),
            P("wide", "narrow"),
            P("wide", "narrow"),
            P("narrow", "wide"),
        ),
        check_vma=False,
    )
```

```python
import functools
import math

import jax
import jax.numpy as jnp
from jax import lax
from jax.experimental import pallas as pl
from jax.experimental.pallas import tpu as pltpu
from jax.sharding import PartitionSpec as P

BLOCK = 256
EPSILON = 1e-06
F32 = jnp.float32
BF16 = jnp.bfloat16


def plain(a, b):
    return jnp.dot(a, b, preferred_element_type=F32)


def against(a, b):
    return lax.dot_general(a, b, (((1,), (1,)), ((), ())), preferred_element_type=F32)


def outer(a, b):
    return lax.dot_general(a, b, (((0,), (0,)), ((), ())), preferred_element_type=F32)


def row_mean(v):
    return jnp.mean(v, axis=-1, keepdims=True)


def valid_rows(scalars, half, rows):
    c, length = scalars[0], scalars[2]
    first = rows * (c if half == 0 else 1 - c)
    return (first + lax.broadcasted_iota(jnp.int32, (rows, 1), 0) < length).astype(F32)


def decays(rate, n):
    i = lax.broadcasted_iota(jnp.int32, (n, n), 0)
    j = lax.broadcasted_iota(jnp.int32, (n, n), 1)
    gap = (i - j).astype(F32)
    mask = jnp.where(gap >= 0, jnp.exp(-rate * jnp.maximum(gap, 0.0)), 0.0)
    step = lax.broadcasted_iota(jnp.int32, (n, 1), 0).astype(F32)
    return mask, jnp.exp(-rate * (step + 1.0)), jnp.exp(-rate * (n - 1.0 - step))


def silu_parts(pre):
    sig = jax.nn.sigmoid(pre)
    act = pre * sig
    return act, sig + act * (1.0 - sig)


class Loaded:
    def __init__(self, source, buffer, sem, queue):
        self.buffer, self.copy, self.ready = buffer, pltpu.make_async_copy(source, buffer, sem), False
        self.queue = queue
        queue.append(self)

    def __call__(self):
        if not self.ready:
            while self in self.queue:
                self.queue.pop(0).copy.start()
            self.copy.wait()
            self.ready = True
            if self.queue:
                self.queue.pop(0).copy.start()
        return self.buffer


class Stored:
    def __init__(self, target, buffer, sem):
        self.buffer, self.copy, self.sent = buffer, pltpu.make_async_copy(buffer, target, sem), False

    def send(self):
        if not self.sent:
            self.copy.start()
            self.sent = True


ANY = pl.BlockSpec(memory_space=pl.ANY)
SMEM = pl.BlockSpec(memory_space=pltpu.SMEM)


def arr(shape, dtype=BF16):
    return jax.ShapeDtypeStruct(shape, dtype)


def call(body, outs, small, args, after=(), parts=None, scratch=(), window=4, slack=8, near=(), name=None):
    parts = parts or {}
    args = [
        a if i in near else pltpu.with_memory_space_constraint(a, pltpu.HBM)
        for i, a in enumerate(args)
    ]
    shapes = [parts[i][1] if i in parts else a.shape for i, a in enumerate(args)]
    n_small, n_in, n_out, n_after = len(small), len(args), len(outs), len(after)

    def kernel(*refs):
        scalars = refs[:n_small]
        at = n_small
        sources = refs[at : at + n_in]
        at += n_in + n_after
        targets = refs[at : at + n_out]
        at += n_out
        in_bufs = refs[at : at + n_in]
        at += n_in
        out_bufs = refs[at : at + n_out]
        at += n_out
        in_sem, out_sem = refs[at : at + 2]
        queue = []
        loaded = [
            Loaded(parts[i][0](scalars[0], s) if i in parts else s, b, in_sem.at[i], queue)
            for i, (s, b) in enumerate(zip(sources, in_bufs))
        ]
        for _ in range(min(window, n_in)):
            queue.pop(0).copy.start()
        stored = [Stored(t, b, out_sem.at[i]) for i, (t, b) in enumerate(zip(targets, out_bufs))]
        body(*scalars, *loaded, *stored, *refs[at + 2 :])
        for one in loaded:
            one()
        for one in stored:
            one.send()
        for one in stored:
            one.copy.wait()

    buffers = [pltpu.VMEM(t, a.dtype) for t, a in zip(shapes, args)]
    buffers += [pltpu.VMEM(o.shape, o.dtype) for o in outs]
    held = sum(b.dtype.itemsize * math.prod(b.shape) for b in [*buffers, *scratch])
    return pl.pallas_call(
        kernel,
        in_specs=[SMEM] * n_small + [ANY] * (n_in + n_after),
        out_specs=[ANY] * n_out,
        out_shape=[pltpu.HBM(o.shape, o.dtype) for o in outs],
        scratch_shapes=buffers
        + [pltpu.SemaphoreType.DMA((max(n_in, 1),)), pltpu.SemaphoreType.DMA((max(n_out, 1),))]
        + list(scratch),
        name=name,
        compiler_params=pltpu.CompilerParams(vmem_limit_bytes=held + (slack << 20)),
    )(*small, *args, *after)


def attention_forward(
    scalars, rates, tok_own, tok_other, w_query, w_key, w_value, w_gate,
    u, nin, q, k, v, dq, dk, gu, dg, att_out, prior_out,
    gate_buf,
):
    rows, cols = BLOCK, q.buffer.shape[1]
    c = scalars[0]
    valid = []
    for half, tok in enumerate((tok_own, tok_other)):
        x = tok()[...].astype(F32)
        nin.buffer[half * rows : (half + 1) * rows, :] = (
            x * lax.rsqrt(row_mean(x * x) + EPSILON)
        ).astype(BF16)
        valid.append(valid_rows(scalars, half, rows))
    nin.send()
    for w, which in ((w_query, 0), (w_key, 1), (w_value, 2), (w_gate, 3)):
        w = w()
        for half in (0, 1):
            part = slice(half * rows, (half + 1) * rows)
            ok = valid[half]
            pre = plain(nin.buffer[part, :], w[...])
            if which == 2:
                v.buffer[part, :] = (pre * ok).astype(BF16)
                continue
            act, slope = silu_parts(pre)
            if which == 0:
                q.buffer[part, :] = act.astype(BF16)
                dq.buffer[part, :] = slope.astype(BF16)
            elif which == 1:
                k.buffer[part, :] = (act * ok).astype(BF16)
                dk.buffer[part, :] = (slope * ok).astype(BF16)
            else:
                gate_buf[part, :] = act
                gu.buffer[part, :] = act.astype(BF16)
                dg.buffer[part, :] = slope.astype(BF16)
    for one in (q, dq, k, dk, v, gu, dg):
        one.send()
    heads, size = prior_out.buffer.shape[:2]
    carried = (scalars[2] > rows).astype(F32)
    first = pl.ds(pl.multiple_of(c * rows, rows), rows)
    second = pl.ds(pl.multiple_of((1 - c) * rows, rows), rows)
    squares = [jnp.zeros((rows, 1), F32), jnp.zeros((rows, 1), F32)]
    for h in range(heads):
        at = slice(h * size, (h + 1) * size)
        mask, query_decay, key_decay = decays(rates[c * heads + h], rows)
        wide = (k.buffer[first, at].astype(F32) * key_decay).astype(BF16)
        prior = (outer(wide, v.buffer[first, at]) * carried).astype(BF16)
        prior_out.buffer[h] = prior
        for b, part in enumerate((first, second)):
            queries = q.buffer[part, at]
            weighted = (against(queries, k.buffer[part, at]) * mask).astype(BF16)
            att = plain(weighted, v.buffer[part, at])
            if b == 1:
                att = att + plain(queries, prior) * query_decay
            att_out.buffer[part, at] = att.astype(BF16)
            u.buffer[part, at] = (att * gate_buf[part, at]).astype(BF16)
            squares[b] = squares[b] + jnp.sum(att * att, axis=-1, keepdims=True)
    lane = lax.broadcasted_iota(jnp.int32, (rows, 128), 1)
    for b, part in enumerate((first, second)):
        high = squares[b].astype(BF16).astype(F32)
        low = squares[b] - high
        u.buffer[part, cols:] = jnp.where(lane < 64, high, low).astype(BF16)


def block_at(wide, dims, pos):
    mask = 0
    for i, d in enumerate(dims):
        if pos >> (len(dims) - 1 - i) & 1:
            mask |= 1 << d
    return wide ^ mask


def transposed(source, flat):
    for at in range(0, flat.shape[0], 128):
        flat[at : at + 128, :] = source[:, at : at + 128].T


def placed_product(scalars, flat, right, dims, stays, goes, placed):
    n = 1 << len(dims)
    rows = flat.shape[0] // n
    half = flat.shape[0] // 2
    for pos in reversed(range(n)):
        block = block_at(scalars[1], dims, pos)
        placed[pos * rows : (pos + 1) * rows, :] = flat[
            pl.ds(pl.multiple_of(block * rows, rows), rows), :
        ]
    step = 256
    for at in range(0, half, step):
        goes[at : at + step, :] = plain(placed[half + at : half + at + step, :], right).astype(BF16)
    for at in range(0, half, step):
        stays[at : at + step, :] = plain(placed[at : at + step, :], right).astype(BF16)


def feed_forward(
    orders, scalars, u_own, u_other, w_out, tok_own, tok_other, cot_own, cot_other, w_left, w_right, w_down,
    joined, d_left, d_right, branch_out, scale_out, *rest,
):
    grads, (nm, d_ffn, flat, flat_mid, placed) = rest[:6], rest[6:]
    rows = BLOCK
    c = scalars[0]
    u_own, u_other, w_out = u_own(), u_other(), w_out()
    cols = u_own.shape[1] - 128
    width = 2 * cols
    own = pl.ds(pl.multiple_of(c * cols, cols), cols)
    other = pl.ds(pl.multiple_of((1 - c) * cols, cols), cols)
    for half in (0, 1):
        part = slice(half * rows, (half + 1) * rows)
        swap = slice((1 - half) * rows, (2 - half) * rows)
        total = jnp.zeros((rows, 1), F32)
        for lane in (0, 64):
            total = total + u_own[part, cols + lane : cols + lane + 1].astype(F32)
            total = total + u_other[swap, cols + lane : cols + lane + 1].astype(F32)
        scale = lax.rsqrt(total / width + EPSILON)
        scale_out.buffer[part, :] = jnp.broadcast_to(scale, (rows, 128))
        branch = scale * (
            plain(u_own[part, :cols], w_out[own, :]) + plain(u_other[swap, :cols], w_out[other, :])
        )
        branch_out.buffer[part, :] = branch.astype(BF16)
        ok = valid_rows(scalars, half, rows)
        hidden = (tok_own, tok_other)[half]()[...].astype(F32) + ok * branch
        nm[part, :] = (hidden * lax.rsqrt(row_mean(hidden * hidden) + EPSILON)).astype(BF16)
        cot = (cot_own, cot_other)[half]()[...].astype(F32)
        d_ffn[part, :] = (cot * ok).astype(BF16)
    branch_out.send()
    scale_out.send()
    w_left, w_right, w_down = w_left(), w_right(), w_down()
    hidden_units = w_left.shape[1]
    for first in range(0, hidden_units, 768):
        at = slice(first, min(first + 768, hidden_units))
        for half in (0, 1):
            part = slice(half * rows, (half + 1) * rows)
            left = plain(nm[part, :], w_left[:, at])
            right = plain(nm[part, :], w_right[:, at])
            joined.buffer[part, at] = (left * right).astype(BF16)
            d_joined = against(d_ffn[part, :], w_down[at, :])
            d_left.buffer[part, at] = (d_joined * right).astype(BF16)
            d_right.buffer[part, at] = (d_joined * left).astype(BF16)
    for one in (joined, d_left, d_right):
        one.send()
    transposed(d_ffn, flat)
    pairs = list(zip(grads[0::2], grads[1::2]))
    for i, right in enumerate((joined, d_left, d_right)):
        if i == 1:
            transposed(nm, flat_mid)
            flat = flat_mid
        stays, goes = pairs[i]
        placed_product(scalars, flat, right.buffer[...], orders[i], stays.buffer, goes.buffer, placed)
        goes.send()
        stays.send()


def mid_gradient(scalars, d_left, w_left, d_right, w_right, out, total):
    rows = BLOCK
    d_left, w_left = d_left(), w_left()
    step = w_left.shape[0] // 2
    places = [(half * rows, first) for half in (0, 1) for first in (0, step)]
    for row, first in places:
        total[row : row + rows, first : first + step] = against(
            d_left[row : row + rows, :], w_left[first : first + step, :]
        )
    d_right, w_right = d_right(), w_right()
    for row, first in places:
        at = (slice(row, row + rows), slice(first, first + step))
        out.buffer[at] = (
            total[at] + against(d_right[row : row + rows, :], w_right[first : first + step, :])
        ).astype(BF16)


def down_projection(scalars, joined, w_down, stays, goes):
    rows = BLOCK
    joined, w_down = joined(), w_down()
    goes.buffer[...] = plain(joined[rows:, :], w_down[...]).astype(BF16)
    goes.send()
    stays.buffer[...] = plain(joined[:rows, :], w_down[...])


def attention_backward(
    orders, scalars, rates, mid_own, mid_other, tok_own, tok_other, cot_own, cot_other, branch, w_out, scale_ref,
    gu, dg, att, u_own, u_other, q, k, v, prior, dq, dk, nin,
    out_goes, out_stays, dpre, x_goes, x_stays, y_goes, y_stays, hidden_out,
    d_att, d_branch, gated, flat, flat_gated, placed,
):
    rows = BLOCK
    cols = dpre.buffer.shape[1] // 4
    c = scalars[0]
    own = pl.ds(pl.multiple_of(c * cols, cols), cols)
    other = pl.ds(pl.multiple_of((1 - c) * cols, cols), cols)
    for half in (0, 1):
        part = slice(half * rows, (half + 1) * rows)
        swap = slice((1 - half) * rows, (2 - half) * rows)
        ok = valid_rows(scalars, half, rows)
        d_mid = mid_own()[part, :].astype(F32) + mid_other()[swap, :].astype(F32)
        x = (tok_own, tok_other)[half]()[...].astype(F32)
        cot = (cot_own, cot_other)[half]()[...].astype(F32)
        lined = branch()[part, :].astype(F32)
        hidden = x + ok * lined
        mid_scale = lax.rsqrt(row_mean(hidden * hidden) + EPSILON)
        normed = hidden * mid_scale
        d_hidden = cot + mid_scale * (d_mid - normed * row_mean(d_mid * normed))
        if half == 0:
            hidden_out.buffer[...] = d_hidden
        d_out = (ok * d_hidden).astype(BF16)
        d_branch[part, :] = d_out
        inner = row_mean(d_out.astype(F32) * lined)
        d_gated = against(d_out, w_out()[...])
        scale = scale_ref()[part, :1]
        normed = att()[part, :].astype(F32) * scale
        dpre.buffer[part, 3 * cols :] = (d_gated * normed * dg()[part, :].astype(F32)).astype(BF16)
        d_att[part, :] = (scale * (d_gated * gu()[part, :].astype(F32) - normed * inner)).astype(BF16)
        gated[part, own] = (u_own()[part, :cols].astype(F32) * scale).astype(BF16)
        gated[part, other] = (u_other()[swap, :cols].astype(F32) * scale).astype(BF16)
    hidden_out.send()
    q, k, v, dq, dk, prior = q(), k(), v(), dq(), dk(), prior()
    heads, size = prior.shape[:2]
    carried = (scalars[2] > rows).astype(F32)
    first = pl.ds(pl.multiple_of(c * rows, rows), rows)
    second = pl.ds(pl.multiple_of((1 - c) * rows, rows), rows)
    row = lax.broadcasted_iota(jnp.int32, (rows, 1), 0)
    for h in range(heads):
        lanes = [slice(i * cols + h * size, i * cols + (h + 1) * size) for i in range(3)]
        at = lanes[0]
        mask, query_decay, key_decay = decays(rates[c * heads + h], rows)
        wide = (q[second, at].astype(F32) * query_decay).astype(BF16)
        state = (outer(wide, d_att[second, at]) * carried).astype(BF16)
        for b, part in enumerate((first, second)):
            q_b, k_b, v_b, d_o = q[part, at], k[part, at], v[part, at], d_att[part, at]
            weighted = (against(q_b, k_b) * mask).astype(BF16)
            d_scores = (against(d_o, v_b) * mask).astype(BF16)
            d_q = plain(d_scores, k_b)
            d_k = outer(d_scores, q_b)
            d_v = outer(weighted, d_o)
            if b == 1:
                d_q = d_q + against(d_o, prior[h]) * query_decay
            else:
                d_k = d_k + against(v_b, state) * key_decay
                d_v = d_v + plain(k_b, state) * key_decay
            ok = jnp.where(b * rows + row < scalars[2], 1.0, 0.0)
            dpre.buffer[part, lanes[0]] = (d_q * dq[part, at].astype(F32)).astype(BF16)
            dpre.buffer[part, lanes[1]] = (d_k * dk[part, at].astype(F32)).astype(BF16)
            dpre.buffer[part, lanes[2]] = (d_v * ok).astype(BF16)
    dpre.send()
    transposed(nin(), flat)
    pairs = ((x_stays, x_goes), (y_stays, y_goes))
    for i, (stays, goes) in enumerate(pairs):
        right = dpre.buffer[:, 2 * i * cols : 2 * (i + 1) * cols]
        placed_product(scalars, flat, right, orders[i], stays.buffer, goes.buffer, placed)
        goes.send()
        stays.send()
    transposed(gated, flat_gated)
    placed_product(scalars, flat_gated, d_branch[:, own], orders[2], out_stays.buffer, out_goes.buffer, placed)


def input_gradient(scalars, dpre, w_query, w_key, w_value, w_gate, stays, goes, total):
    rows = stays.buffer.shape[0]
    cols = w_query.buffer.shape[1]
    dpre = dpre()
    for i, w in enumerate((w_query, w_key, w_value, w_gate)):
        w = w()
        for half in (0, 1):
            part = slice(half * rows, (half + 1) * rows)
            term = against(dpre[part, i * cols : (i + 1) * cols], w[...])
            if i == 0:
                total[part, :] = term
            elif i < 3:
                total[part, :] += term
            elif half == 0:
                stays.buffer[...] = total[part, :] + term
            else:
                goes.buffer[...] = (total[part, :] + term).astype(BF16)


def finish_rows(
    scalars, tok, branch, ffn_stays, ffn_came, d_hidden, in_stays, in_came, mixed, input_grad
):
    x = tok()[...].astype(F32)
    ffn = ffn_stays()[...] + ffn_came()[...].astype(F32)
    ok = valid_rows(scalars, 0, x.shape[0])
    mixed.buffer[...] = (x + ok * (branch()[...].astype(F32) + ffn)).astype(BF16)
    mixed.send()
    scale = lax.rsqrt(row_mean(x * x) + EPSILON)
    normed = x * scale
    d_in = in_stays()[...] + in_came()[...].astype(F32)
    input_grad.buffer[...] = d_hidden()[...] + scale * (d_in - normed * row_mean(d_in * normed))


def last_feed_forward(scalars, stays, came, left, right, down):
    total = stays()[...].astype(F32) + came()[...].astype(F32)
    units = left.buffer.shape[1]
    left.buffer[...] = total[:, units : 2 * units]
    right.buffer[...] = total[:, 2 * units :]
    for at in range(0, units, 128):
        down.buffer[at : at + 128, :] = total[:, at : at + 128].T


def last_attention(scalars, stays, came, mine):
    mine.buffer[...] = stays()[...].astype(F32) + came()[...].astype(F32)


def join_columns(scalars, mine, theirs, *outs):
    mine, theirs = mine(), theirs()
    cols = mine.shape[1] // len(outs)
    own = pl.ds(pl.multiple_of(scalars[0] * cols, cols), cols)
    other = pl.ds(pl.multiple_of((1 - scalars[0]) * cols, cols), cols)
    for i, out in enumerate(outs):
        at = slice(i * cols, (i + 1) * cols)
        out.buffer[:, own] = mine[:, at]
        out.buffer[:, other] = theirs[:, at]


def on_device(
    tokens,
    seq_lens,
    decay_rate,
    w_query,
    w_key,
    w_value,
    w_gate_u,
    w_out,
    w_left,
    w_right,
    w_down,
    cotangent,
):
    n_wide = lax.axis_size("wide")
    bits = n_wide.bit_length() - 1
    tail = list(range(3, bits))
    order_x, order_y, order_z = [0, 1, 2] + tail, [1, 2, 0] + tail, [2, 0, 1] + tail
    rows, width = tokens.shape
    units = w_left.shape[1]
    heads = decay_rate.shape[0] // 2
    size = width // decay_rate.shape[0]
    cols = width // 2
    group = 2 * rows
    c = lax.axis_index("narrow")
    scalars = jnp.stack([c, lax.axis_index("wide"), seq_lens[0, 0]]).astype(jnp.int32)

    def other(v):
        return lax.ppermute(v, "narrow", [(0, 1), (1, 0)])

    def over(v, bit):
        return lax.ppermute(v, "wide", [(i, i ^ (1 << bit)) for i in range(n_wide)])

    def half_cols(s, ref):
        return ref.at[:, pl.ds(pl.multiple_of(s[0] * cols, cols), cols)]

    def half_rows(s, ref):
        return ref.at[pl.ds(pl.multiple_of(s[0] * cols, cols), cols), :]

    halves = (half_cols, (width, cols))
    small = (scalars,)
    tok_other, cot_other = other(tokens), other(cotangent)
    u, nin, q, k, v, dq, dk, gu, dg, att, prior = call(
        attention_forward,
        [arr((group, cols + 128)), arr((group, width))]
        + [arr((group, cols))] * 8
        + [arr((heads, size, size))],
        (scalars, decay_rate),
        (tokens, tok_other, w_query, w_key, w_value, w_gate_u),
        parts={i: halves for i in (2, 3, 4, 5)},
        near=(1,),
        window=3,
        scratch=[pltpu.VMEM((group, cols), F32)],
        name="attention_forward",
    )
    u_other = other(u)
    part = arr((width // 2, units))
    joined, d_left, d_right, branch, scale, *grads = call(
        functools.partial(feed_forward, (order_z, order_x, order_y)),
        [arr((group, units))] * 3
        + [arr((group, width)), arr((group, 128), F32)]
        + [part] * 6,
        small,
        (u, u_other, w_out, tokens, tok_other, cotangent, cot_other, w_left, w_right, w_down),
        scratch=[pltpu.VMEM((group, width), BF16)] * 2 + [pltpu.VMEM((width, group), BF16)] * 3,
        near=(1, 4, 6),
        window=7,
        name="feed_forward",
    )
    (mid,) = call(
        mid_gradient,
        [arr((group, width))],
        small,
        (d_left, w_left, d_right, w_right),
        scratch=[pltpu.VMEM((group, width), F32)],
        name="mid_gradient",
    )
    mid_other = other(mid)
    ffn_stays, ffn_goes = call(
        down_projection,
        [arr((rows, width), F32), arr((rows, width))],
        small,
        (joined, w_down),
        after=(mid,),
        name="down_projection",
    )
    ffn_came = other(ffn_goes)
    wide_part = arr((width // 2, width))
    out_part = arr((width // 2, cols))
    out_goes, out_stays, dpre, x_goes, x_stays, y_goes, y_stays, d_hidden = call(
        functools.partial(attention_backward, (order_x, order_y, order_z)),
        [out_part] * 2 + [arr((group, 4 * cols))] + [wide_part] * 4 + [arr((rows, width), F32)],
        (scalars, decay_rate),
        (mid, mid_other, tokens, tok_other, cotangent, cot_other, branch, w_out, scale)
        + (gu, dg, att, u, u_other, q, k, v, prior, dq, dk, nin),
        after=(ffn_stays,),
        parts={7: (half_rows, (cols, width))},
        near=(1, 3, 5, 13),
        window=8,
        scratch=[pltpu.VMEM((group, cols), BF16)]
        + [pltpu.VMEM((group, width), BF16)] * 2
        + [pltpu.VMEM((width, group), BF16)] * 3,
        name="attention_backward",
    )
    in_stays, in_goes = call(
        input_gradient,
        [arr((rows, width), F32), arr((rows, width))],
        small,
        (dpre, w_query, w_key, w_value, w_gate_u),
        parts={i: halves for i in (1, 2, 3, 4)},
        scratch=[pltpu.VMEM((group, width), F32)],
        name="input_gradient",
    )
    in_came = other(in_goes)

    def halves_of(stays, came):
        half = stays.shape[0] // 2
        total = [
            (stays[at, :].astype(F32) + came[at, :].astype(F32)).astype(BF16)
            for at in (slice(half, 2 * half), slice(0, half))
        ]
        return tuple(total)

    ffn_orders = (order_z, order_x, order_y)
    ffn = list(zip(grads[1::2], grads[0::2]))
    attn_orders = (order_x, order_y, order_z)
    attn = [(x_goes, x_stays), (y_goes, y_stays), (out_goes, out_stays)]
    last = in_stays

    def step(pairs, orders, phase, merge=False):
        nonlocal last
        out = []
        for (goes, stays), order in zip(pairs, orders):
            came = over(goes, order[phase])
            came, last = lax.optimization_barrier((came, last))
            out.append(halves_of(stays, came))
            last = out[-1][0]
        if merge:
            out = [tuple(jnp.concatenate(side, axis=1) for side in zip(*out))]
            last = out[0][0]
        return out

    ffn = step(ffn, ffn_orders, 0)
    mixed, input_grad = call(
        finish_rows,
        [arr((rows, width)), arr((rows, width), F32)],
        small,
        (tokens, branch, ffn_stays, ffn_came, d_hidden, in_stays, in_came),
        after=(last,),
        parts={1: (lambda s, ref: ref.at[pl.ds(0, rows), :], (rows, width))},
        near=(3, 6),
        window=7,
        name="finish_rows",
    )
    last = mixed
    ffn = step(ffn, ffn_orders, 1)
    attn = step(attn, attn_orders, 0)
    ffn = step(ffn, ffn_orders, 2, True)
    attn = step(attn, attn_orders, 1)
    for phase in tail[:-1]:
        ffn = step(ffn, [order_x], phase)
    ((goes, stays),) = ffn
    slab = width // n_wide
    grad_left, grad_right, grad_down = call(
        last_feed_forward,
        [arr((slab, units), F32)] * 2 + [arr((units, slab), F32)],
        small,
        (stays, over(goes, bits - 1)),
        after=(last,),
        near=(0, 1),
        name="last_feed_forward",
    )
    last = grad_left
    attn = step(attn, attn_orders, 2, True)
    for phase in tail[:-1]:
        attn = step(attn, [order_x], phase)
    ((goes, stays),) = attn
    (mine,) = call(
        last_attention,
        [arr(stays.shape[:1] + stays.shape[1:], F32)],
        small,
        (stays, over(goes, bits - 1)),
        near=(0, 1),
        name="last_attention",
    )
    joint = call(
        join_columns,
        [arr((slab, width), F32)] * 5,
        small,
        (mine, other(mine)),
        near=(0, 1),
        name="join_columns",
    )
    return (mixed, input_grad, *joint, grad_left, grad_right, grad_down)


def solution(mesh):
    placed = (
        P(("wide", "narrow"), None),
        P("wide", None),
        P(),
        P(),
        P(),
        P(),
        P(),
        P(),
        P(None, "narrow"),
        P(None, "narrow"),
        P("narrow", None),
        P(("wide", "narrow"), None),
    )
    return jax.shard_map(
        on_device,
        mesh=mesh,
        in_specs=placed,
        out_specs=(
            P(("wide", "narrow"), None),
            P(("wide", "narrow"), None),
            P("wide", None),
            P("wide", None),
            P("wide", None),
            P("wide", None),
            P("wide", None),
            P("wide", "narrow"),
            P("wide", "narrow"),
            P("narrow", "wide"),
        ),
        check_vma=False,
    )
```

```python
import functools
import math

import jax
import jax.numpy as jnp
from jax import lax
from jax.experimental import pallas as pl
from jax.experimental.pallas import tpu as pltpu
from jax.sharding import PartitionSpec as P

BLOCK = 256
EPSILON = 1e-06
F32 = jnp.float32
BF16 = jnp.bfloat16


def plain(a, b):
    return jnp.dot(a, b, preferred_element_type=F32)


def against(a, b):
    return lax.dot_general(a, b, (((1,), (1,)), ((), ())), preferred_element_type=F32)


def outer(a, b):
    return lax.dot_general(a, b, (((0,), (0,)), ((), ())), preferred_element_type=F32)


def row_mean(v):
    return jnp.mean(v, axis=-1, keepdims=True)


def valid_rows(scalars, half, rows):
    c, length = scalars[0], scalars[2]
    first = rows * (c if half == 0 else 1 - c)
    return (first + lax.broadcasted_iota(jnp.int32, (rows, 1), 0) < length).astype(F32)


def decays(rate, n):
    i = lax.broadcasted_iota(jnp.int32, (n, n), 0)
    j = lax.broadcasted_iota(jnp.int32, (n, n), 1)
    gap = (i - j).astype(F32)
    mask = jnp.where(gap >= 0, jnp.exp(-rate * jnp.maximum(gap, 0.0)), 0.0)
    step = lax.broadcasted_iota(jnp.int32, (n, 1), 0).astype(F32)
    return mask, jnp.exp(-rate * (step + 1.0)), jnp.exp(-rate * (n - 1.0 - step))


def silu_parts(pre):
    sig = jax.nn.sigmoid(pre)
    act = pre * sig
    return act, sig + act * (1.0 - sig)


class Loaded:
    def __init__(self, source, buffer, sem, queue):
        self.buffer, self.copy, self.ready = buffer, pltpu.make_async_copy(source, buffer, sem), False
        self.queue = queue
        queue.append(self)

    def __call__(self):
        if not self.ready:
            while self in self.queue:
                self.queue.pop(0).copy.start()
            self.copy.wait()
            self.ready = True
            if self.queue:
                self.queue.pop(0).copy.start()
        return self.buffer


class Stored:
    def __init__(self, target, buffer, sem):
        self.buffer, self.copy, self.sent = buffer, pltpu.make_async_copy(buffer, target, sem), False

    def send(self):
        if not self.sent:
            self.copy.start()
            self.sent = True

    def finish(self):
        self.send()
        self.copy.wait()


class Here:
    def __init__(self, buffer):
        self.buffer = buffer

    def __call__(self):
        return self.buffer

    def send(self):
        pass

    def finish(self):
        pass


ANY = pl.BlockSpec(memory_space=pl.ANY)
VMEM = pl.BlockSpec(memory_space=pltpu.VMEM)
SMEM = pl.BlockSpec(memory_space=pltpu.SMEM)


def arr(shape, dtype=BF16):
    return jax.ShapeDtypeStruct(shape, dtype)


class here:
    def __init__(self, shape, dtype=BF16):
        self.shape, self.dtype = shape, jnp.dtype(dtype)


def call(
    body, outs, small, args, after=(), parts=None, scratch=(), window=4, slack=8, near=(), inside=(),
    into=None, name=None,
):
    parts, into = parts or {}, into or {}
    args = [
        a if i in near else pltpu.with_memory_space_constraint(a, pltpu.VMEM if i in inside else pltpu.HBM)
        for i, a in enumerate(args)
    ]
    shapes = [parts[i][1] if i in parts else a.shape for i, a in enumerate(args)]
    n_small, n_in, n_out, n_after = len(small), len(args), len(outs), len(after)
    copied = [i for i in range(n_in) if i not in inside and i not in into]
    sent = [i for i in range(n_out) if not isinstance(outs[i], here)]

    def kernel(*refs):
        scalars = refs[:n_small]
        at = n_small
        sources = refs[at : at + n_in]
        at += n_in + n_after
        targets = refs[at : at + n_out]
        at += n_out
        in_bufs = dict(zip(copied, refs[at:]))
        at += len(copied)
        out_bufs = dict(zip(sent, refs[at:]))
        at += len(sent)
        in_sem, out_sem = refs[at : at + 2]
        queue = []
        loaded = []
        for i, source in enumerate(sources):
            if i in inside:
                loaded.append(Here(source))
                continue
            source = parts[i][0](scalars[0], source) if i in parts else source
            buffer = targets[into[i]] if i in into else in_bufs[i]
            loaded.append(Loaded(source, buffer, in_sem.at[i], queue))
        for _ in range(min(window, len(queue))):
            queue.pop(0).copy.start()
        stored = [
            Stored(t, out_bufs[i], out_sem.at[i]) if i in out_bufs else Here(t)
            for i, t in enumerate(targets)
        ]
        results = [one for i, one in enumerate(stored) if i not in into.values()]
        body(*scalars, *loaded, *results, *refs[at + 2 :])
        for one in loaded:
            one()
        for one in stored:
            one.send()
        for one in stored:
            one.finish()

    buffers = [pltpu.VMEM(shapes[i], args[i].dtype) for i in copied]
    buffers += [pltpu.VMEM(outs[i].shape, outs[i].dtype) for i in sent]
    held = sum(b.dtype.itemsize * math.prod(b.shape) for b in [*buffers, *scratch])
    return pl.pallas_call(
        kernel,
        in_specs=[SMEM] * n_small
        + [VMEM if i in inside else ANY for i in range(n_in)]
        + [ANY] * n_after,
        out_specs=[ANY if i in sent else VMEM for i in range(n_out)],
        out_shape=[
            (pltpu.HBM if i in sent else pltpu.VMEM)(o.shape, o.dtype) for i, o in enumerate(outs)
        ],
        scratch_shapes=buffers
        + [pltpu.SemaphoreType.DMA((max(n_in, 1),)), pltpu.SemaphoreType.DMA((max(n_out, 1),))]
        + list(scratch),
        name=name,
        compiler_params=pltpu.CompilerParams(vmem_limit_bytes=held + (slack << 20)),
    )(*small, *args, *after)


def normed_rows(x):
    return x * lax.rsqrt(row_mean(x * x) + EPSILON)


def activations(i, pre, ok, part, q, k, v, dq, dk, gu, dg, gate):
    if i == 2:
        v[part, :] = (pre * ok).astype(BF16)
        return
    act, slope = silu_parts(pre)
    if i == 0:
        q[part, :] = act.astype(BF16)
        dq[part, :] = slope.astype(BF16)
    elif i == 1:
        k[part, :] = (act * ok).astype(BF16)
        dk[part, :] = (slope * ok).astype(BF16)
    else:
        gate[part, :] = act
        gu[part, :] = act.astype(BF16)
        dg[part, :] = slope.astype(BF16)


def project_own(scalars, tok, w_query, w_key, w_value, w_gate, nin, *outs):
    nin.buffer[...] = normed_rows(tok()[...].astype(F32)).astype(BF16)
    rows = nin.buffer.shape[0]
    ok = valid_rows(scalars, 0, rows)
    outs = [out.buffer for out in outs]
    for i, w in enumerate((w_query, w_key, w_value, w_gate)):
        activations(i, plain(nin.buffer[...], w()[...]), ok, slice(0, rows), *outs)


def attention_forward(
    scalars, rates, nin_own, *refs
):
    own, (tok_other, w_query, w_key, w_value, w_gate, w_out, w_left) = refs[:8], refs[8:15]
    (u, nin, q, k, v, dq, dk, gu, dg, att_out, prior_out), (gate_buf,) = refs[15:26], refs[26:]
    rows, cols = BLOCK, q.buffer.shape[1]
    c = scalars[0]
    nin.buffer[:rows, :] = nin_own()[...]
    nin.buffer[rows:, :] = normed_rows(tok_other()[...].astype(F32)).astype(BF16)
    nin.send()
    kept = [*(one.buffer for one in (q, k, v, dq, dk, gu, dg)), gate_buf]
    for mine, whole in zip(own, kept):
        whole[:rows, :] = mine()[...]
    ok = valid_rows(scalars, 1, rows)
    for i, w in enumerate((w_query, w_key, w_value, w_gate)):
        activations(i, plain(nin.buffer[rows:, :], w()[...]), ok, slice(rows, 2 * rows), *kept)
    for one in (q, dq, k, dk, v, gu, dg):
        one.send()
    heads, size = prior_out.buffer.shape[:2]
    carried = (scalars[2] > rows).astype(F32)
    first = pl.ds(pl.multiple_of(c * rows, rows), rows)
    second = pl.ds(pl.multiple_of((1 - c) * rows, rows), rows)
    squares = [jnp.zeros((rows, 1), F32), jnp.zeros((rows, 1), F32)]
    for h in range(heads):
        at = slice(h * size, (h + 1) * size)
        mask, query_decay, key_decay = decays(rates[c * heads + h], rows)
        wide = (k.buffer[first, at].astype(F32) * key_decay).astype(BF16)
        prior = (outer(wide, v.buffer[first, at]) * carried).astype(BF16)
        prior_out.buffer[h] = prior
        for b, part in enumerate((first, second)):
            queries = q.buffer[part, at]
            weighted = (against(queries, k.buffer[part, at]) * mask).astype(BF16)
            att = plain(weighted, v.buffer[part, at])
            if b == 1:
                att = att + plain(queries, prior) * query_decay
            att_out.buffer[part, at] = att.astype(BF16)
            u.buffer[part, at] = (att * gate_buf[part, at]).astype(BF16)
            squares[b] = squares[b] + jnp.sum(att * att, axis=-1, keepdims=True)
    lane = lax.broadcasted_iota(jnp.int32, (rows, 128), 1)
    for b, part in enumerate((first, second)):
        high = squares[b].astype(BF16).astype(F32)
        low = squares[b] - high
        u.buffer[part, cols:] = jnp.where(lane < 64, high, low).astype(BF16)


def block_at(wide, dims, pos):
    mask = 0
    for i, d in enumerate(dims):
        if pos >> (len(dims) - 1 - i) & 1:
            mask |= 1 << d
    return wide ^ mask


def transposed(source, flat):
    for at in range(0, flat.shape[0], 128):
        flat[at : at + 128, :] = source[:, at : at + 128].T


def place(scalars, flat, placed, dims):
    n = 1 << len(dims)
    rows = flat.shape[0] // n
    for pos in range(n):
        block = block_at(scalars[1], dims, pos)
        placed[pos * rows : (pos + 1) * rows, :] = flat[
            pl.ds(pl.multiple_of(block * rows, rows), rows), :
        ]


def product(placed, right, at, stays, goes):
    half = placed.shape[0] // 2
    step = 256
    for out, first in ((goes, half), (stays, 0)):
        for row in range(0, half, step):
            out.buffer[row : row + step, :] = plain(
                placed[first + row : first + row + step, :], right[:, at]
            ).astype(BF16)
        out.send()


def early_products(order, scalars, cot_own, cot_other, w_down, w_right, d_joined, placed, d_ffn, flat):
    rows = BLOCK
    for half in (0, 1):
        part = slice(half * rows, (half + 1) * rows)
        cot = (cot_own, cot_other)[half]()[...].astype(F32)
        d_ffn[part, :] = (cot * valid_rows(scalars, half, rows)).astype(BF16)
    transposed(d_ffn, flat)
    place(scalars, flat, placed.buffer, order)
    w_down = w_down()
    for half in (0, 1):
        part = slice(half * rows, (half + 1) * rows)
        d_joined.buffer[part, :] = against(d_ffn[part, :], w_down[...])


def feed_forward(
    orders, scalars, u_own, u_other, w_out, tok_own, tok_other, w_left, w_right, d_joined, placed_d,
    joined, d_left, d_right, branch_out, scale_out, *rest,
):
    grads, (nm, flat, placed_l, placed_r) = rest[:6], rest[6:]
    rows = BLOCK
    c = scalars[0]
    u_own, u_other, w_out = u_own(), u_other(), w_out()
    cols = u_own.shape[1] - 128
    width = 2 * cols
    own = pl.ds(pl.multiple_of(c * cols, cols), cols)
    other = pl.ds(pl.multiple_of((1 - c) * cols, cols), cols)
    for half in (0, 1):
        part = slice(half * rows, (half + 1) * rows)
        swap = slice((1 - half) * rows, (2 - half) * rows)
        total = jnp.zeros((rows, 1), F32)
        for lane in (0, 64):
            total = total + u_own[part, cols + lane : cols + lane + 1].astype(F32)
            total = total + u_other[swap, cols + lane : cols + lane + 1].astype(F32)
        scale = lax.rsqrt(total / width + EPSILON)
        scale_out.buffer[part, :] = jnp.broadcast_to(scale, (rows, 128))
        branch = scale * (
            plain(u_own[part, :cols], w_out[own, :]) + plain(u_other[swap, :cols], w_out[other, :])
        )
        branch_out.buffer[part, :] = branch.astype(BF16)
        ok = valid_rows(scalars, half, rows)
        hidden = (tok_own, tok_other)[half]()[...].astype(F32) + ok * branch
        nm[part, :] = normed_rows(hidden).astype(BF16)
    branch_out.send()
    scale_out.send()
    w_left, w_right, d_joined = w_left(), w_right(), d_joined()
    units = w_left.shape[1]
    for first in range(0, units, 768):
        at = slice(first, min(first + 768, units))
        for half in (0, 1):
            part = slice(half * rows, (half + 1) * rows)
            left = plain(nm[part, :], w_left[:, at])
            right = plain(nm[part, :], w_right[:, at])
            joined.buffer[part, at] = (left * right).astype(BF16)
            d_left.buffer[part, at] = (d_joined[part, at] * right).astype(BF16)
            d_right.buffer[part, at] = (d_joined[part, at] * left).astype(BF16)
    for one in (joined, d_left, d_right):
        one.send()
    transposed(nm, flat)
    place(scalars, flat, placed_l, orders[1])
    place(scalars, flat, placed_r, orders[2])
    pairs = list(zip(grads[0::2], grads[1::2]))
    for i, (placed, right) in enumerate(
        ((placed_d(), joined), (placed_l, d_left), (placed_r, d_right))
    ):
        product(placed, right.buffer, slice(0, units), *pairs[i])


def mid_gradient(d_left, w_left, d_right, w_right, out, total):
    rows = BLOCK
    d_left, w_left = d_left(), w_left()
    step = w_left.shape[0] // 2
    places = [(half * rows, first) for half in (0, 1) for first in (0, step)]
    for row, first in places:
        total[row : row + rows, first : first + step] = against(
            d_left[row : row + rows, :], w_left[first : first + step, :]
        )
    d_right, w_right = d_right(), w_right()
    for row, first in places:
        at = (slice(row, row + rows), slice(first, first + step))
        out.buffer[at] = (
            total[at] + against(d_right[row : row + rows, :], w_right[first : first + step, :])
        ).astype(BF16)


def down_projection(joined, w_down, stays, goes):
    rows = BLOCK
    joined, w_down = joined(), w_down()
    goes.buffer[...] = plain(joined[rows:, :], w_down[...]).astype(BF16)
    goes.send()
    stays.buffer[...] = plain(joined[:rows, :], w_down[...])


def attention_backward(
    orders, scalars, rates, mid_own, mid_other, tok_own, tok_other, cot_own, cot_other, branch, w_out, scale_ref,
    gu, dg, att, u_own, u_other, q, k, v, prior, dq, dk, nin,
    dpre, x_goes, x_stays, y_goes, y_stays, hidden_out,
    d_att, d_branch, gated, flat, flat_gated, *placed,
):
    rows = BLOCK
    cols = dpre.buffer.shape[1] // 4
    c = scalars[0]
    own = pl.ds(pl.multiple_of(c * cols, cols), cols)
    other = pl.ds(pl.multiple_of((1 - c) * cols, cols), cols)
    for half in (0, 1):
        part = slice(half * rows, (half + 1) * rows)
        swap = slice((1 - half) * rows, (2 - half) * rows)
        ok = valid_rows(scalars, half, rows)
        d_mid = mid_own()[part, :].astype(F32) + mid_other()[swap, :].astype(F32)
        x = (tok_own, tok_other)[half]()[...].astype(F32)
        cot = (cot_own, cot_other)[half]()[...].astype(F32)
        lined = branch()[part, :].astype(F32)
        hidden = x + ok * lined
        mid_scale = lax.rsqrt(row_mean(hidden * hidden) + EPSILON)
        normed = hidden * mid_scale
        d_hidden = cot + mid_scale * (d_mid - normed * row_mean(d_mid * normed))
        if half == 0:
            hidden_out.buffer[...] = d_hidden
        d_out = (ok * d_hidden).astype(BF16)
        d_branch[part, :] = d_out
        inner = row_mean(d_out.astype(F32) * lined)
        d_gated = against(d_out, w_out()[...])
        scale = scale_ref()[part, :1]
        normed = att()[part, :].astype(F32) * scale
        dpre.buffer[part, 3 * cols :] = (d_gated * normed * dg()[part, :].astype(F32)).astype(BF16)
        d_att[part, :] = (scale * (d_gated * gu()[part, :].astype(F32) - normed * inner)).astype(BF16)
        gated[part, own] = (u_own()[part, :cols].astype(F32) * scale).astype(BF16)
        gated[part, other] = (u_other()[swap, :cols].astype(F32) * scale).astype(BF16)
    hidden_out.send()
    q, k, v, dq, dk, prior = q(), k(), v(), dq(), dk(), prior()
    heads, size = prior.shape[:2]
    carried = (scalars[2] > rows).astype(F32)
    first = pl.ds(pl.multiple_of(c * rows, rows), rows)
    second = pl.ds(pl.multiple_of((1 - c) * rows, rows), rows)
    row = lax.broadcasted_iota(jnp.int32, (rows, 1), 0)
    for h in range(heads):
        lanes = [slice(i * cols + h * size, i * cols + (h + 1) * size) for i in range(3)]
        at = lanes[0]
        mask, query_decay, key_decay = decays(rates[c * heads + h], rows)
        wide = (q[second, at].astype(F32) * query_decay).astype(BF16)
        state = (outer(wide, d_att[second, at]) * carried).astype(BF16)
        for b, part in enumerate((first, second)):
            q_b, k_b, v_b, d_o = q[part, at], k[part, at], v[part, at], d_att[part, at]
            weighted = (against(q_b, k_b) * mask).astype(BF16)
            d_scores = (against(d_o, v_b) * mask).astype(BF16)
            d_q = plain(d_scores, k_b)
            d_k = outer(d_scores, q_b)
            d_v = outer(weighted, d_o)
            if b == 1:
                d_q = d_q + against(d_o, prior[h]) * query_decay
            else:
                d_k = d_k + against(v_b, state) * key_decay
                d_v = d_v + plain(k_b, state) * key_decay
            ok = jnp.where(b * rows + row < scalars[2], 1.0, 0.0)
            dpre.buffer[part, lanes[0]] = (d_q * dq[part, at].astype(F32)).astype(BF16)
            dpre.buffer[part, lanes[1]] = (d_k * dk[part, at].astype(F32)).astype(BF16)
            dpre.buffer[part, lanes[2]] = (d_v * ok).astype(BF16)
    dpre.send()
    transposed(nin(), flat)
    transposed(gated, flat_gated)
    place(scalars, flat, placed[0], orders[0])
    lanes = x_stays.buffer.shape[1]
    product(placed[0], dpre.buffer, slice(0, lanes), x_stays, x_goes)
    place(scalars, flat, placed[1], orders[1])
    place(scalars, flat_gated, placed[2], orders[1])
    between = dpre.buffer.shape[1] - lanes
    half = flat.shape[0] // 2
    for out, first in ((y_goes, half), (y_stays, 0)):
        for row in range(0, half, 256):
            at = slice(first + row, first + row + 256)
            to = slice(row, row + 256)
            out.buffer[to, :between] = plain(placed[1][at, :], dpre.buffer[:, lanes:]).astype(BF16)
            out.buffer[to, between:] = plain(placed[2][at, :], d_branch[:, own]).astype(BF16)
        out.send()


def input_gradient(scalars, dpre, w_query, w_key, w_value, w_gate, stays, goes, total):
    rows = stays.buffer.shape[0]
    cols = w_query.buffer.shape[1]
    dpre = dpre()
    for i, w in enumerate((w_query, w_key, w_value, w_gate)):
        w = w()
        for half in (0, 1):
            part = slice(half * rows, (half + 1) * rows)
            term = against(dpre[part, i * cols : (i + 1) * cols], w[...])
            if i == 0:
                total[part, :] = term
            elif i < 3:
                total[part, :] += term
            elif half == 0:
                stays.buffer[...] = total[part, :] + term
            else:
                goes.buffer[...] = (total[part, :] + term).astype(BF16)


def finish_rows(
    scalars, tok, branch, ffn_stays, ffn_came, d_hidden, in_stays, in_came, mixed, input_grad
):
    x = tok()[...].astype(F32)
    ffn = ffn_stays()[...] + ffn_came()[...].astype(F32)
    ok = valid_rows(scalars, 0, x.shape[0])
    mixed.buffer[...] = (x + ok * (branch()[...].astype(F32) + ffn)).astype(BF16)
    mixed.send()
    scale = lax.rsqrt(row_mean(x * x) + EPSILON)
    normed = x * scale
    d_in = in_stays()[...] + in_came()[...].astype(F32)
    input_grad.buffer[...] = d_hidden()[...] + scale * (d_in - normed * row_mean(d_in * normed))


def join_columns(scalars, *refs):
    ins, outs = refs[:8], refs[8:]
    cols = outs[0].buffer.shape[1] // 2
    own = pl.multiple_of(scalars[0] * cols, cols)
    other = pl.multiple_of((1 - scalars[0]) * cols, cols)
    step = 128
    for first, side in ((own, 0), (other, 2)):
        place_at = 0
        for i in range(2):
            total = ins[side + i]()[...].astype(F32) + ins[4 + side + i]()[...].astype(F32)
            for at in range(0, total.shape[1], step):
                lanes = pl.ds(pl.multiple_of(first + place_at % cols, step), step)
                outs[place_at // cols].buffer[:, lanes] = total[:, at : at + step]
                place_at += step


ORDERS = {"D": "yxab", "L": "xbya", "R": "axyb", "X": "axyb", "Y": "yxab"}
WAITS = "RYDRXYLRDXYLDXLYX"


def on_device(
    tokens,
    seq_lens,
    decay_rate,
    w_query,
    w_key,
    w_value,
    w_gate_u,
    w_out,
    w_left,
    w_right,
    w_down,
    cotangent,
):
    n_wide = lax.axis_size("wide")
    bits = n_wide.bit_length() - 1
    tail = list(range(4, bits))
    orders = {c: ["xyab".index(d) for d in dims] + tail for c, dims in ORDERS.items()}
    ffn_orders = [orders[c] for c in "DLR"]
    attn_orders = [orders[c] for c in "XY"]
    rows, width = tokens.shape
    units = w_left.shape[1]
    heads = decay_rate.shape[0] // 2
    size = width // decay_rate.shape[0]
    cols = width // 2
    group = 2 * rows
    c = lax.axis_index("narrow")
    scalars = jnp.stack([c, lax.axis_index("wide"), seq_lens[0, 0]]).astype(jnp.int32)

    def other(v):
        return lax.ppermute(v, "narrow", [(0, 1), (1, 0)])

    def over(v, bit):
        return lax.ppermute(v, "wide", [(i, i ^ (1 << bit)) for i in range(n_wide)])

    def half_cols(s, ref):
        return ref.at[:, pl.ds(pl.multiple_of(s[0] * cols, cols), cols)]

    def half_rows(s, ref):
        return ref.at[pl.ds(pl.multiple_of(s[0] * cols, cols), cols), :]

    halves = (half_cols, (width, cols))
    small = (scalars,)
    tok_other, cot_other = other(tokens), other(cotangent)
    weights = (w_query, w_key, w_value, w_gate_u)
    *held, nin_own, q, k, v, dq, dk, gu, dg, gate = call(
        project_own,
        [here((width, cols))] * 4
        + [here((rows, width))]
        + [here((rows, cols))] * 7
        + [here((rows, cols), F32)],
        small,
        (tokens, *weights),
        parts={i: halves for i in (1, 2, 3, 4)},
        into={1: 0, 2: 1, 3: 2, 4: 3},
        window=5,
        name="project_own",
    )
    u, nin, q, k, v, dq, dk, gu, dg, att, prior, out_held, left_held = call(
        attention_forward,
        [here((group, cols + 128)), arr((group, width))]
        + [arr((group, cols))] * 8
        + [arr((heads, size, size)), here((width, width)), here((width, units))],
        (scalars, decay_rate),
        (nin_own, q, k, v, dq, dk, gu, dg, gate, tok_other, *held, w_out, w_left),
        into={14: 11, 15: 12},
        inside=(0, 1, 2, 3, 4, 5, 6, 7, 8, 10, 11, 12, 13),
        after=(cot_other,),
        near=(9,),
        scratch=[pltpu.VMEM((group, cols), F32)],
        name="attention_forward",
    )
    u_other = other(u)
    down_held, right_held, d_joined, placed_d = call(
        functools.partial(early_products, orders["D"]),
        [here((units, width)), here((width, units))]
        + [here((group, units), F32), here((width, group))],
        small,
        (cotangent, cot_other, w_down, w_right),
        after=(u,),
        near=(1,),
        into={2: 0, 3: 1},
        scratch=[pltpu.VMEM((group, width), BF16), pltpu.VMEM((width, group), BF16)],
        window=6,
        name="early_products",
    )
    part = here((width // 2, units))
    joined, d_left, d_right, branch, scale, *grads = call(
        functools.partial(feed_forward, ffn_orders),
        [here((group, units))] * 3
        + [arr((group, width)), arr((group, 128), F32)]
        + [part] * 6,
        small,
        (u, u_other, out_held, tokens, tok_other, left_held, right_held, d_joined, placed_d),
        inside=(0, 2, 5, 6, 7, 8),
        near=(1, 4),
        scratch=[pltpu.VMEM((group, width), BF16)] + [pltpu.VMEM((width, group), BF16)] * 3,
        name="feed_forward",
    )
    (mid,) = call(
        mid_gradient,
        [here((group, width))],
        (),
        (d_left, left_held, d_right, right_held),
        inside=(0, 1, 2, 3),
        scratch=[pltpu.VMEM((group, width), F32)],
        name="mid_gradient",
    )
    mid_other = other(mid)
    attn_part = (width // 2, 5 * cols // 2)
    dpre, x_goes, x_stays, y_goes, y_stays, d_hidden = call(
        functools.partial(attention_backward, attn_orders),
        [here((group, 4 * cols))]
        + [here(attn_part)] * 4
        + [arr((rows, width), F32)],
        (scalars, decay_rate),
        (mid, mid_other, tokens, tok_other, cotangent, cot_other, branch, w_out, scale)
        + (gu, dg, att, u, u_other, q, k, v, prior, dq, dk, nin),
        parts={7: (half_rows, (cols, width))},
        inside=(0,),
        near=(1, 3, 5, 12, 13),
        window=8,
        scratch=[pltpu.VMEM((group, cols), BF16)]
        + [pltpu.VMEM((group, width), BF16)] * 2
        + [pltpu.VMEM((width, group), BF16)] * 5,
        name="attention_backward",
    )
    ffn_stays, ffn_goes = call(
        down_projection,
        [here((rows, width), F32), here((rows, width))],
        (),
        (joined, down_held),
        inside=(0, 1),
        after=(dpre,),
        name="down_projection",
    )
    ffn_came = other(ffn_goes)
    in_stays, in_goes = call(
        input_gradient,
        [arr((rows, width), F32), here((rows, width))],
        small,
        (dpre, w_query, w_key, w_value, w_gate_u),
        inside=(0,),
        after=(ffn_goes,),
        parts={i: halves for i in (1, 2, 3, 4)},
        scratch=[pltpu.VMEM((group, width), F32)],
        name="input_gradient",
    )
    in_came = other(in_goes)

    held_parts = dict(zip("DLR", zip(grads[0::2], grads[1::2])))
    held_parts.update(X=(x_stays, x_goes), Y=(y_stays, y_goes))

    def add(chunk, came):
        stays = held_parts[chunk][0]
        total = stays.astype(F32) + came.astype(F32)
        half = total.shape[0] // 2
        held_parts[chunk] = total[:half].astype(BF16), total[half:].astype(BF16)
        return held_parts[chunk][1]

    first = [over(held_parts[c][1], orders[c][0]) for c in "RDL"]
    *first, last = lax.optimization_barrier((*first, in_stays))
    for chunk, came in zip("RDL", first):
        came, last = lax.optimization_barrier((came, last))
        last = add(chunk, came)
    mixed, input_grad = call(
        finish_rows,
        [arr((rows, width)), arr((rows, width), F32)],
        small,
        (tokens, branch, ffn_stays, ffn_came, d_hidden, in_stays, in_came),
        after=(last,),
        parts={1: (lambda s, ref: ref.at[pl.ds(0, rows), :], (rows, width))},
        near=(2, 3, 6),
        window=7,
        name="finish_rows",
    )
    last = mixed
    arrived, full = {}, {}
    done = dict(D=1, L=1, R=1, X=0, Y=0)
    for chunk in WAITS:
        first = done[chunk]
        done[chunk] += 1
        for phase in range(first, bits if first == 3 else first + 1):
            came = over(held_parts[chunk][1], orders[chunk][phase])
            came, last = lax.optimization_barrier((came, last))
            if phase == bits - 1:
                arrived[chunk] = last = came
                if chunk in "DLR":
                    last = full[chunk] = held_parts[chunk][0].astype(F32) + came.astype(F32)
            else:
                last = add(chunk, came)
    slab = width // n_wide
    stays = [held_parts[c][0] for c in "XY"]
    came = [arrived[c] for c in "XY"]
    joint = call(
        join_columns,
        [arr((slab, width), F32)] * 5,
        small,
        (*stays, *map(other, stays), *came, *map(other, came)),
        inside=range(8),
        name="join_columns",
    )
    grad_left, grad_right, grad_down = full["L"], full["R"], full["D"].T
    return (mixed, input_grad, *joint, grad_left, grad_right, grad_down)


def solution(mesh):
    placed = (
        P(("wide", "narrow"), None),
        P("wide", None),
        P(),
        P(),
        P(),
        P(),
        P(),
        P(),
        P(None, "narrow"),
        P(None, "narrow"),
        P("narrow", None),
        P(("wide", "narrow"), None),
    )
    return jax.shard_map(
        on_device,
        mesh=mesh,
        in_specs=placed,
        out_specs=(
            P(("wide", "narrow"), None),
            P(("wide", "narrow"), None),
            P("wide", None),
            P("wide", None),
            P("wide", None),
            P("wide", None),
            P("wide", None),
            P("wide", "narrow"),
            P("wide", "narrow"),
            P("narrow", "wide"),
        ),
        check_vma=False,
    )
```

```python
import functools
import math

import jax
import jax.numpy as jnp
from jax import lax
from jax.experimental import pallas as pl
from jax.experimental.pallas import tpu as pltpu
from jax.sharding import PartitionSpec as P

BLOCK = 256
EPSILON = 1e-06
F32 = jnp.float32
BF16 = jnp.bfloat16


def plain(a, b):
    return jnp.dot(a, b, preferred_element_type=F32)


def against(a, b):
    return lax.dot_general(a, b, (((1,), (1,)), ((), ())), preferred_element_type=F32)


def outer(a, b):
    return lax.dot_general(a, b, (((0,), (0,)), ((), ())), preferred_element_type=F32)


def row_mean(v):
    return jnp.mean(v, axis=-1, keepdims=True)


def valid_rows(scalars, half, rows):
    c, length = scalars[0], scalars[2]
    first = rows * (c if half == 0 else 1 - c)
    return (first + lax.broadcasted_iota(jnp.int32, (rows, 1), 0) < length).astype(F32)


def decays(rate, n):
    i = lax.broadcasted_iota(jnp.int32, (n, n), 0)
    j = lax.broadcasted_iota(jnp.int32, (n, n), 1)
    gap = (i - j).astype(F32)
    mask = jnp.where(gap >= 0, jnp.exp(-rate * jnp.maximum(gap, 0.0)), 0.0)
    step = lax.broadcasted_iota(jnp.int32, (n, 1), 0).astype(F32)
    return mask, jnp.exp(-rate * (step + 1.0)), jnp.exp(-rate * (n - 1.0 - step))


def silu_parts(pre):
    sig = jax.nn.sigmoid(pre)
    act = pre * sig
    return act, sig + act * (1.0 - sig)


class Loaded:
    def __init__(self, source, buffer, sem, queue):
        self.buffer, self.copy, self.ready = buffer, pltpu.make_async_copy(source, buffer, sem), False
        self.queue = queue
        queue.append(self)

    def __call__(self):
        if not self.ready:
            while self in self.queue:
                self.queue.pop(0).copy.start()
            self.copy.wait()
            self.ready = True
            if self.queue:
                self.queue.pop(0).copy.start()
        return self.buffer


class Stored:
    def __init__(self, target, buffer, sem):
        self.buffer, self.copy, self.sent = buffer, pltpu.make_async_copy(buffer, target, sem), False

    def send(self):
        if not self.sent:
            self.copy.start()
            self.sent = True

    def finish(self):
        self.send()
        self.copy.wait()


class Here:
    def __init__(self, buffer):
        self.buffer = buffer

    def __call__(self):
        return self.buffer

    def send(self):
        pass

    def finish(self):
        pass


ANY = pl.BlockSpec(memory_space=pl.ANY)
VMEM = pl.BlockSpec(memory_space=pltpu.VMEM)
SMEM = pl.BlockSpec(memory_space=pltpu.SMEM)


def arr(shape, dtype=BF16):
    return jax.ShapeDtypeStruct(shape, dtype)


class here:
    def __init__(self, shape, dtype=BF16):
        self.shape, self.dtype = shape, jnp.dtype(dtype)


def call(
    body, outs, small, args, after=(), parts=None, scratch=(), window=4, slack=8, near=(), inside=(),
    into=None, name=None,
):
    parts, into = parts or {}, into or {}
    args = [
        a if i in near else pltpu.with_memory_space_constraint(a, pltpu.VMEM if i in inside else pltpu.HBM)
        for i, a in enumerate(args)
    ]
    shapes = [parts[i][1] if i in parts else a.shape for i, a in enumerate(args)]
    n_small, n_in, n_out, n_after = len(small), len(args), len(outs), len(after)
    copied = [i for i in range(n_in) if i not in inside and i not in into]
    sent = [i for i in range(n_out) if not isinstance(outs[i], here)]

    def kernel(*refs):
        scalars = refs[:n_small]
        at = n_small
        sources = refs[at : at + n_in]
        at += n_in + n_after
        targets = refs[at : at + n_out]
        at += n_out
        in_bufs = dict(zip(copied, refs[at:]))
        at += len(copied)
        out_bufs = dict(zip(sent, refs[at:]))
        at += len(sent)
        in_sem, out_sem = refs[at : at + 2]
        queue = []
        loaded = []
        for i, source in enumerate(sources):
            if i in inside:
                loaded.append(Here(source))
                continue
            source = parts[i][0](scalars[0], source) if i in parts else source
            buffer = targets[into[i]] if i in into else in_bufs[i]
            loaded.append(Loaded(source, buffer, in_sem.at[i], queue))
        for _ in range(min(window, len(queue))):
            queue.pop(0).copy.start()
        stored = [
            Stored(t, out_bufs[i], out_sem.at[i]) if i in out_bufs else Here(t)
            for i, t in enumerate(targets)
        ]
        results = [one for i, one in enumerate(stored) if i not in into.values()]
        body(*scalars, *loaded, *results, *refs[at + 2 :])
        for one in loaded:
            one()
        for one in stored:
            one.send()
        for one in stored:
            one.finish()

    buffers = [pltpu.VMEM(shapes[i], args[i].dtype) for i in copied]
    buffers += [pltpu.VMEM(outs[i].shape, outs[i].dtype) for i in sent]
    held = sum(b.dtype.itemsize * math.prod(b.shape) for b in [*buffers, *scratch])
    return pl.pallas_call(
        kernel,
        in_specs=[SMEM] * n_small
        + [VMEM if i in inside else ANY for i in range(n_in)]
        + [ANY] * n_after,
        out_specs=[ANY if i in sent else VMEM for i in range(n_out)],
        out_shape=[
            (pltpu.HBM if i in sent else pltpu.VMEM)(o.shape, o.dtype) for i, o in enumerate(outs)
        ],
        scratch_shapes=buffers
        + [pltpu.SemaphoreType.DMA((max(n_in, 1),)), pltpu.SemaphoreType.DMA((max(n_out, 1),))]
        + list(scratch),
        name=name,
        compiler_params=pltpu.CompilerParams(vmem_limit_bytes=held + (slack << 20)),
    )(*small, *args, *after)


def normed_rows(x):
    return x * lax.rsqrt(row_mean(x * x) + EPSILON)


def activations(i, pre, ok, part, q, k, v, dq, dk, gu, dg, gate):
    if i == 2:
        v[part, :] = (pre * ok).astype(BF16)
        return
    act, slope = silu_parts(pre)
    if i == 0:
        q[part, :] = act.astype(BF16)
        dq[part, :] = slope.astype(BF16)
    elif i == 1:
        k[part, :] = (act * ok).astype(BF16)
        dk[part, :] = (slope * ok).astype(BF16)
    else:
        gate[part, :] = act
        gu[part, :] = act.astype(BF16)
        dg[part, :] = slope.astype(BF16)


def project_own(scalars, tok, w_query, w_key, w_value, w_gate, nin, *outs):
    nin.buffer[...] = normed_rows(tok()[...].astype(F32)).astype(BF16)
    rows = nin.buffer.shape[0]
    ok = valid_rows(scalars, 0, rows)
    outs = [out.buffer for out in outs]
    for i, w in enumerate((w_query, w_key, w_value, w_gate)):
        activations(i, plain(nin.buffer[...], w()[...]), ok, slice(0, rows), *outs)


def attention_forward(
    scalars, rates, nin_own, *refs
):
    own, (tok_other, w_query, w_key, w_value, w_gate, w_out, w_left) = refs[:8], refs[8:15]
    (u, nin, q, k, v, dq, dk, gu, dg, att_out, prior_out), (gate_buf,) = refs[15:26], refs[26:]
    rows, cols = BLOCK, q.buffer.shape[1]
    c = scalars[0]
    nin.buffer[:rows, :] = nin_own()[...]
    nin.buffer[rows:, :] = normed_rows(tok_other()[...].astype(F32)).astype(BF16)
    nin.send()
    kept = [*(one.buffer for one in (q, k, v, dq, dk, gu, dg)), gate_buf]
    for mine, whole in zip(own, kept):
        whole[:rows, :] = mine()[...]
    ok = valid_rows(scalars, 1, rows)
    for i, w in enumerate((w_query, w_key, w_value, w_gate)):
        activations(i, plain(nin.buffer[rows:, :], w()[...]), ok, slice(rows, 2 * rows), *kept)
    for one in (q, dq, k, dk, v, gu, dg):
        one.send()
    heads, size = prior_out.buffer.shape[:2]
    carried = (scalars[2] > rows).astype(F32)
    first = pl.ds(pl.multiple_of(c * rows, rows), rows)
    second = pl.ds(pl.multiple_of((1 - c) * rows, rows), rows)
    squares = [jnp.zeros((rows, 1), F32), jnp.zeros((rows, 1), F32)]
    for h in range(heads):
        at = slice(h * size, (h + 1) * size)
        mask, query_decay, key_decay = decays(rates[c * heads + h], rows)
        wide = (k.buffer[first, at].astype(F32) * key_decay).astype(BF16)
        prior = (outer(wide, v.buffer[first, at]) * carried).astype(BF16)
        prior_out.buffer[h] = prior
        for b, part in enumerate((first, second)):
            queries = q.buffer[part, at]
            weighted = (against(queries, k.buffer[part, at]) * mask).astype(BF16)
            att = plain(weighted, v.buffer[part, at])
            if b == 1:
                att = att + plain(queries, prior) * query_decay
            att_out.buffer[part, at] = att.astype(BF16)
            u.buffer[part, at] = (att * gate_buf[part, at]).astype(BF16)
            squares[b] = squares[b] + jnp.sum(att * att, axis=-1, keepdims=True)
    lane = lax.broadcasted_iota(jnp.int32, (rows, 128), 1)
    for b, part in enumerate((first, second)):
        high = squares[b].astype(BF16).astype(F32)
        low = squares[b] - high
        u.buffer[part, cols:] = jnp.where(lane < 64, high, low).astype(BF16)


def block_at(wide, dims, pos):
    mask = 0
    for i, d in enumerate(dims):
        if pos >> (len(dims) - 1 - i) & 1:
            mask |= 1 << d
    return wide ^ mask


def transposed(source, flat):
    for at in range(0, flat.shape[0], 128):
        flat[at : at + 128, :] = source[:, at : at + 128].T


def place(scalars, flat, placed, dims):
    n = 1 << len(dims)
    rows = flat.shape[0] // n
    for pos in range(n):
        block = block_at(scalars[1], dims, pos)
        placed[pos * rows : (pos + 1) * rows, :] = flat[
            pl.ds(pl.multiple_of(block * rows, rows), rows), :
        ]


def product(placed, right, at, stays, goes):
    half = placed.shape[0] // 2
    step = 256
    for out, first in ((goes, half), (stays, 0)):
        for row in range(0, half, step):
            out.buffer[row : row + step, :] = plain(
                placed[first + row : first + row + step, :], right[:, at]
            ).astype(BF16)
        out.send()


def early_products(order, scalars, cot_own, cot_other, w_down, w_right, d_joined, placed, d_ffn, flat):
    rows = BLOCK
    for half in (0, 1):
        part = slice(half * rows, (half + 1) * rows)
        cot = (cot_own, cot_other)[half]()[...].astype(F32)
        d_ffn[part, :] = (cot * valid_rows(scalars, half, rows)).astype(BF16)
    transposed(d_ffn, flat)
    place(scalars, flat, placed.buffer, order)
    w_down = w_down()
    for half in (0, 1):
        part = slice(half * rows, (half + 1) * rows)
        d_joined.buffer[part, :] = against(d_ffn[part, :], w_down[...])


def feed_forward(
    orders, scalars, u_own, u_other, w_out, tok_own, tok_other, w_left, w_right, d_joined, placed_d,
    joined, d_left, d_right, branch_out, scale_out, *rest,
):
    grads, (nm, flat, placed_l, placed_r) = rest[:6], rest[6:]
    rows = BLOCK
    c = scalars[0]
    u_own, u_other, w_out = u_own(), u_other(), w_out()
    cols = u_own.shape[1] - 128
    width = 2 * cols
    own = pl.ds(pl.multiple_of(c * cols, cols), cols)
    other = pl.ds(pl.multiple_of((1 - c) * cols, cols), cols)
    for half in (0, 1):
        part = slice(half * rows, (half + 1) * rows)
        swap = slice((1 - half) * rows, (2 - half) * rows)
        total = jnp.zeros((rows, 1), F32)
        for lane in (0, 64):
            total = total + u_own[part, cols + lane : cols + lane + 1].astype(F32)
            total = total + u_other[swap, cols + lane : cols + lane + 1].astype(F32)
        scale = lax.rsqrt(total / width + EPSILON)
        scale_out.buffer[part, :] = jnp.broadcast_to(scale, (rows, 128))
        branch = scale * (
            plain(u_own[part, :cols], w_out[own, :]) + plain(u_other[swap, :cols], w_out[other, :])
        )
        branch_out.buffer[part, :] = branch.astype(BF16)
        ok = valid_rows(scalars, half, rows)
        hidden = (tok_own, tok_other)[half]()[...].astype(F32) + ok * branch
        nm[part, :] = normed_rows(hidden).astype(BF16)
    branch_out.send()
    scale_out.send()
    w_left, w_right, d_joined = w_left(), w_right(), d_joined()
    units = w_left.shape[1]
    for first in range(0, units, 768):
        at = slice(first, min(first + 768, units))
        for half in (0, 1):
            part = slice(half * rows, (half + 1) * rows)
            left = plain(nm[part, :], w_left[:, at])
            right = plain(nm[part, :], w_right[:, at])
            joined.buffer[part, at] = (left * right).astype(BF16)
            d_left.buffer[part, at] = (d_joined[part, at] * right).astype(BF16)
            d_right.buffer[part, at] = (d_joined[part, at] * left).astype(BF16)
    for one in (joined, d_left, d_right):
        one.send()
    transposed(nm, flat)
    place(scalars, flat, placed_l, orders[1])
    place(scalars, flat, placed_r, orders[2])
    pairs = list(zip(grads[0::2], grads[1::2]))
    for i, (placed, right) in enumerate(
        ((placed_d(), joined), (placed_l, d_left), (placed_r, d_right))
    ):
        product(placed, right.buffer, slice(0, units), *pairs[i])


def mid_gradient(d_left, w_left, d_right, w_right, out, total):
    rows = BLOCK
    d_left, w_left = d_left(), w_left()
    step = w_left.shape[0] // 2
    places = [(half * rows, first) for half in (0, 1) for first in (0, step)]
    for row, first in places:
        total[row : row + rows, first : first + step] = against(
            d_left[row : row + rows, :], w_left[first : first + step, :]
        )
    d_right, w_right = d_right(), w_right()
    for row, first in places:
        at = (slice(row, row + rows), slice(first, first + step))
        out.buffer[at] = (
            total[at] + against(d_right[row : row + rows, :], w_right[first : first + step, :])
        ).astype(BF16)


def down_projection(joined, w_down, stays, goes):
    rows = BLOCK
    joined, w_down = joined(), w_down()
    goes.buffer[...] = plain(joined[rows:, :], w_down[...]).astype(BF16)
    goes.send()
    stays.buffer[...] = plain(joined[:rows, :], w_down[...])


def attention_backward(
    orders, scalars, rates, mid_own, mid_other, tok_own, tok_other, cot_own, cot_other, branch, w_out, scale_ref,
    gu, dg, att, u_own, u_other, q, k, v, prior, dq, dk, nin,
    dpre, x_goes, x_stays, y_goes, y_stays, hidden_out,
    d_att, d_branch, gated, flat, flat_gated, *placed,
):
    rows = BLOCK
    cols = dpre.buffer.shape[1] // 4
    c = scalars[0]
    own = pl.ds(pl.multiple_of(c * cols, cols), cols)
    other = pl.ds(pl.multiple_of((1 - c) * cols, cols), cols)
    for half in (0, 1):
        part = slice(half * rows, (half + 1) * rows)
        swap = slice((1 - half) * rows, (2 - half) * rows)
        ok = valid_rows(scalars, half, rows)
        d_mid = mid_own()[part, :].astype(F32) + mid_other()[swap, :].astype(F32)
        x = (tok_own, tok_other)[half]()[...].astype(F32)
        cot = (cot_own, cot_other)[half]()[...].astype(F32)
        lined = branch()[part, :].astype(F32)
        hidden = x + ok * lined
        mid_scale = lax.rsqrt(row_mean(hidden * hidden) + EPSILON)
        normed = hidden * mid_scale
        d_hidden = cot + mid_scale * (d_mid - normed * row_mean(d_mid * normed))
        if half == 0:
            hidden_out.buffer[...] = d_hidden
        d_out = (ok * d_hidden).astype(BF16)
        d_branch[part, :] = d_out
        inner = row_mean(d_out.astype(F32) * lined)
        d_gated = against(d_out, w_out()[...])
        scale = scale_ref()[part, :1]
        normed = att()[part, :].astype(F32) * scale
        dpre.buffer[part, 3 * cols :] = (d_gated * normed * dg()[part, :].astype(F32)).astype(BF16)
        d_att[part, :] = (scale * (d_gated * gu()[part, :].astype(F32) - normed * inner)).astype(BF16)
        gated[part, own] = (u_own()[part, :cols].astype(F32) * scale).astype(BF16)
        gated[part, other] = (u_other()[swap, :cols].astype(F32) * scale).astype(BF16)
    hidden_out.send()
    q, k, v, dq, dk, prior = q(), k(), v(), dq(), dk(), prior()
    heads, size = prior.shape[:2]
    carried = (scalars[2] > rows).astype(F32)
    first = pl.ds(pl.multiple_of(c * rows, rows), rows)
    second = pl.ds(pl.multiple_of((1 - c) * rows, rows), rows)
    row = lax.broadcasted_iota(jnp.int32, (rows, 1), 0)
    for h in range(heads):
        lanes = [slice(i * cols + h * size, i * cols + (h + 1) * size) for i in range(3)]
        at = lanes[0]
        mask, query_decay, key_decay = decays(rates[c * heads + h], rows)
        wide = (q[second, at].astype(F32) * query_decay).astype(BF16)
        state = (outer(wide, d_att[second, at]) * carried).astype(BF16)
        for b, part in enumerate((first, second)):
            q_b, k_b, v_b, d_o = q[part, at], k[part, at], v[part, at], d_att[part, at]
            weighted = (against(q_b, k_b) * mask).astype(BF16)
            d_scores = (against(d_o, v_b) * mask).astype(BF16)
            d_q = plain(d_scores, k_b)
            d_k = outer(d_scores, q_b)
            d_v = outer(weighted, d_o)
            if b == 1:
                d_q = d_q + against(d_o, prior[h]) * query_decay
            else:
                d_k = d_k + against(v_b, state) * key_decay
                d_v = d_v + plain(k_b, state) * key_decay
            ok = jnp.where(b * rows + row < scalars[2], 1.0, 0.0)
            dpre.buffer[part, lanes[0]] = (d_q * dq[part, at].astype(F32)).astype(BF16)
            dpre.buffer[part, lanes[1]] = (d_k * dk[part, at].astype(F32)).astype(BF16)
            dpre.buffer[part, lanes[2]] = (d_v * ok).astype(BF16)
    dpre.send()
    transposed(nin(), flat)
    transposed(gated, flat_gated)
    place(scalars, flat, placed[0], orders[0])
    lanes = x_stays.buffer.shape[1]
    product(placed[0], dpre.buffer, slice(0, lanes), x_stays, x_goes)
    place(scalars, flat, placed[1], orders[1])
    place(scalars, flat_gated, placed[2], orders[1])
    between = dpre.buffer.shape[1] - lanes
    half = flat.shape[0] // 2
    for out, first in ((y_goes, half), (y_stays, 0)):
        for row in range(0, half, 256):
            at = slice(first + row, first + row + 256)
            to = slice(row, row + 256)
            out.buffer[to, :between] = plain(placed[1][at, :], dpre.buffer[:, lanes:]).astype(BF16)
            out.buffer[to, between:] = plain(placed[2][at, :], d_branch[:, own]).astype(BF16)
        out.send()


def input_gradient(scalars, dpre, w_query, w_key, w_value, w_gate, stays, goes, total):
    rows = stays.buffer.shape[0]
    cols = w_query.buffer.shape[1]
    dpre = dpre()
    for i, w in enumerate((w_query, w_key, w_value, w_gate)):
        w = w()
        for half in (0, 1):
            part = slice(half * rows, (half + 1) * rows)
            term = against(dpre[part, i * cols : (i + 1) * cols], w[...])
            if i == 0:
                total[part, :] = term
            elif i < 3:
                total[part, :] += term
            elif half == 0:
                stays.buffer[...] = total[part, :] + term
            else:
                goes.buffer[...] = (total[part, :] + term).astype(BF16)


def finish_rows(
    scalars, tok, branch, ffn_stays, ffn_came, d_hidden, in_stays, in_came, mixed, input_grad
):
    x = tok()[...].astype(F32)
    ffn = ffn_stays()[...] + ffn_came()[...].astype(F32)
    ok = valid_rows(scalars, 0, x.shape[0])
    mixed.buffer[...] = (x + ok * (branch()[...].astype(F32) + ffn)).astype(BF16)
    mixed.send()
    scale = lax.rsqrt(row_mean(x * x) + EPSILON)
    normed = x * scale
    d_in = in_stays()[...] + in_came()[...].astype(F32)
    input_grad.buffer[...] = d_hidden()[...] + scale * (d_in - normed * row_mean(d_in * normed))


def join_columns(scalars, *refs):
    ins, outs = refs[:8], refs[8:]
    cols = outs[0].buffer.shape[1] // 2
    own = pl.multiple_of(scalars[0] * cols, cols)
    other = pl.multiple_of((1 - scalars[0]) * cols, cols)
    step = 128
    for first, side in ((own, 0), (other, 2)):
        place_at = 0
        for i in range(2):
            total = ins[side + i]()[...].astype(F32) + ins[4 + side + i]()[...].astype(F32)
            for at in range(0, total.shape[1], step):
                lanes = pl.ds(pl.multiple_of(first + place_at % cols, step), step)
                outs[place_at // cols].buffer[:, lanes] = total[:, at : at + step]
                place_at += step


ORDERS = {"D": "yxab", "L": "xbya", "R": "axyb", "X": "axyb", "Y": "yxab"}
WAITS = "RYDRXYLRDXYLDXLYX"


def on_device(
    tokens,
    seq_lens,
    decay_rate,
    w_query,
    w_key,
    w_value,
    w_gate_u,
    w_out,
    w_left,
    w_right,
    w_down,
    cotangent,
):
    n_wide = lax.axis_size("wide")
    bits = n_wide.bit_length() - 1
    tail = list(range(4, bits))
    orders = {c: ["xyab".index(d) for d in dims] + tail for c, dims in ORDERS.items()}
    ffn_orders = [orders[c] for c in "DLR"]
    attn_orders = [orders[c] for c in "XY"]
    rows, width = tokens.shape
    units = w_left.shape[1]
    heads = decay_rate.shape[0] // 2
    size = width // decay_rate.shape[0]
    cols = width // 2
    group = 2 * rows
    c = lax.axis_index("narrow")
    scalars = jnp.stack([c, lax.axis_index("wide"), seq_lens[0, 0]]).astype(jnp.int32)

    def other(v):
        return lax.ppermute(v, "narrow", [(0, 1), (1, 0)])

    def over(v, bit):
        return lax.ppermute(v, "wide", [(i, i ^ (1 << bit)) for i in range(n_wide)])

    def half_cols(s, ref):
        return ref.at[:, pl.ds(pl.multiple_of(s[0] * cols, cols), cols)]

    def half_rows(s, ref):
        return ref.at[pl.ds(pl.multiple_of(s[0] * cols, cols), cols), :]

    halves = (half_cols, (width, cols))
    small = (scalars,)
    tok_other, cot_other = other(tokens), other(cotangent)
    weights = (w_query, w_key, w_value, w_gate_u)
    *held, nin_own, q, k, v, dq, dk, gu, dg, gate = call(
        project_own,
        [here((width, cols))] * 4
        + [here((rows, width))]
        + [here((rows, cols))] * 7
        + [here((rows, cols), F32)],
        small,
        (tokens, *weights),
        parts={i: halves for i in (1, 2, 3, 4)},
        into={1: 0, 2: 1, 3: 2, 4: 3},
        window=3,
        name="project_own",
    )
    u, nin, q, k, v, dq, dk, gu, dg, att, prior, out_held, left_held = call(
        attention_forward,
        [here((group, cols + 128)), arr((group, width))]
        + [arr((group, cols))] * 8
        + [arr((heads, size, size)), here((width, width)), here((width, units))],
        (scalars, decay_rate),
        (nin_own, q, k, v, dq, dk, gu, dg, gate, tok_other, *held, w_out, w_left),
        into={14: 11, 15: 12},
        inside=(0, 1, 2, 3, 4, 5, 6, 7, 8, 10, 11, 12, 13),
        after=(cot_other,),
        near=(9,),
        scratch=[pltpu.VMEM((group, cols), F32)],
        name="attention_forward",
    )
    u_other = other(u)
    down_held, right_held, d_joined, placed_d = call(
        functools.partial(early_products, orders["D"]),
        [here((units, width)), here((width, units))]
        + [here((group, units), F32), here((width, group))],
        small,
        (cotangent, cot_other, w_down, w_right),
        after=(u,),
        near=(1,),
        into={2: 0, 3: 1},
        scratch=[pltpu.VMEM((group, width), BF16), pltpu.VMEM((width, group), BF16)],
        window=3,
        name="early_products",
    )
    part = here((width // 2, units))
    joined, d_left, d_right, branch, scale, *grads = call(
        functools.partial(feed_forward, ffn_orders),
        [here((group, units))] * 3
        + [arr((group, width)), arr((group, 128), F32)]
        + [part] * 6,
        small,
        (u, u_other, out_held, tokens, tok_other, left_held, right_held, d_joined, placed_d),
        inside=(0, 2, 5, 6, 7, 8),
        near=(1, 4),
        scratch=[pltpu.VMEM((group, width), BF16)] + [pltpu.VMEM((width, group), BF16)] * 3,
        name="feed_forward",
    )
    (mid,) = call(
        mid_gradient,
        [here((group, width))],
        (),
        (d_left, left_held, d_right, right_held),
        inside=(0, 1, 2, 3),
        scratch=[pltpu.VMEM((group, width), F32)],
        name="mid_gradient",
    )
    mid_other = other(mid)
    attn_part = (width // 2, 5 * cols // 2)
    dpre, x_goes, x_stays, y_goes, y_stays, d_hidden = call(
        functools.partial(attention_backward, attn_orders),
        [here((group, 4 * cols))]
        + [here(attn_part)] * 4
        + [arr((rows, width), F32)],
        (scalars, decay_rate),
        (mid, mid_other, tokens, tok_other, cotangent, cot_other, branch, w_out, scale)
        + (gu, dg, att, u, u_other, q, k, v, prior, dq, dk, nin),
        parts={7: (half_rows, (cols, width))},
        inside=(0,),
        near=(1, 3, 5, 12, 13),
        window=8,
        scratch=[pltpu.VMEM((group, cols), BF16)]
        + [pltpu.VMEM((group, width), BF16)] * 2
        + [pltpu.VMEM((width, group), BF16)] * 5,
        slack=4,
        name="attention_backward",
    )
    ffn_stays, ffn_goes = call(
        down_projection,
        [here((rows, width), F32), here((rows, width))],
        (),
        (joined, down_held),
        inside=(0, 1),
        after=(dpre,),
        name="down_projection",
    )
    ffn_came = other(ffn_goes)
    in_stays, in_goes = call(
        input_gradient,
        [arr((rows, width), F32), here((rows, width))],
        small,
        (dpre, w_query, w_key, w_value, w_gate_u),
        inside=(0,),
        after=(ffn_goes,),
        parts={i: halves for i in (1, 2, 3, 4)},
        scratch=[pltpu.VMEM((group, width), F32)],
        name="input_gradient",
    )
    in_came = other(in_goes)

    held_parts = dict(zip("DLR", zip(grads[0::2], grads[1::2])))
    held_parts.update(X=(x_stays, x_goes), Y=(y_stays, y_goes))

    def add(chunk, came):
        stays = held_parts[chunk][0]
        total = stays.astype(F32) + came.astype(F32)
        half = total.shape[0] // 2
        held_parts[chunk] = total[:half].astype(BF16), total[half:].astype(BF16)
        return held_parts[chunk][1]

    first = [over(held_parts[c][1], orders[c][0]) for c in "RDL"]
    *first, last = lax.optimization_barrier((*first, in_stays))
    for chunk, came in zip("RDL", first):
        came, last = lax.optimization_barrier((came, last))
        last = add(chunk, came)
    mixed, input_grad = call(
        finish_rows,
        [arr((rows, width)), arr((rows, width), F32)],
        small,
        (tokens, branch, ffn_stays, ffn_came, d_hidden, in_stays, in_came),
        after=(last,),
        parts={1: (lambda s, ref: ref.at[pl.ds(0, rows), :], (rows, width))},
        near=(2, 3, 6),
        window=7,
        name="finish_rows",
    )
    last = mixed
    arrived, full = {}, {}
    done = dict(D=1, L=1, R=1, X=0, Y=0)
    for chunk in WAITS:
        first = done[chunk]
        done[chunk] += 1
        for phase in range(first, bits if first == 3 else first + 1):
            came = over(held_parts[chunk][1], orders[chunk][phase])
            came, last = lax.optimization_barrier((came, last))
            if phase == bits - 1:
                arrived[chunk] = last = came
                if chunk in "DLR":
                    last = full[chunk] = held_parts[chunk][0].astype(F32) + came.astype(F32)
            else:
                last = add(chunk, came)
    slab = width // n_wide
    stays = [held_parts[c][0] for c in "XY"]
    came = [arrived[c] for c in "XY"]
    joint = call(
        join_columns,
        [arr((slab, width), F32)] * 5,
        small,
        (*stays, *map(other, stays), *came, *map(other, came)),
        inside=range(8),
        name="join_columns",
    )
    grad_left, grad_right, grad_down = full["L"], full["R"], full["D"].T
    return (mixed, input_grad, *joint, grad_left, grad_right, grad_down)


def solution(mesh):
    placed = (
        P(("wide", "narrow"), None),
        P("wide", None),
        P(),
        P(),
        P(),
        P(),
        P(),
        P(),
        P(None, "narrow"),
        P(None, "narrow"),
        P("narrow", None),
        P(("wide", "narrow"), None),
    )
    return jax.shard_map(
        on_device,
        mesh=mesh,
        in_specs=placed,
        out_specs=(
            P(("wide", "narrow"), None),
            P(("wide", "narrow"), None),
            P("wide", None),
            P("wide", None),
            P("wide", None),
            P("wide", None),
            P("wide", None),
            P("wide", "narrow"),
            P("wide", "narrow"),
            P("narrow", "wide"),
        ),
        check_vma=False,
    )
```

```python
import functools
import math

import jax
import jax.numpy as jnp
from jax import lax
from jax.experimental import pallas as pl
from jax.experimental.pallas import tpu as pltpu
from jax.sharding import PartitionSpec as P

BLOCK = 256
EPSILON = 1e-06
F32 = jnp.float32
BF16 = jnp.bfloat16


def plain(a, b):
    return jnp.dot(a, b, preferred_element_type=F32)


def against(a, b):
    return lax.dot_general(a, b, (((1,), (1,)), ((), ())), preferred_element_type=F32)


def outer(a, b):
    return lax.dot_general(a, b, (((0,), (0,)), ((), ())), preferred_element_type=F32)


def row_mean(v):
    return jnp.mean(v, axis=-1, keepdims=True)


def valid_rows(scalars, half, rows):
    c, length = scalars[0], scalars[2]
    first = rows * (c if half == 0 else 1 - c)
    return (first + lax.broadcasted_iota(jnp.int32, (rows, 1), 0) < length).astype(F32)


def decays(rate, n):
    i = lax.broadcasted_iota(jnp.int32, (n, n), 0)
    j = lax.broadcasted_iota(jnp.int32, (n, n), 1)
    gap = (i - j).astype(F32)
    mask = jnp.where(gap >= 0, jnp.exp(-rate * jnp.maximum(gap, 0.0)), 0.0)
    step = lax.broadcasted_iota(jnp.int32, (n, 1), 0).astype(F32)
    return mask, jnp.exp(-rate * (step + 1.0)), jnp.exp(-rate * (n - 1.0 - step))


def silu_parts(pre):
    sig = jax.nn.sigmoid(pre)
    act = pre * sig
    return act, sig + act * (1.0 - sig)


class Loaded:
    def __init__(self, source, buffer, sem, queue):
        self.buffer, self.copy, self.ready = buffer, pltpu.make_async_copy(source, buffer, sem), False
        self.queue = queue
        queue.append(self)

    def __call__(self):
        if not self.ready:
            while self in self.queue:
                self.queue.pop(0).copy.start()
            self.copy.wait()
            self.ready = True
            if self.queue:
                self.queue.pop(0).copy.start()
        return self.buffer


class Stored:
    def __init__(self, target, buffer, sem):
        self.buffer, self.copy, self.sent = buffer, pltpu.make_async_copy(buffer, target, sem), False

    def send(self):
        if not self.sent:
            self.copy.start()
            self.sent = True

    def finish(self):
        self.send()
        self.copy.wait()


class Here:
    def __init__(self, buffer):
        self.buffer = buffer

    def __call__(self):
        return self.buffer

    def send(self):
        pass

    def finish(self):
        pass


ANY = pl.BlockSpec(memory_space=pl.ANY)
VMEM = pl.BlockSpec(memory_space=pltpu.VMEM)
SMEM = pl.BlockSpec(memory_space=pltpu.SMEM)


def arr(shape, dtype=BF16):
    return jax.ShapeDtypeStruct(shape, dtype)


class here:
    def __init__(self, shape, dtype=BF16):
        self.shape, self.dtype = shape, jnp.dtype(dtype)


def call(
    body, outs, small, args, after=(), parts=None, scratch=(), window=4, slack=8, near=(), inside=(),
    into=None, name=None,
):
    parts, into = parts or {}, into or {}
    args = [
        a if i in near else pltpu.with_memory_space_constraint(a, pltpu.VMEM if i in inside else pltpu.HBM)
        for i, a in enumerate(args)
    ]
    shapes = [parts[i][1] if i in parts else a.shape for i, a in enumerate(args)]
    n_small, n_in, n_out, n_after = len(small), len(args), len(outs), len(after)
    copied = [i for i in range(n_in) if i not in inside and i not in into]
    sent = [i for i in range(n_out) if not isinstance(outs[i], here)]

    def kernel(*refs):
        scalars = refs[:n_small]
        at = n_small
        sources = refs[at : at + n_in]
        at += n_in + n_after
        targets = refs[at : at + n_out]
        at += n_out
        in_bufs = dict(zip(copied, refs[at:]))
        at += len(copied)
        out_bufs = dict(zip(sent, refs[at:]))
        at += len(sent)
        in_sem, out_sem = refs[at : at + 2]
        queue = []
        loaded = []
        for i, source in enumerate(sources):
            if i in inside:
                loaded.append(Here(source))
                continue
            source = parts[i][0](scalars[0], source) if i in parts else source
            buffer = targets[into[i]] if i in into else in_bufs[i]
            loaded.append(Loaded(source, buffer, in_sem.at[i], queue))
        for _ in range(min(window, len(queue))):
            queue.pop(0).copy.start()
        stored = [
            Stored(t, out_bufs[i], out_sem.at[i]) if i in out_bufs else Here(t)
            for i, t in enumerate(targets)
        ]
        results = [one for i, one in enumerate(stored) if i not in into.values()]
        body(*scalars, *loaded, *results, *refs[at + 2 :])
        for one in loaded:
            one()
        for one in stored:
            one.send()
        for one in stored:
            one.finish()

    buffers = [pltpu.VMEM(shapes[i], args[i].dtype) for i in copied]
    buffers += [pltpu.VMEM(outs[i].shape, outs[i].dtype) for i in sent]
    held = sum(b.dtype.itemsize * math.prod(b.shape) for b in [*buffers, *scratch])
    return pl.pallas_call(
        kernel,
        in_specs=[SMEM] * n_small
        + [VMEM if i in inside else ANY for i in range(n_in)]
        + [ANY] * n_after,
        out_specs=[ANY if i in sent else VMEM for i in range(n_out)],
        out_shape=[
            (pltpu.HBM if i in sent else pltpu.VMEM)(o.shape, o.dtype) for i, o in enumerate(outs)
        ],
        scratch_shapes=buffers
        + [pltpu.SemaphoreType.DMA((max(n_in, 1),)), pltpu.SemaphoreType.DMA((max(n_out, 1),))]
        + list(scratch),
        name=name,
        compiler_params=pltpu.CompilerParams(vmem_limit_bytes=held + (slack << 20)),
    )(*small, *args, *after)


def normed_rows(x):
    return x * lax.rsqrt(row_mean(x * x) + EPSILON)


def activations(i, pre, ok, part, q, k, v, dq, dk, gu, dg, gate):
    if i == 2:
        v[part, :] = (pre * ok).astype(BF16)
        return
    act, slope = silu_parts(pre)
    if i == 0:
        q[part, :] = act.astype(BF16)
        dq[part, :] = slope.astype(BF16)
    elif i == 1:
        k[part, :] = (act * ok).astype(BF16)
        dk[part, :] = (slope * ok).astype(BF16)
    else:
        gate[part, :] = act
        gu[part, :] = act.astype(BF16)
        dg[part, :] = slope.astype(BF16)


def project_own(scalars, tok, w_query, w_key, w_value, w_gate, nin, *outs):
    nin.buffer[...] = normed_rows(tok()[...].astype(F32)).astype(BF16)
    rows = nin.buffer.shape[0]
    ok = valid_rows(scalars, 0, rows)
    outs = [out.buffer for out in outs]
    for i, w in enumerate((w_query, w_key, w_value, w_gate)):
        activations(i, plain(nin.buffer[...], w()[...]), ok, slice(0, rows), *outs)


def attention_forward(
    scalars, rates, nin_own, *refs
):
    own, (tok_other, w_query, w_key, w_value, w_gate, w_down, w_out, w_left) = refs[:8], refs[8:16]
    (u, nin, q, k, v, dq, dk, gu, dg, att_out, prior_out), (gate_buf,) = refs[16:27], refs[27:]
    rows, cols = BLOCK, q.buffer.shape[1]
    c = scalars[0]
    nin.buffer[:rows, :] = nin_own()[...]
    nin.buffer[rows:, :] = normed_rows(tok_other()[...].astype(F32)).astype(BF16)
    nin.send()
    kept = [*(one.buffer for one in (q, k, v, dq, dk, gu, dg)), gate_buf]
    for mine, whole in zip(own, kept):
        whole[:rows, :] = mine()[...]
    ok = valid_rows(scalars, 1, rows)
    for i, w in enumerate((w_query, w_key, w_value, w_gate)):
        activations(i, plain(nin.buffer[rows:, :], w()[...]), ok, slice(rows, 2 * rows), *kept)
    for one in (q, dq, k, dk, v, gu, dg):
        one.send()
    heads, size = prior_out.buffer.shape[:2]
    carried = (scalars[2] > rows).astype(F32)
    first = pl.ds(pl.multiple_of(c * rows, rows), rows)
    second = pl.ds(pl.multiple_of((1 - c) * rows, rows), rows)
    squares = [jnp.zeros((rows, 1), F32), jnp.zeros((rows, 1), F32)]
    for h in range(heads):
        at = slice(h * size, (h + 1) * size)
        mask, query_decay, key_decay = decays(rates[c * heads + h], rows)
        wide = (k.buffer[first, at].astype(F32) * key_decay).astype(BF16)
        prior = (outer(wide, v.buffer[first, at]) * carried).astype(BF16)
        prior_out.buffer[h] = prior
        for b, part in enumerate((first, second)):
            queries = q.buffer[part, at]
            weighted = (against(queries, k.buffer[part, at]) * mask).astype(BF16)
            att = plain(weighted, v.buffer[part, at])
            if b == 1:
                att = att + plain(queries, prior) * query_decay
            att_out.buffer[part, at] = att.astype(BF16)
            u.buffer[part, at] = (att * gate_buf[part, at]).astype(BF16)
            squares[b] = squares[b] + jnp.sum(att * att, axis=-1, keepdims=True)
    lane = lax.broadcasted_iota(jnp.int32, (rows, 128), 1)
    for b, part in enumerate((first, second)):
        high = squares[b].astype(BF16).astype(F32)
        low = squares[b] - high
        u.buffer[part, cols:] = jnp.where(lane < 64, high, low).astype(BF16)


def block_at(wide, dims, pos):
    mask = 0
    for i, d in enumerate(dims):
        if pos >> (len(dims) - 1 - i) & 1:
            mask |= 1 << d
    return wide ^ mask


def transposed(source, flat):
    for at in range(0, flat.shape[0], 128):
        flat[at : at + 128, :] = source[:, at : at + 128].T


def place(scalars, flat, placed, dims, half=None):
    n = 1 << len(dims)
    rows = flat.shape[0] // n
    first, count = (0, n) if half is None else (half * n // 2, n // 2)
    for pos in range(count):
        block = block_at(scalars[1], dims, first + pos)
        placed[pos * rows : (pos + 1) * rows, :] = flat[
            pl.ds(pl.multiple_of(block * rows, rows), rows), :
        ]


def product(placed, right, at, *outs):
    step = 256
    rows = placed.shape[0] // len(outs)
    for i, out in reversed(list(enumerate(outs))):
        for row in range(0, rows, step):
            first = i * rows + row
            out.buffer[row : row + step, :] = plain(
                placed[first : first + step, :], right[:, at]
            ).astype(BF16)
        out.send()


def early_products(order, scalars, cot_own, cot_other, w_down, w_right, d_joined, placed, d_ffn, flat):
    rows = BLOCK
    for half in (0, 1):
        part = slice(half * rows, (half + 1) * rows)
        cot = (cot_own, cot_other)[half]()[...].astype(F32)
        d_ffn[part, :] = (cot * valid_rows(scalars, half, rows)).astype(BF16)
    transposed(d_ffn, flat)
    place(scalars, flat, placed.buffer, order)
    w_down = w_down()
    for half in (0, 1):
        part = slice(half * rows, (half + 1) * rows)
        d_joined.buffer[part, :] = against(d_ffn[part, :], w_down[...])


def feed_forward(
    orders, scalars, u_own, u_other, w_out, tok_own, tok_other, w_left, w_right, d_joined, placed_d,
    joined, d_left, d_right, branch_out, scale_out, flat, down_goes, left_goes, right_goes,
    nm, placed_l, placed_r,
):
    rows = BLOCK
    c = scalars[0]
    u_own, u_other, w_out = u_own(), u_other(), w_out()
    cols = u_own.shape[1] - 128
    width = 2 * cols
    own = pl.ds(pl.multiple_of(c * cols, cols), cols)
    other = pl.ds(pl.multiple_of((1 - c) * cols, cols), cols)
    for half in (0, 1):
        part = slice(half * rows, (half + 1) * rows)
        swap = slice((1 - half) * rows, (2 - half) * rows)
        total = jnp.zeros((rows, 1), F32)
        for lane in (0, 64):
            total = total + u_own[part, cols + lane : cols + lane + 1].astype(F32)
            total = total + u_other[swap, cols + lane : cols + lane + 1].astype(F32)
        scale = lax.rsqrt(total / width + EPSILON)
        scale_out.buffer[part, :] = jnp.broadcast_to(scale, (rows, 128))
        branch = scale * (
            plain(u_own[part, :cols], w_out[own, :]) + plain(u_other[swap, :cols], w_out[other, :])
        )
        branch_out.buffer[part, :] = branch.astype(BF16)
        ok = valid_rows(scalars, half, rows)
        hidden = (tok_own, tok_other)[half]()[...].astype(F32) + ok * branch
        nm[part, :] = normed_rows(hidden).astype(BF16)
    branch_out.send()
    scale_out.send()
    w_left, w_right, d_joined = w_left(), w_right(), d_joined()
    units = w_left.shape[1]
    for first in range(0, units, 768):
        at = slice(first, min(first + 768, units))
        for half in (0, 1):
            part = slice(half * rows, (half + 1) * rows)
            left = plain(nm[part, :], w_left[:, at])
            right = plain(nm[part, :], w_right[:, at])
            joined.buffer[part, at] = (left * right).astype(BF16)
            d_left.buffer[part, at] = (d_joined[part, at] * right).astype(BF16)
            d_right.buffer[part, at] = (d_joined[part, at] * left).astype(BF16)
    for one in (joined, d_left, d_right):
        one.send()
    transposed(nm, flat.buffer)
    place(scalars, flat.buffer, placed_l, orders[1], 1)
    place(scalars, flat.buffer, placed_r, orders[2], 1)
    every = slice(0, units)
    half = width // 2
    product(placed_d().at[half:, :], joined.buffer, every, down_goes)
    product(placed_l, d_left.buffer, every, left_goes)
    product(placed_r, d_right.buffer, every, right_goes)


def staying_products(
    orders, scalars, placed_d, flat, joined, d_left, d_right, down_stays, left_stays, right_stays,
    placed_l, placed_r,
):
    every = slice(0, joined.buffer.shape[1])
    place(scalars, flat(), placed_l, orders[1], 0)
    place(scalars, flat(), placed_r, orders[2], 0)
    half = flat().shape[0] // 2
    product(placed_d().at[:half, :], joined(), every, down_stays)
    product(placed_l, d_left(), every, left_stays)
    product(placed_r, d_right(), every, right_stays)


def mid_gradient(d_left, w_left, d_right, w_right, out, total):
    rows = BLOCK
    d_left, w_left = d_left(), w_left()
    step = w_left.shape[0] // 2
    places = [(half * rows, first) for half in (0, 1) for first in (0, step)]
    for row, first in places:
        total[row : row + rows, first : first + step] = against(
            d_left[row : row + rows, :], w_left[first : first + step, :]
        )
    d_right, w_right = d_right(), w_right()
    for row, first in places:
        at = (slice(row, row + rows), slice(first, first + step))
        out.buffer[at] = (
            total[at] + against(d_right[row : row + rows, :], w_right[first : first + step, :])
        ).astype(BF16)


def down_projection(joined, w_down, stays, goes):
    rows = BLOCK
    joined, w_down = joined(), w_down()
    goes.buffer[...] = plain(joined[rows:, :], w_down[...]).astype(BF16)
    goes.send()
    stays.buffer[...] = plain(joined[:rows, :], w_down[...])


def attention_backward(
    orders, scalars, rates, mid_own, mid_other, tok_own, tok_other, cot_own, cot_other, branch, w_out, scale_ref,
    gu, dg, att, u_own, u_other, q, k, v, prior, dq, dk, nin,
    dpre, x_goes, x_stays, y_goes, y_stays, hidden_out,
    d_att, d_branch, gated, flat, flat_gated, *placed,
):
    rows = BLOCK
    cols = dpre.buffer.shape[1] // 4
    c = scalars[0]
    own = pl.ds(pl.multiple_of(c * cols, cols), cols)
    other = pl.ds(pl.multiple_of((1 - c) * cols, cols), cols)
    for half in (0, 1):
        part = slice(half * rows, (half + 1) * rows)
        swap = slice((1 - half) * rows, (2 - half) * rows)
        ok = valid_rows(scalars, half, rows)
        d_mid = mid_own()[part, :].astype(F32) + mid_other()[swap, :].astype(F32)
        x = (tok_own, tok_other)[half]()[...].astype(F32)
        cot = (cot_own, cot_other)[half]()[...].astype(F32)
        lined = branch()[part, :].astype(F32)
        hidden = x + ok * lined
        mid_scale = lax.rsqrt(row_mean(hidden * hidden) + EPSILON)
        normed = hidden * mid_scale
        d_hidden = cot + mid_scale * (d_mid - normed * row_mean(d_mid * normed))
        if half == 0:
            hidden_out.buffer[...] = d_hidden
        d_out = (ok * d_hidden).astype(BF16)
        d_branch[part, :] = d_out
        inner = row_mean(d_out.astype(F32) * lined)
        d_gated = against(d_out, w_out()[...])
        scale = scale_ref()[part, :1]
        normed = att()[part, :].astype(F32) * scale
        dpre.buffer[part, 3 * cols :] = (d_gated * normed * dg()[part, :].astype(F32)).astype(BF16)
        d_att[part, :] = (scale * (d_gated * gu()[part, :].astype(F32) - normed * inner)).astype(BF16)
        gated[part, own] = (u_own()[part, :cols].astype(F32) * scale).astype(BF16)
        gated[part, other] = (u_other()[swap, :cols].astype(F32) * scale).astype(BF16)
    hidden_out.send()
    q, k, v, dq, dk, prior = q(), k(), v(), dq(), dk(), prior()
    heads, size = prior.shape[:2]
    carried = (scalars[2] > rows).astype(F32)
    first = pl.ds(pl.multiple_of(c * rows, rows), rows)
    second = pl.ds(pl.multiple_of((1 - c) * rows, rows), rows)
    row = lax.broadcasted_iota(jnp.int32, (rows, 1), 0)
    for h in range(heads):
        lanes = [slice(i * cols + h * size, i * cols + (h + 1) * size) for i in range(3)]
        at = lanes[0]
        mask, query_decay, key_decay = decays(rates[c * heads + h], rows)
        wide = (q[second, at].astype(F32) * query_decay).astype(BF16)
        state = (outer(wide, d_att[second, at]) * carried).astype(BF16)
        for b, part in enumerate((first, second)):
            q_b, k_b, v_b, d_o = q[part, at], k[part, at], v[part, at], d_att[part, at]
            weighted = (against(q_b, k_b) * mask).astype(BF16)
            d_scores = (against(d_o, v_b) * mask).astype(BF16)
            d_q = plain(d_scores, k_b)
            d_k = outer(d_scores, q_b)
            d_v = outer(weighted, d_o)
            if b == 1:
                d_q = d_q + against(d_o, prior[h]) * query_decay
            else:
                d_k = d_k + against(v_b, state) * key_decay
                d_v = d_v + plain(k_b, state) * key_decay
            ok = jnp.where(b * rows + row < scalars[2], 1.0, 0.0)
            dpre.buffer[part, lanes[0]] = (d_q * dq[part, at].astype(F32)).astype(BF16)
            dpre.buffer[part, lanes[1]] = (d_k * dk[part, at].astype(F32)).astype(BF16)
            dpre.buffer[part, lanes[2]] = (d_v * ok).astype(BF16)
    dpre.send()
    transposed(nin(), flat)
    transposed(gated, flat_gated)
    place(scalars, flat, placed[0], orders[0])
    lanes = x_stays.buffer.shape[1]
    product(placed[0], dpre.buffer, slice(0, lanes), x_stays, x_goes)
    place(scalars, flat, placed[1], orders[1])
    place(scalars, flat_gated, placed[2], orders[1])
    between = dpre.buffer.shape[1] - lanes
    half = flat.shape[0] // 2
    for out, first in ((y_goes, half), (y_stays, 0)):
        for row in range(0, half, 256):
            at = slice(first + row, first + row + 256)
            to = slice(row, row + 256)
            out.buffer[to, :between] = plain(placed[1][at, :], dpre.buffer[:, lanes:]).astype(BF16)
            out.buffer[to, between:] = plain(placed[2][at, :], d_branch[:, own]).astype(BF16)
        out.send()


def input_gradient(scalars, dpre, w_query, w_key, w_value, w_gate, stays, goes, total):
    rows = stays.buffer.shape[0]
    cols = w_query.buffer.shape[1]
    dpre = dpre()
    for i, w in enumerate((w_query, w_key, w_value, w_gate)):
        w = w()
        for half in (0, 1):
            part = slice(half * rows, (half + 1) * rows)
            term = against(dpre[part, i * cols : (i + 1) * cols], w[...])
            if i == 0:
                total[part, :] = term
            elif i < 3:
                total[part, :] += term
            elif half == 0:
                stays.buffer[...] = total[part, :] + term
            else:
                goes.buffer[...] = (total[part, :] + term).astype(BF16)


def finish_rows(
    scalars, tok, branch, ffn_stays, ffn_came, d_hidden, in_stays, in_came, mixed, input_grad
):
    x = tok()[...].astype(F32)
    ffn = ffn_stays()[...] + ffn_came()[...].astype(F32)
    ok = valid_rows(scalars, 0, x.shape[0])
    mixed.buffer[...] = (x + ok * (branch()[...].astype(F32) + ffn)).astype(BF16)
    mixed.send()
    scale = lax.rsqrt(row_mean(x * x) + EPSILON)
    normed = x * scale
    d_in = in_stays()[...] + in_came()[...].astype(F32)
    input_grad.buffer[...] = d_hidden()[...] + scale * (d_in - normed * row_mean(d_in * normed))


def join_columns(scalars, *refs):
    ins, outs = refs[:8], refs[8:]
    cols = outs[0].buffer.shape[1] // 2
    own = pl.multiple_of(scalars[0] * cols, cols)
    other = pl.multiple_of((1 - scalars[0]) * cols, cols)
    step = 128
    for first, side in ((own, 0), (other, 2)):
        place_at = 0
        for i in range(2):
            total = ins[side + i]()[...].astype(F32) + ins[4 + side + i]()[...].astype(F32)
            for at in range(0, total.shape[1], step):
                lanes = pl.ds(pl.multiple_of(first + place_at % cols, step), step)
                outs[place_at // cols].buffer[:, lanes] = total[:, at : at + step]
                place_at += step


ORDERS = {"D": "yxab", "L": "xbya", "R": "axyb", "X": "axyb", "Y": "yxab"}
WAITS = "RYDRXYLRDXYLDXLYX"


def on_device(
    tokens,
    seq_lens,
    decay_rate,
    w_query,
    w_key,
    w_value,
    w_gate_u,
    w_out,
    w_left,
    w_right,
    w_down,
    cotangent,
):
    n_wide = lax.axis_size("wide")
    bits = n_wide.bit_length() - 1
    tail = list(range(4, bits))
    orders = {c: ["xyab".index(d) for d in dims] + tail for c, dims in ORDERS.items()}
    ffn_orders = [orders[c] for c in "DLR"]
    attn_orders = [orders[c] for c in "XY"]
    rows, width = tokens.shape
    units = w_left.shape[1]
    heads = decay_rate.shape[0] // 2
    size = width // decay_rate.shape[0]
    cols = width // 2
    group = 2 * rows
    c = lax.axis_index("narrow")
    scalars = jnp.stack([c, lax.axis_index("wide"), seq_lens[0, 0]]).astype(jnp.int32)

    def other(v):
        return lax.ppermute(v, "narrow", [(0, 1), (1, 0)])

    def over(v, bit):
        return lax.ppermute(v, "wide", [(i, i ^ (1 << bit)) for i in range(n_wide)])

    def half_cols(s, ref):
        return ref.at[:, pl.ds(pl.multiple_of(s[0] * cols, cols), cols)]

    def half_rows(s, ref):
        return ref.at[pl.ds(pl.multiple_of(s[0] * cols, cols), cols), :]

    halves = (half_cols, (width, cols))
    small = (scalars,)
    tok_other, cot_other = other(tokens), other(cotangent)
    weights = (w_query, w_key, w_value, w_gate_u)
    *held, nin_own, q, k, v, dq, dk, gu, dg, gate = call(
        project_own,
        [here((width, cols))] * 4
        + [here((rows, width))]
        + [here((rows, cols))] * 7
        + [here((rows, cols), F32)],
        small,
        (tokens, *weights),
        parts={i: halves for i in (1, 2, 3, 4)},
        into={1: 0, 2: 1, 3: 2, 4: 3},
        window=3,
        name="project_own",
    )
    u, nin, q, k, v, dq, dk, gu, dg, att, prior, down_held, out_held, left_held = call(
        attention_forward,
        [here((group, cols + 128)), arr((group, width))]
        + [arr((group, cols))] * 8
        + [arr((heads, size, size)), here((units, width))]
        + [here((width, width)), here((width, units))],
        (scalars, decay_rate),
        (nin_own, q, k, v, dq, dk, gu, dg, gate, tok_other, *held, w_down, w_out, w_left),
        into={14: 11, 15: 12, 16: 13},
        inside=(0, 1, 2, 3, 4, 5, 6, 7, 8, 10, 11, 12, 13),
        after=(cot_other,),
        near=(9,),
        scratch=[pltpu.VMEM((group, cols), F32)],
        name="attention_forward",
    )
    u_other = other(u)
    right_held, d_joined, placed_d = call(
        functools.partial(early_products, orders["D"]),
        [here((width, units)), here((group, units), F32), here((width, group))],
        small,
        (cotangent, cot_other, down_held, w_right),
        after=(u,),
        near=(1,),
        inside=(2,),
        into={3: 0},
        scratch=[pltpu.VMEM((group, width), BF16), pltpu.VMEM((width, group), BF16)],
        window=3,
        name="early_products",
    )
    part = here((width // 2, units))
    joined, d_left, d_right, branch, scale, flat, *goes = call(
        functools.partial(feed_forward, ffn_orders),
        [here((group, units))] * 3
        + [arr((group, width)), arr((group, 128), F32), here((width, group))]
        + [part] * 3,
        small,
        (u, u_other, out_held, tokens, tok_other, left_held, right_held, d_joined, placed_d),
        inside=(0, 2, 5, 6, 7, 8),
        near=(1, 4),
        scratch=[pltpu.VMEM((group, width), BF16)] + [pltpu.VMEM((width // 2, group), BF16)] * 2,
        name="feed_forward",
    )
    (mid,) = call(
        mid_gradient,
        [here((group, width))],
        (),
        (d_left, left_held, d_right, right_held),
        inside=(0, 1, 2, 3),
        scratch=[pltpu.VMEM((group, width), F32)],
        name="mid_gradient",
    )
    mid_other = other(mid)
    attn_part = (width // 2, 5 * cols // 2)
    dpre, x_goes, x_stays, y_goes, y_stays, d_hidden = call(
        functools.partial(attention_backward, attn_orders),
        [here((group, 4 * cols))]
        + [here(attn_part)] * 4
        + [arr((rows, width), F32)],
        (scalars, decay_rate),
        (mid, mid_other, tokens, tok_other, cotangent, cot_other, branch, w_out, scale)
        + (gu, dg, att, u, u_other, q, k, v, prior, dq, dk, nin),
        parts={7: (half_rows, (cols, width))},
        inside=(0,),
        near=(1, 3, 5, 12, 13),
        window=8,
        scratch=[pltpu.VMEM((group, cols), BF16)]
        + [pltpu.VMEM((group, width), BF16)] * 2
        + [pltpu.VMEM((width, group), BF16)] * 5,
        slack=4,
        name="attention_backward",
    )
    ffn_stays, ffn_goes = call(
        down_projection,
        [here((rows, width), F32), here((rows, width))],
        (),
        (joined, down_held),
        inside=(0, 1),
        after=(dpre,),
        name="down_projection",
    )
    ffn_came = other(ffn_goes)
    stays = call(
        functools.partial(staying_products, ffn_orders),
        [part] * 3,
        small,
        (placed_d, flat, joined, d_left, d_right),
        inside=range(5),
        after=(ffn_goes,),
        scratch=[pltpu.VMEM((width // 2, group), BF16)] * 2,
        name="staying_products",
    )
    in_stays, in_goes = call(
        input_gradient,
        [arr((rows, width), F32), here((rows, width))],
        small,
        (dpre, w_query, w_key, w_value, w_gate_u),
        inside=(0,),
        after=(stays[0],),
        parts={i: halves for i in (1, 2, 3, 4)},
        scratch=[pltpu.VMEM((group, width), F32)],
        name="input_gradient",
    )
    in_came = other(in_goes)

    held_parts = dict(zip("DLR", zip(stays, goes)))
    held_parts.update(X=(x_stays, x_goes), Y=(y_stays, y_goes))

    def add(chunk, came):
        stays = held_parts[chunk][0]
        total = stays.astype(F32) + came.astype(F32)
        half = total.shape[0] // 2
        held_parts[chunk] = total[:half].astype(BF16), total[half:].astype(BF16)
        return held_parts[chunk][1]

    first = [over(held_parts[c][1], orders[c][0]) for c in "RDL"]
    *first, last = lax.optimization_barrier((*first, in_stays))
    for chunk, came in zip("RDL", first):
        came, last = lax.optimization_barrier((came, last))
        last = add(chunk, came)
    mixed, input_grad = call(
        finish_rows,
        [arr((rows, width)), arr((rows, width), F32)],
        small,
        (tokens, branch, ffn_stays, ffn_came, d_hidden, in_stays, in_came),
        after=(last,),
        parts={1: (lambda s, ref: ref.at[pl.ds(0, rows), :], (rows, width))},
        near=(2, 3, 6),
        window=7,
        name="finish_rows",
    )
    last = mixed
    arrived, full = {}, {}
    done = dict(D=1, L=1, R=1, X=0, Y=0)
    for chunk in WAITS:
        first = done[chunk]
        done[chunk] += 1
        for phase in range(first, bits if first == 3 else first + 1):
            came = over(held_parts[chunk][1], orders[chunk][phase])
            came, last = lax.optimization_barrier((came, last))
            if phase == bits - 1:
                arrived[chunk] = last = came
                if chunk in "DLR":
                    last = full[chunk] = held_parts[chunk][0].astype(F32) + came.astype(F32)
            else:
                last = add(chunk, came)
    slab = width // n_wide
    stays = [held_parts[c][0] for c in "XY"]
    came = [arrived[c] for c in "XY"]
    joint = call(
        join_columns,
        [arr((slab, width), F32)] * 5,
        small,
        (*stays, *map(other, stays), *came, *map(other, came)),
        inside=range(8),
        name="join_columns",
    )
    grad_left, grad_right, grad_down = full["L"], full["R"], full["D"].T
    return (mixed, input_grad, *joint, grad_left, grad_right, grad_down)


def solution(mesh):
    placed = (
        P(("wide", "narrow"), None),
        P("wide", None),
        P(),
        P(),
        P(),
        P(),
        P(),
        P(),
        P(None, "narrow"),
        P(None, "narrow"),
        P("narrow", None),
        P(("wide", "narrow"), None),
    )
    return jax.shard_map(
        on_device,
        mesh=mesh,
        in_specs=placed,
        out_specs=(
            P(("wide", "narrow"), None),
            P(("wide", "narrow"), None),
            P("wide", None),
            P("wide", None),
            P("wide", None),
            P("wide", None),
            P("wide", None),
            P("wide", "narrow"),
            P("wide", "narrow"),
            P("narrow", "wide"),
        ),
        check_vma=False,
    )
```

```python
import functools
import math

import jax
import jax.numpy as jnp
from jax import lax
from jax.experimental import pallas as pl
from jax.experimental.pallas import tpu as pltpu
from jax.sharding import PartitionSpec as P

BLOCK = 256
EPSILON = 1e-06
F32 = jnp.float32
BF16 = jnp.bfloat16


def plain(a, b):
    return jnp.dot(a, b, preferred_element_type=F32)


def against(a, b):
    return lax.dot_general(a, b, (((1,), (1,)), ((), ())), preferred_element_type=F32)


def outer(a, b):
    return lax.dot_general(a, b, (((0,), (0,)), ((), ())), preferred_element_type=F32)


def row_mean(v):
    return jnp.mean(v, axis=-1, keepdims=True)


def valid_rows(scalars, half, rows):
    c, length = scalars[0], scalars[2]
    first = rows * (c if half == 0 else 1 - c)
    return (first + lax.broadcasted_iota(jnp.int32, (rows, 1), 0) < length).astype(F32)


def decays(rate, n):
    i = lax.broadcasted_iota(jnp.int32, (n, n), 0)
    j = lax.broadcasted_iota(jnp.int32, (n, n), 1)
    gap = (i - j).astype(F32)
    mask = jnp.where(gap >= 0, jnp.exp(-rate * jnp.maximum(gap, 0.0)), 0.0)
    step = lax.broadcasted_iota(jnp.int32, (n, 1), 0).astype(F32)
    return mask, jnp.exp(-rate * (step + 1.0)), jnp.exp(-rate * (n - 1.0 - step))


def silu_parts(pre):
    sig = jax.nn.sigmoid(pre)
    act = pre * sig
    return act, sig + act * (1.0 - sig)


class Loaded:
    def __init__(self, source, buffer, sem, queue):
        self.buffer, self.copy, self.ready = buffer, pltpu.make_async_copy(source, buffer, sem), False
        self.queue = queue
        queue.append(self)

    def __call__(self):
        if not self.ready:
            while self in self.queue:
                self.queue.pop(0).copy.start()
            self.copy.wait()
            self.ready = True
            if self.queue:
                self.queue.pop(0).copy.start()
        return self.buffer


class Stored:
    def __init__(self, target, buffer, sem):
        self.buffer, self.copy, self.sent = buffer, pltpu.make_async_copy(buffer, target, sem), False

    def send(self):
        if not self.sent:
            self.copy.start()
            self.sent = True

    def finish(self):
        self.send()
        self.copy.wait()


class Here:
    def __init__(self, buffer):
        self.buffer = buffer

    def __call__(self):
        return self.buffer

    def send(self):
        pass

    def finish(self):
        pass


ANY = pl.BlockSpec(memory_space=pl.ANY)
VMEM = pl.BlockSpec(memory_space=pltpu.VMEM)
SMEM = pl.BlockSpec(memory_space=pltpu.SMEM)


def arr(shape, dtype=BF16):
    return jax.ShapeDtypeStruct(shape, dtype)


class here:
    def __init__(self, shape, dtype=BF16):
        self.shape, self.dtype = shape, jnp.dtype(dtype)


def call(
    body, outs, small, args, after=(), parts=None, scratch=(), window=4, slack=8, near=(), inside=(),
    into=None, name=None,
):
    parts, into = parts or {}, into or {}
    args = [
        a if i in near else pltpu.with_memory_space_constraint(a, pltpu.VMEM if i in inside else pltpu.HBM)
        for i, a in enumerate(args)
    ]
    shapes = [parts[i][1] if i in parts else a.shape for i, a in enumerate(args)]
    n_small, n_in, n_out, n_after = len(small), len(args), len(outs), len(after)
    copied = [i for i in range(n_in) if i not in inside and i not in into]
    sent = [i for i in range(n_out) if not isinstance(outs[i], here)]

    def kernel(*refs):
        scalars = refs[:n_small]
        at = n_small
        sources = refs[at : at + n_in]
        at += n_in + n_after
        targets = refs[at : at + n_out]
        at += n_out
        in_bufs = dict(zip(copied, refs[at:]))
        at += len(copied)
        out_bufs = dict(zip(sent, refs[at:]))
        at += len(sent)
        in_sem, out_sem = refs[at : at + 2]
        queue = []
        loaded = []
        for i, source in enumerate(sources):
            if i in inside:
                loaded.append(Here(source))
                continue
            source = parts[i][0](scalars[0], source) if i in parts else source
            buffer = targets[into[i]] if i in into else in_bufs[i]
            loaded.append(Loaded(source, buffer, in_sem.at[i], queue))
        for _ in range(min(window, len(queue))):
            queue.pop(0).copy.start()
        stored = [
            Stored(t, out_bufs[i], out_sem.at[i]) if i in out_bufs else Here(t)
            for i, t in enumerate(targets)
        ]
        results = [one for i, one in enumerate(stored) if i not in into.values()]
        body(*scalars, *loaded, *results, *refs[at + 2 :])
        for one in loaded:
            one()
        for one in stored:
            one.send()
        for one in stored:
            one.finish()

    buffers = [pltpu.VMEM(shapes[i], args[i].dtype) for i in copied]
    buffers += [pltpu.VMEM(outs[i].shape, outs[i].dtype) for i in sent]
    held = sum(b.dtype.itemsize * math.prod(b.shape) for b in [*buffers, *scratch])
    return pl.pallas_call(
        kernel,
        in_specs=[SMEM] * n_small
        + [VMEM if i in inside else ANY for i in range(n_in)]
        + [ANY] * n_after,
        out_specs=[ANY if i in sent else VMEM for i in range(n_out)],
        out_shape=[
            (pltpu.HBM if i in sent else pltpu.VMEM)(o.shape, o.dtype) for i, o in enumerate(outs)
        ],
        scratch_shapes=buffers
        + [pltpu.SemaphoreType.DMA((max(n_in, 1),)), pltpu.SemaphoreType.DMA((max(n_out, 1),))]
        + list(scratch),
        name=name,
        compiler_params=pltpu.CompilerParams(vmem_limit_bytes=held + (slack << 20)),
    )(*small, *args, *after)


def normed_rows(x):
    return x * lax.rsqrt(row_mean(x * x) + EPSILON)


def activations(i, pre, ok, part, q, k, v, dq, dk, gu, dg, gate):
    if i == 2:
        v[part, :] = (pre * ok).astype(BF16)
        return
    act, slope = silu_parts(pre)
    if i == 0:
        q[part, :] = act.astype(BF16)
        dq[part, :] = slope.astype(BF16)
    elif i == 1:
        k[part, :] = (act * ok).astype(BF16)
        dk[part, :] = (slope * ok).astype(BF16)
    else:
        gate[part, :] = act
        gu[part, :] = act.astype(BF16)
        dg[part, :] = slope.astype(BF16)


def project_own(scalars, tok, w_query, w_key, w_value, w_gate, nin, *outs):
    nin.buffer[...] = normed_rows(tok()[...].astype(F32)).astype(BF16)
    rows = nin.buffer.shape[0]
    ok = valid_rows(scalars, 0, rows)
    outs = [out.buffer for out in outs]
    for i, w in enumerate((w_query, w_key, w_value, w_gate)):
        activations(i, plain(nin.buffer[...], w()[...]), ok, slice(0, rows), *outs)


def attention_forward(
    scalars, rates, nin_own, *refs
):
    own, (tok_other, w_query, w_key, w_value, w_gate, w_down, w_out, w_left) = refs[:8], refs[8:16]
    (u, nin, q, k, v, dq, dk, gu, dg, att_out, prior_out), (gate_buf,) = refs[16:27], refs[27:]
    rows, cols = BLOCK, q.buffer.shape[1]
    c = scalars[0]
    nin.buffer[:rows, :] = nin_own()[...]
    nin.buffer[rows:, :] = normed_rows(tok_other()[...].astype(F32)).astype(BF16)
    nin.send()
    kept = [*(one.buffer for one in (q, k, v, dq, dk, gu, dg)), gate_buf]
    for mine, whole in zip(own, kept):
        whole[:rows, :] = mine()[...]
    ok = valid_rows(scalars, 1, rows)
    for i, w in enumerate((w_query, w_key, w_value, w_gate)):
        activations(i, plain(nin.buffer[rows:, :], w()[...]), ok, slice(rows, 2 * rows), *kept)
    for one in (q, dq, k, dk, v, gu, dg):
        one.send()
    heads, size = prior_out.buffer.shape[:2]
    carried = (scalars[2] > rows).astype(F32)
    first = pl.ds(pl.multiple_of(c * rows, rows), rows)
    second = pl.ds(pl.multiple_of((1 - c) * rows, rows), rows)
    squares = [jnp.zeros((rows, 1), F32), jnp.zeros((rows, 1), F32)]
    for h in range(heads):
        at = slice(h * size, (h + 1) * size)
        mask, query_decay, key_decay = decays(rates[c * heads + h], rows)
        wide = (k.buffer[first, at].astype(F32) * key_decay).astype(BF16)
        prior = (outer(wide, v.buffer[first, at]) * carried).astype(BF16)
        prior_out.buffer[h] = prior
        for b, part in enumerate((first, second)):
            queries = q.buffer[part, at]
            weighted = (against(queries, k.buffer[part, at]) * mask).astype(BF16)
            att = plain(weighted, v.buffer[part, at])
            if b == 1:
                att = att + plain(queries, prior) * query_decay
            att_out.buffer[part, at] = att.astype(BF16)
            u.buffer[part, at] = (att * gate_buf[part, at]).astype(BF16)
            squares[b] = squares[b] + jnp.sum(att * att, axis=-1, keepdims=True)
    lane = lax.broadcasted_iota(jnp.int32, (rows, 128), 1)
    for b, part in enumerate((first, second)):
        high = squares[b].astype(BF16).astype(F32)
        low = squares[b] - high
        u.buffer[part, cols:] = jnp.where(lane < 64, high, low).astype(BF16)


def block_at(wide, dims, pos):
    mask = 0
    for i, d in enumerate(dims):
        if pos >> (len(dims) - 1 - i) & 1:
            mask |= 1 << d
    return wide ^ mask


def transposed(source, flat):
    for at in range(0, flat.shape[0], 128):
        flat[at : at + 128, :] = source[:, at : at + 128].T


def place(scalars, flat, placed, dims, half=None):
    n = 1 << len(dims)
    rows = flat.shape[0] // n
    first, count = (0, n) if half is None else (half * n // 2, n // 2)
    for pos in range(count):
        block = block_at(scalars[1], dims, first + pos)
        placed[pos * rows : (pos + 1) * rows, :] = flat[
            pl.ds(pl.multiple_of(block * rows, rows), rows), :
        ]


def product(placed, right, at, *outs):
    step = 256
    rows = placed.shape[0] // len(outs)
    for i, out in reversed(list(enumerate(outs))):
        for row in range(0, rows, step):
            first = i * rows + row
            out.buffer[row : row + step, :] = plain(
                placed[first : first + step, :], right[:, at]
            ).astype(BF16)
        out.send()


def early_products(order, scalars, cot_own, cot_other, w_down, w_right, d_joined, placed, d_ffn, flat):
    rows = BLOCK
    for half in (0, 1):
        part = slice(half * rows, (half + 1) * rows)
        cot = (cot_own, cot_other)[half]()[...].astype(F32)
        d_ffn[part, :] = (cot * valid_rows(scalars, half, rows)).astype(BF16)
    transposed(d_ffn, flat)
    place(scalars, flat, placed.buffer, order)
    w_down = w_down()
    for half in (0, 1):
        part = slice(half * rows, (half + 1) * rows)
        d_joined.buffer[part, :] = against(d_ffn[part, :], w_down[...])


def feed_forward(
    orders, scalars, u_own, u_other, w_out, tok_own, tok_other, w_left, w_right, d_joined, placed_d,
    joined, d_left, d_right, branch_out, scale_out, flat, down_goes, left_goes, right_goes,
    nm, placed_l, placed_r,
):
    rows = BLOCK
    c = scalars[0]
    u_own, u_other, w_out = u_own(), u_other(), w_out()
    cols = u_own.shape[1] - 128
    width = 2 * cols
    own = pl.ds(pl.multiple_of(c * cols, cols), cols)
    other = pl.ds(pl.multiple_of((1 - c) * cols, cols), cols)
    for half in (0, 1):
        part = slice(half * rows, (half + 1) * rows)
        swap = slice((1 - half) * rows, (2 - half) * rows)
        total = jnp.zeros((rows, 1), F32)
        for lane in (0, 64):
            total = total + u_own[part, cols + lane : cols + lane + 1].astype(F32)
            total = total + u_other[swap, cols + lane : cols + lane + 1].astype(F32)
        scale = lax.rsqrt(total / width + EPSILON)
        scale_out.buffer[part, :] = jnp.broadcast_to(scale, (rows, 128))
        branch = scale * (
            plain(u_own[part, :cols], w_out[own, :]) + plain(u_other[swap, :cols], w_out[other, :])
        )
        branch_out.buffer[part, :] = branch.astype(BF16)
        ok = valid_rows(scalars, half, rows)
        hidden = (tok_own, tok_other)[half]()[...].astype(F32) + ok * branch
        nm[part, :] = normed_rows(hidden).astype(BF16)
    branch_out.send()
    scale_out.send()
    w_left, w_right, d_joined = w_left(), w_right(), d_joined()
    units = w_left.shape[1]
    for first in range(0, units, 768):
        at = slice(first, min(first + 768, units))
        for half in (0, 1):
            part = slice(half * rows, (half + 1) * rows)
            left = plain(nm[part, :], w_left[:, at])
            right = plain(nm[part, :], w_right[:, at])
            joined.buffer[part, at] = (left * right).astype(BF16)
            d_left.buffer[part, at] = (d_joined[part, at] * right).astype(BF16)
            d_right.buffer[part, at] = (d_joined[part, at] * left).astype(BF16)
    for one in (joined, d_left, d_right):
        one.send()
    transposed(nm, flat.buffer)
    place(scalars, flat.buffer, placed_l, orders[1], 1)
    place(scalars, flat.buffer, placed_r, orders[2], 1)
    every = slice(0, units)
    half = width // 2
    product(placed_d().at[half:, :], joined.buffer, every, down_goes)
    product(placed_l, d_left.buffer, every, left_goes)
    product(placed_r, d_right.buffer, every, right_goes)


def staying_products(
    orders, scalars, placed_d, flat, joined, d_left, d_right, down_stays, left_stays, right_stays,
    placed_l, placed_r,
):
    every = slice(0, joined.buffer.shape[1])
    place(scalars, flat(), placed_l, orders[1], 0)
    place(scalars, flat(), placed_r, orders[2], 0)
    half = flat().shape[0] // 2
    product(placed_d().at[:half, :], joined(), every, down_stays)
    product(placed_l, d_left(), every, left_stays)
    product(placed_r, d_right(), every, right_stays)


def mid_gradient(d_left, w_left, d_right, w_right, out, total):
    rows = BLOCK
    d_left, w_left = d_left(), w_left()
    step = w_left.shape[0] // 2
    places = [(half * rows, first) for half in (0, 1) for first in (0, step)]
    for row, first in places:
        total[row : row + rows, first : first + step] = against(
            d_left[row : row + rows, :], w_left[first : first + step, :]
        )
    d_right, w_right = d_right(), w_right()
    for row, first in places:
        at = (slice(row, row + rows), slice(first, first + step))
        out.buffer[at] = (
            total[at] + against(d_right[row : row + rows, :], w_right[first : first + step, :])
        ).astype(BF16)


def down_projection(joined, w_down, stays, goes):
    rows = BLOCK
    joined, w_down = joined(), w_down()
    goes.buffer[...] = plain(joined[rows:, :], w_down[...]).astype(BF16)
    goes.send()
    stays.buffer[...] = plain(joined[:rows, :], w_down[...])


def attention_backward(
    orders, scalars, rates, mid_own, mid_other, tok_own, tok_other, cot_own, cot_other, branch, w_out, scale_ref,
    gu, dg, att, u_own, u_other, q, k, v, prior, dq, dk, nin,
    dpre, x_goes, x_stays, y_goes, y_stays, hidden_out,
    d_att, d_branch, gated, flat, flat_gated, *placed,
):
    rows = BLOCK
    cols = dpre.buffer.shape[1] // 4
    c = scalars[0]
    own = pl.ds(pl.multiple_of(c * cols, cols), cols)
    other = pl.ds(pl.multiple_of((1 - c) * cols, cols), cols)
    for half in (0, 1):
        part = slice(half * rows, (half + 1) * rows)
        swap = slice((1 - half) * rows, (2 - half) * rows)
        ok = valid_rows(scalars, half, rows)
        d_mid = mid_own()[part, :].astype(F32) + mid_other()[swap, :].astype(F32)
        x = (tok_own, tok_other)[half]()[...].astype(F32)
        cot = (cot_own, cot_other)[half]()[...].astype(F32)
        lined = branch()[part, :].astype(F32)
        hidden = x + ok * lined
        mid_scale = lax.rsqrt(row_mean(hidden * hidden) + EPSILON)
        normed = hidden * mid_scale
        d_hidden = cot + mid_scale * (d_mid - normed * row_mean(d_mid * normed))
        if half == 0:
            hidden_out.buffer[...] = d_hidden
        d_out = (ok * d_hidden).astype(BF16)
        d_branch[part, :] = d_out
        inner = row_mean(d_out.astype(F32) * lined)
        d_gated = against(d_out, w_out()[...])
        scale = scale_ref()[part, :1]
        normed = att()[part, :].astype(F32) * scale
        dpre.buffer[part, 3 * cols :] = (d_gated * normed * dg()[part, :].astype(F32)).astype(BF16)
        d_att[part, :] = (scale * (d_gated * gu()[part, :].astype(F32) - normed * inner)).astype(BF16)
        gated[part, own] = (u_own()[part, :cols].astype(F32) * scale).astype(BF16)
        gated[part, other] = (u_other()[swap, :cols].astype(F32) * scale).astype(BF16)
    hidden_out.send()
    q, k, v, dq, dk, prior = q(), k(), v(), dq(), dk(), prior()
    heads, size = prior.shape[:2]
    carried = (scalars[2] > rows).astype(F32)
    first = pl.ds(pl.multiple_of(c * rows, rows), rows)
    second = pl.ds(pl.multiple_of((1 - c) * rows, rows), rows)
    row = lax.broadcasted_iota(jnp.int32, (rows, 1), 0)
    for h in range(heads):
        lanes = [slice(i * cols + h * size, i * cols + (h + 1) * size) for i in range(3)]
        at = lanes[0]
        mask, query_decay, key_decay = decays(rates[c * heads + h], rows)
        wide = (q[second, at].astype(F32) * query_decay).astype(BF16)
        state = (outer(wide, d_att[second, at]) * carried).astype(BF16)
        for b, part in enumerate((first, second)):
            q_b, k_b, v_b, d_o = q[part, at], k[part, at], v[part, at], d_att[part, at]
            weighted = (against(q_b, k_b) * mask).astype(BF16)
            d_scores = (against(d_o, v_b) * mask).astype(BF16)
            d_q = plain(d_scores, k_b)
            d_k = outer(d_scores, q_b)
            d_v = outer(weighted, d_o)
            if b == 1:
                d_q = d_q + against(d_o, prior[h]) * query_decay
            else:
                d_k = d_k + against(v_b, state) * key_decay
                d_v = d_v + plain(k_b, state) * key_decay
            ok = jnp.where(b * rows + row < scalars[2], 1.0, 0.0)
            dpre.buffer[part, lanes[0]] = (d_q * dq[part, at].astype(F32)).astype(BF16)
            dpre.buffer[part, lanes[1]] = (d_k * dk[part, at].astype(F32)).astype(BF16)
            dpre.buffer[part, lanes[2]] = (d_v * ok).astype(BF16)
    dpre.send()
    transposed(nin(), flat)
    transposed(gated, flat_gated)
    place(scalars, flat, placed[0], orders[0])
    lanes = x_stays.buffer.shape[1]
    product(placed[0], dpre.buffer, slice(0, lanes), x_stays, x_goes)
    place(scalars, flat, placed[1], orders[1])
    place(scalars, flat_gated, placed[2], orders[1])
    between = dpre.buffer.shape[1] - lanes
    half = flat.shape[0] // 2
    for out, first in ((y_goes, half), (y_stays, 0)):
        for row in range(0, half, 256):
            at = slice(first + row, first + row + 256)
            to = slice(row, row + 256)
            out.buffer[to, :between] = plain(placed[1][at, :], dpre.buffer[:, lanes:]).astype(BF16)
            out.buffer[to, between:] = plain(placed[2][at, :], d_branch[:, own]).astype(BF16)
        out.send()


def input_gradient(scalars, dpre, w_query, w_key, w_value, w_gate, stays, goes, total):
    rows = stays.buffer.shape[0]
    cols = w_query.buffer.shape[1]
    dpre = dpre()
    for i, w in enumerate((w_query, w_key, w_value, w_gate)):
        w = w()
        for half in (0, 1):
            part = slice(half * rows, (half + 1) * rows)
            term = against(dpre[part, i * cols : (i + 1) * cols], w[...])
            if i == 0:
                total[part, :] = term
            elif i < 3:
                total[part, :] += term
            elif half == 0:
                stays.buffer[...] = total[part, :] + term
            else:
                goes.buffer[...] = (total[part, :] + term).astype(BF16)


def finish_rows(
    scalars, tok, branch, ffn_stays, ffn_came, d_hidden, in_stays, in_came, mixed, input_grad
):
    x = tok()[...].astype(F32)
    ffn = ffn_stays()[...] + ffn_came()[...].astype(F32)
    ok = valid_rows(scalars, 0, x.shape[0])
    mixed.buffer[...] = (x + ok * (branch()[...].astype(F32) + ffn)).astype(BF16)
    mixed.send()
    scale = lax.rsqrt(row_mean(x * x) + EPSILON)
    normed = x * scale
    d_in = in_stays()[...] + in_came()[...].astype(F32)
    input_grad.buffer[...] = d_hidden()[...] + scale * (d_in - normed * row_mean(d_in * normed))


def join_columns(scalars, *refs):
    ins, outs = refs[:8], refs[8:]
    cols = outs[0].buffer.shape[1] // 2
    own = pl.multiple_of(scalars[0] * cols, cols)
    other = pl.multiple_of((1 - scalars[0]) * cols, cols)
    step = 128
    for first, side in ((own, 0), (other, 2)):
        place_at = 0
        for i in range(2):
            total = ins[side + i]()[...].astype(F32) + ins[4 + side + i]()[...].astype(F32)
            for at in range(0, total.shape[1], step):
                lanes = pl.ds(pl.multiple_of(first + place_at % cols, step), step)
                outs[place_at // cols].buffer[:, lanes] = total[:, at : at + step]
                place_at += step


ORDERS = {"D": "yxab", "L": "xbya", "R": "axyb", "X": "axyb", "Y": "yxab"}
WAITS = "RYDRXYLRDXYLDXLYX"


def on_device(
    tokens,
    seq_lens,
    decay_rate,
    w_query,
    w_key,
    w_value,
    w_gate_u,
    w_out,
    w_left,
    w_right,
    w_down,
    cotangent,
):
    n_wide = lax.axis_size("wide")
    bits = n_wide.bit_length() - 1
    tail = list(range(4, bits))
    orders = {c: ["xyab".index(d) for d in dims] + tail for c, dims in ORDERS.items()}
    ffn_orders = [orders[c] for c in "DLR"]
    attn_orders = [orders[c] for c in "XY"]
    rows, width = tokens.shape
    units = w_left.shape[1]
    heads = decay_rate.shape[0] // 2
    size = width // decay_rate.shape[0]
    cols = width // 2
    group = 2 * rows
    c = lax.axis_index("narrow")
    scalars = jnp.stack([c, lax.axis_index("wide"), seq_lens[0, 0]]).astype(jnp.int32)

    def other(v):
        return lax.ppermute(v, "narrow", [(0, 1), (1, 0)])

    def over(v, bit):
        return lax.ppermute(v, "wide", [(i, i ^ (1 << bit)) for i in range(n_wide)])

    def half_cols(s, ref):
        return ref.at[:, pl.ds(pl.multiple_of(s[0] * cols, cols), cols)]

    def half_rows(s, ref):
        return ref.at[pl.ds(pl.multiple_of(s[0] * cols, cols), cols), :]

    halves = (half_cols, (width, cols))
    small = (scalars,)
    tok_other, cot_other = other(tokens), other(cotangent)
    weights = (w_query, w_key, w_value, w_gate_u)
    *held, nin_own, q, k, v, dq, dk, gu, dg, gate = call(
        project_own,
        [here((width, cols))] * 4
        + [here((rows, width))]
        + [here((rows, cols))] * 7
        + [here((rows, cols), F32)],
        small,
        (tokens, *weights),
        parts={i: halves for i in (1, 2, 3, 4)},
        into={1: 0, 2: 1, 3: 2, 4: 3},
        window=3,
        name="project_own",
    )
    u, nin, q, k, v, dq, dk, gu, dg, att, prior, down_held, out_held, left_held = call(
        attention_forward,
        [here((group, cols + 128)), arr((group, width))]
        + [arr((group, cols))] * 8
        + [arr((heads, size, size)), here((units, width))]
        + [here((width, width)), here((width, units))],
        (scalars, decay_rate),
        (nin_own, q, k, v, dq, dk, gu, dg, gate, tok_other, *held, w_down, w_out, w_left),
        into={14: 11, 15: 12, 16: 13},
        inside=(0, 1, 2, 3, 4, 5, 6, 7, 8, 10, 11, 12, 13),
        after=(cot_other,),
        near=(9,),
        scratch=[pltpu.VMEM((group, cols), F32)],
        name="attention_forward",
    )
    u_other = other(u)
    right_held, d_joined, placed_d = call(
        functools.partial(early_products, orders["D"]),
        [here((width, units)), here((group, units), F32), here((width, group))],
        small,
        (cotangent, cot_other, down_held, w_right),
        after=(u,),
        near=(1,),
        inside=(2,),
        into={3: 0},
        scratch=[pltpu.VMEM((group, width), BF16), pltpu.VMEM((width, group), BF16)],
        window=3,
        name="early_products",
    )
    part = here((width // 2, units))
    joined, d_left, d_right, branch, scale, flat, *goes = call(
        functools.partial(feed_forward, ffn_orders),
        [here((group, units))] * 3
        + [arr((group, width)), arr((group, 128), F32), here((width, group))]
        + [part] * 3,
        small,
        (u, u_other, out_held, tokens, tok_other, left_held, right_held, d_joined, placed_d),
        inside=(0, 2, 5, 6, 7, 8),
        near=(1, 4),
        scratch=[pltpu.VMEM((group, width), BF16)] + [pltpu.VMEM((width // 2, group), BF16)] * 2,
        name="feed_forward",
    )
    (mid,) = call(
        mid_gradient,
        [here((group, width))],
        (),
        (d_left, left_held, d_right, right_held),
        inside=(0, 1, 2, 3),
        scratch=[pltpu.VMEM((group, width), F32)],
        name="mid_gradient",
    )
    mid_other = other(mid)
    attn_part = (width // 2, 5 * cols // 2)
    dpre, x_goes, x_stays, y_goes, y_stays, d_hidden = call(
        functools.partial(attention_backward, attn_orders),
        [here((group, 4 * cols))]
        + [here(attn_part)] * 4
        + [arr((rows, width), F32)],
        (scalars, decay_rate),
        (mid, mid_other, tokens, tok_other, cotangent, cot_other, branch, w_out, scale)
        + (gu, dg, att, u, u_other, q, k, v, prior, dq, dk, nin),
        parts={7: (half_rows, (cols, width))},
        inside=(0,),
        near=(1, 3, 5, 12, 13),
        window=8,
        scratch=[pltpu.VMEM((group, cols), BF16)]
        + [pltpu.VMEM((group, width), BF16)] * 2
        + [pltpu.VMEM((width, group), BF16)] * 5,
        slack=4,
        name="attention_backward",
    )
    ffn_stays, ffn_goes = call(
        down_projection,
        [here((rows, width), F32), here((rows, width))],
        (),
        (joined, down_held),
        inside=(0, 1),
        after=(dpre,),
        name="down_projection",
    )
    ffn_came = other(ffn_goes)
    stays = call(
        functools.partial(staying_products, ffn_orders),
        [part] * 3,
        small,
        (placed_d, flat, joined, d_left, d_right),
        inside=range(5),
        after=(ffn_goes,),
        scratch=[pltpu.VMEM((width // 2, group), BF16)] * 2,
        name="staying_products",
    )
    in_stays, in_goes = call(
        input_gradient,
        [arr((rows, width), F32), here((rows, width))],
        small,
        (dpre, w_query, w_key, w_value, w_gate_u),
        inside=(0,),
        after=(stays[0],),
        parts={i: halves for i in (1, 2, 3, 4)},
        scratch=[pltpu.VMEM((group, width), F32)],
        name="input_gradient",
    )
    in_came = other(in_goes)

    held_parts = dict(zip("DLR", zip(stays, goes)))
    held_parts.update(X=(x_stays, x_goes), Y=(y_stays, y_goes))

    def add(chunk, came):
        stays = held_parts[chunk][0]
        total = stays.astype(F32) + came.astype(F32)
        half = total.shape[0] // 2
        held_parts[chunk] = total[:half].astype(BF16), total[half:].astype(BF16)
        return held_parts[chunk][1]

    first = [over(held_parts[c][1], orders[c][0]) for c in "RDL"]
    *first, last = lax.optimization_barrier((*first, in_stays))
    for chunk, came in zip("RDL", first):
        came, last = lax.optimization_barrier((came, last))
        last = add(chunk, came)
    mixed, input_grad = call(
        finish_rows,
        [arr((rows, width)), arr((rows, width), F32)],
        small,
        (tokens, branch, ffn_stays, ffn_came, d_hidden, in_stays, in_came),
        after=(last,),
        parts={1: (lambda s, ref: ref.at[pl.ds(0, rows), :], (rows, width))},
        near=(2, 3, 6),
        window=7,
        name="finish_rows",
    )
    last = mixed
    arrived, full = {}, {}
    done = dict(D=1, L=1, R=1, X=0, Y=0)
    for chunk in WAITS:
        first = done[chunk]
        done[chunk] += 1
        for phase in range(first, bits if first == 3 else first + 1):
            came = over(held_parts[chunk][1], orders[chunk][phase])
            came, last = lax.optimization_barrier((came, last))
            if phase == bits - 1:
                arrived[chunk] = last = came
                if chunk in "DLR":
                    last = full[chunk] = held_parts[chunk][0].astype(F32) + came.astype(F32)
            else:
                last = add(chunk, came)
    slab = width // n_wide
    stays = [held_parts[c][0] for c in "XY"]
    came = [arrived[c] for c in "XY"]
    joint = call(
        join_columns,
        [arr((slab, width), F32)] * 5,
        small,
        (*stays, *map(other, stays), *came, *map(other, came)),
        inside=range(8),
        name="join_columns",
    )
    came, *joint = lax.optimization_barrier((arrived["L"], *joint))
    full["L"] = held_parts["L"][0].astype(F32) + came.astype(F32)
    grad_left, grad_right, grad_down = full["L"], full["R"], full["D"].T
    return (mixed, input_grad, *joint, grad_left, grad_right, grad_down)


def solution(mesh):
    placed = (
        P(("wide", "narrow"), None),
        P("wide", None),
        P(),
        P(),
        P(),
        P(),
        P(),
        P(),
        P(None, "narrow"),
        P(None, "narrow"),
        P("narrow", None),
        P(("wide", "narrow"), None),
    )
    return jax.shard_map(
        on_device,
        mesh=mesh,
        in_specs=placed,
        out_specs=(
            P(("wide", "narrow"), None),
            P(("wide", "narrow"), None),
            P("wide", None),
            P("wide", None),
            P("wide", None),
            P("wide", None),
            P("wide", None),
            P("wide", "narrow"),
            P("wide", "narrow"),
            P("narrow", "wide"),
        ),
        check_vma=False,
    )
```

```python
import functools
import math

import jax
import jax.numpy as jnp
from jax import lax
from jax.experimental import pallas as pl
from jax.experimental.pallas import tpu as pltpu
from jax.sharding import PartitionSpec as P

BLOCK = 256
EPSILON = 1e-06
F32 = jnp.float32
BF16 = jnp.bfloat16


def plain(a, b):
    return jnp.dot(a, b, preferred_element_type=F32)


def against(a, b):
    return lax.dot_general(a, b, (((1,), (1,)), ((), ())), preferred_element_type=F32)


def outer(a, b):
    return lax.dot_general(a, b, (((0,), (0,)), ((), ())), preferred_element_type=F32)


def row_mean(v):
    return jnp.mean(v, axis=-1, keepdims=True)


def valid_rows(scalars, half, rows):
    c, length = scalars[0], scalars[2]
    first = rows * (c if half == 0 else 1 - c)
    return (first + lax.broadcasted_iota(jnp.int32, (rows, 1), 0) < length).astype(F32)


def decays(rate, n):
    i = lax.broadcasted_iota(jnp.int32, (n, n), 0)
    j = lax.broadcasted_iota(jnp.int32, (n, n), 1)
    gap = (i - j).astype(F32)
    mask = jnp.where(gap >= 0, jnp.exp(-rate * jnp.maximum(gap, 0.0)), 0.0)
    step = lax.broadcasted_iota(jnp.int32, (n, 1), 0).astype(F32)
    return mask, jnp.exp(-rate * (step + 1.0)), jnp.exp(-rate * (n - 1.0 - step))


def silu_parts(pre):
    sig = jax.nn.sigmoid(pre)
    act = pre * sig
    return act, sig + act * (1.0 - sig)


class Loaded:
    def __init__(self, source, buffer, sem, queue):
        self.buffer, self.copy, self.ready = buffer, pltpu.make_async_copy(source, buffer, sem), False
        self.queue = queue
        queue.append(self)

    def __call__(self):
        if not self.ready:
            while self in self.queue:
                self.queue.pop(0).copy.start()
            self.copy.wait()
            self.ready = True
            if self.queue:
                self.queue.pop(0).copy.start()
        return self.buffer


class Stored:
    def __init__(self, target, buffer, sem):
        self.buffer, self.copy, self.sent = buffer, pltpu.make_async_copy(buffer, target, sem), False

    def send(self):
        if not self.sent:
            self.copy.start()
            self.sent = True

    def finish(self):
        self.send()
        self.copy.wait()


class Here:
    def __init__(self, buffer):
        self.buffer = buffer

    def __call__(self):
        return self.buffer

    def send(self):
        pass

    def finish(self):
        pass


ANY = pl.BlockSpec(memory_space=pl.ANY)
VMEM = pl.BlockSpec(memory_space=pltpu.VMEM)
SMEM = pl.BlockSpec(memory_space=pltpu.SMEM)


def arr(shape, dtype=BF16):
    return jax.ShapeDtypeStruct(shape, dtype)


class here:
    def __init__(self, shape, dtype=BF16):
        self.shape, self.dtype = shape, jnp.dtype(dtype)


def call(
    body, outs, small, args, after=(), parts=None, scratch=(), window=4, slack=8, near=(), inside=(),
    into=None, name=None,
):
    parts, into = parts or {}, into or {}
    args = [
        a if i in near else pltpu.with_memory_space_constraint(a, pltpu.VMEM if i in inside else pltpu.HBM)
        for i, a in enumerate(args)
    ]
    shapes = [parts[i][1] if i in parts else a.shape for i, a in enumerate(args)]
    n_small, n_in, n_out, n_after = len(small), len(args), len(outs), len(after)
    copied = [i for i in range(n_in) if i not in inside and i not in into]
    sent = [i for i in range(n_out) if not isinstance(outs[i], here)]

    def kernel(*refs):
        scalars = refs[:n_small]
        at = n_small
        sources = refs[at : at + n_in]
        at += n_in + n_after
        targets = refs[at : at + n_out]
        at += n_out
        in_bufs = dict(zip(copied, refs[at:]))
        at += len(copied)
        out_bufs = dict(zip(sent, refs[at:]))
        at += len(sent)
        in_sem, out_sem = refs[at : at + 2]
        queue = []
        loaded = []
        for i, source in enumerate(sources):
            if i in inside:
                loaded.append(Here(source))
                continue
            source = parts[i][0](scalars[0], source) if i in parts else source
            buffer = targets[into[i]] if i in into else in_bufs[i]
            loaded.append(Loaded(source, buffer, in_sem.at[i], queue))
        for _ in range(min(window, len(queue))):
            queue.pop(0).copy.start()
        stored = [
            Stored(t, out_bufs[i], out_sem.at[i]) if i in out_bufs else Here(t)
            for i, t in enumerate(targets)
        ]
        results = [one for i, one in enumerate(stored) if i not in into.values()]
        body(*scalars, *loaded, *results, *refs[at + 2 :])
        for one in loaded:
            one()
        for one in stored:
            one.send()
        for one in stored:
            one.finish()

    buffers = [pltpu.VMEM(shapes[i], args[i].dtype) for i in copied]
    buffers += [pltpu.VMEM(outs[i].shape, outs[i].dtype) for i in sent]
    held = sum(b.dtype.itemsize * math.prod(b.shape) for b in [*buffers, *scratch])
    return pl.pallas_call(
        kernel,
        in_specs=[SMEM] * n_small
        + [VMEM if i in inside else ANY for i in range(n_in)]
        + [ANY] * n_after,
        out_specs=[ANY if i in sent else VMEM for i in range(n_out)],
        out_shape=[
            (pltpu.HBM if i in sent else pltpu.VMEM)(o.shape, o.dtype) for i, o in enumerate(outs)
        ],
        scratch_shapes=buffers
        + [pltpu.SemaphoreType.DMA((max(n_in, 1),)), pltpu.SemaphoreType.DMA((max(n_out, 1),))]
        + list(scratch),
        name=name,
        compiler_params=pltpu.CompilerParams(vmem_limit_bytes=held + (slack << 20)),
    )(*small, *args, *after)


def normed_rows(x):
    return x * lax.rsqrt(row_mean(x * x) + EPSILON)


def activations(i, pre, ok, part, q, k, v, dq, dk, gu, dg, gate):
    if i == 2:
        v[part, :] = (pre * ok).astype(BF16)
        return
    act, slope = silu_parts(pre)
    if i == 0:
        q[part, :] = act.astype(BF16)
        dq[part, :] = slope.astype(BF16)
    elif i == 1:
        k[part, :] = (act * ok).astype(BF16)
        dk[part, :] = (slope * ok).astype(BF16)
    else:
        gate[part, :] = act
        gu[part, :] = act.astype(BF16)
        dg[part, :] = slope.astype(BF16)


def project_own(scalars, tok, w_query, w_key, w_value, w_gate, nin, *outs):
    nin.buffer[...] = normed_rows(tok()[...].astype(F32)).astype(BF16)
    rows = nin.buffer.shape[0]
    ok = valid_rows(scalars, 0, rows)
    outs = [out.buffer for out in outs]
    for i, w in enumerate((w_query, w_key, w_value, w_gate)):
        activations(i, plain(nin.buffer[...], w()[...]), ok, slice(0, rows), *outs)


def attention_forward(
    scalars, rates, nin_own, *refs
):
    own, (tok_other, w_query, w_key, w_value, w_gate, w_down, w_out, w_left) = refs[:8], refs[8:16]
    (u, nin, q, k, v, dq, dk, gu, dg, att_out, prior_out), (gate_buf,) = refs[16:27], refs[27:]
    rows, cols = BLOCK, q.buffer.shape[1]
    c = scalars[0]
    nin.buffer[:rows, :] = nin_own()[...]
    nin.buffer[rows:, :] = normed_rows(tok_other()[...].astype(F32)).astype(BF16)
    nin.send()
    kept = [*(one.buffer for one in (q, k, v, dq, dk, gu, dg)), gate_buf]
    for mine, whole in zip(own, kept):
        whole[:rows, :] = mine()[...]
    ok = valid_rows(scalars, 1, rows)
    for i, w in enumerate((w_query, w_key, w_value, w_gate)):
        activations(i, plain(nin.buffer[rows:, :], w()[...]), ok, slice(rows, 2 * rows), *kept)
    for one in (q, dq, k, dk, v, gu, dg):
        one.send()
    heads, size = prior_out.buffer.shape[:2]
    carried = (scalars[2] > rows).astype(F32)
    first = pl.ds(pl.multiple_of(c * rows, rows), rows)
    second = pl.ds(pl.multiple_of((1 - c) * rows, rows), rows)
    squares = [jnp.zeros((rows, 1), F32), jnp.zeros((rows, 1), F32)]
    for h in range(heads):
        at = slice(h * size, (h + 1) * size)
        mask, query_decay, key_decay = decays(rates[c * heads + h], rows)
        wide = (k.buffer[first, at].astype(F32) * key_decay).astype(BF16)
        prior = (outer(wide, v.buffer[first, at]) * carried).astype(BF16)
        prior_out.buffer[h] = prior
        for b, part in enumerate((first, second)):
            queries = q.buffer[part, at]
            weighted = (against(queries, k.buffer[part, at]) * mask).astype(BF16)
            att = plain(weighted, v.buffer[part, at])
            if b == 1:
                att = att + plain(queries, prior) * query_decay
            att_out.buffer[part, at] = att.astype(BF16)
            u.buffer[part, at] = (att * gate_buf[part, at]).astype(BF16)
            squares[b] = squares[b] + jnp.sum(att * att, axis=-1, keepdims=True)
    lane = lax.broadcasted_iota(jnp.int32, (rows, 128), 1)
    for b, part in enumerate((first, second)):
        high = squares[b].astype(BF16).astype(F32)
        low = squares[b] - high
        u.buffer[part, cols:] = jnp.where(lane < 64, high, low).astype(BF16)


def block_at(wide, dims, pos):
    mask = 0
    for i, d in enumerate(dims):
        if pos >> (len(dims) - 1 - i) & 1:
            mask |= 1 << d
    return wide ^ mask


def transposed(source, flat):
    for at in range(0, flat.shape[0], 128):
        flat[at : at + 128, :] = source[:, at : at + 128].T


def place(scalars, flat, placed, dims, half=None):
    n = 1 << len(dims)
    rows = flat.shape[0] // n
    first, count = (0, n) if half is None else (half * n // 2, n // 2)
    for pos in range(count):
        block = block_at(scalars[1], dims, first + pos)
        placed[pos * rows : (pos + 1) * rows, :] = flat[
            pl.ds(pl.multiple_of(block * rows, rows), rows), :
        ]


def product(placed, right, at, *outs):
    step = 256
    rows = placed.shape[0] // len(outs)
    for i, out in reversed(list(enumerate(outs))):
        for row in range(0, rows, step):
            first = i * rows + row
            out.buffer[row : row + step, :] = plain(
                placed[first : first + step, :], right[:, at]
            ).astype(BF16)
        out.send()


def early_products(order, scalars, cot_own, cot_other, w_down, w_right, d_joined, placed, d_ffn, flat):
    rows = BLOCK
    for half in (0, 1):
        part = slice(half * rows, (half + 1) * rows)
        cot = (cot_own, cot_other)[half]()[...].astype(F32)
        d_ffn[part, :] = (cot * valid_rows(scalars, half, rows)).astype(BF16)
    transposed(d_ffn, flat)
    place(scalars, flat, placed.buffer, order)
    w_down = w_down()
    for half in (0, 1):
        part = slice(half * rows, (half + 1) * rows)
        d_joined.buffer[part, :] = against(d_ffn[part, :], w_down[...])


def feed_forward(
    orders, scalars, u_own, u_other, w_out, tok_own, tok_other, w_left, w_right, d_joined, placed_d,
    joined, d_left, d_right, branch_out, scale_out, flat, down_goes, left_goes, right_goes,
    nm, placed_l, placed_r,
):
    rows = BLOCK
    c = scalars[0]
    u_own, u_other, w_out = u_own(), u_other(), w_out()
    cols = u_own.shape[1] - 128
    width = 2 * cols
    own = pl.ds(pl.multiple_of(c * cols, cols), cols)
    other = pl.ds(pl.multiple_of((1 - c) * cols, cols), cols)
    for half in (0, 1):
        part = slice(half * rows, (half + 1) * rows)
        swap = slice((1 - half) * rows, (2 - half) * rows)
        total = jnp.zeros((rows, 1), F32)
        for lane in (0, 64):
            total = total + u_own[part, cols + lane : cols + lane + 1].astype(F32)
            total = total + u_other[swap, cols + lane : cols + lane + 1].astype(F32)
        scale = lax.rsqrt(total / width + EPSILON)
        scale_out.buffer[part, :] = jnp.broadcast_to(scale, (rows, 128))
        branch = scale * (
            plain(u_own[part, :cols], w_out[own, :]) + plain(u_other[swap, :cols], w_out[other, :])
        )
        branch_out.buffer[part, :] = branch.astype(BF16)
        ok = valid_rows(scalars, half, rows)
        hidden = (tok_own, tok_other)[half]()[...].astype(F32) + ok * branch
        nm[part, :] = normed_rows(hidden).astype(BF16)
    branch_out.send()
    scale_out.send()
    w_left, w_right, d_joined = w_left(), w_right(), d_joined()
    units = w_left.shape[1]
    for first in range(0, units, 768):
        at = slice(first, min(first + 768, units))
        for half in (0, 1):
            part = slice(half * rows, (half + 1) * rows)
            left = plain(nm[part, :], w_left[:, at])
            right = plain(nm[part, :], w_right[:, at])
            joined.buffer[part, at] = (left * right).astype(BF16)
            d_left.buffer[part, at] = (d_joined[part, at] * right).astype(BF16)
            d_right.buffer[part, at] = (d_joined[part, at] * left).astype(BF16)
    for one in (joined, d_left, d_right):
        one.send()
    transposed(nm, flat.buffer)
    place(scalars, flat.buffer, placed_l, orders[1], 1)
    place(scalars, flat.buffer, placed_r, orders[2], 1)
    every = slice(0, units)
    half = width // 2
    product(placed_d().at[half:, :], joined.buffer, every, down_goes)
    product(placed_l, d_left.buffer, every, left_goes)
    product(placed_r, d_right.buffer, every, right_goes)


def staying_products(
    orders, scalars, placed_d, flat, joined, d_left, d_right, down_stays, left_stays, right_stays,
    placed_l, placed_r,
):
    every = slice(0, joined.buffer.shape[1])
    place(scalars, flat(), placed_l, orders[1], 0)
    place(scalars, flat(), placed_r, orders[2], 0)
    half = flat().shape[0] // 2
    product(placed_d().at[:half, :], joined(), every, down_stays)
    product(placed_l, d_left(), every, left_stays)
    product(placed_r, d_right(), every, right_stays)


def down_and_staying(orders, scalars, w_down, placed_d, flat, joined, d_left, d_right, stays, goes, *rest):
    down_projection(joined, w_down, stays, goes)
    staying_products(orders, scalars, placed_d, flat, joined, d_left, d_right, *rest)


def mid_gradient(d_left, w_left, d_right, w_right, out, total):
    rows = BLOCK
    d_left, w_left = d_left(), w_left()
    step = w_left.shape[0] // 2
    places = [(half * rows, first) for half in (0, 1) for first in (0, step)]
    for row, first in places:
        total[row : row + rows, first : first + step] = against(
            d_left[row : row + rows, :], w_left[first : first + step, :]
        )
    d_right, w_right = d_right(), w_right()
    for row, first in places:
        at = (slice(row, row + rows), slice(first, first + step))
        out.buffer[at] = (
            total[at] + against(d_right[row : row + rows, :], w_right[first : first + step, :])
        ).astype(BF16)


def down_projection(joined, w_down, stays, goes):
    rows = BLOCK
    joined, w_down = joined(), w_down()
    goes.buffer[...] = plain(joined[rows:, :], w_down[...]).astype(BF16)
    goes.send()
    stays.buffer[...] = plain(joined[:rows, :], w_down[...])


def attention_backward(
    orders, scalars, rates, mid_own, mid_other, tok_own, tok_other, cot_own, cot_other, branch, w_out, scale_ref,
    gu, dg, att, u_own, u_other, q, k, v, prior, dq, dk, nin,
    dpre, x_goes, x_stays, y_goes, y_stays, hidden_out,
    d_att, d_branch, gated, flat, flat_gated, *placed,
):
    rows = BLOCK
    cols = dpre.buffer.shape[1] // 4
    c = scalars[0]
    own = pl.ds(pl.multiple_of(c * cols, cols), cols)
    other = pl.ds(pl.multiple_of((1 - c) * cols, cols), cols)
    for half in (0, 1):
        part = slice(half * rows, (half + 1) * rows)
        swap = slice((1 - half) * rows, (2 - half) * rows)
        ok = valid_rows(scalars, half, rows)
        d_mid = mid_own()[part, :].astype(F32) + mid_other()[swap, :].astype(F32)
        x = (tok_own, tok_other)[half]()[...].astype(F32)
        cot = (cot_own, cot_other)[half]()[...].astype(F32)
        lined = branch()[part, :].astype(F32)
        hidden = x + ok * lined
        mid_scale = lax.rsqrt(row_mean(hidden * hidden) + EPSILON)
        normed = hidden * mid_scale
        d_hidden = cot + mid_scale * (d_mid - normed * row_mean(d_mid * normed))
        if half == 0:
            hidden_out.buffer[...] = d_hidden
        d_out = (ok * d_hidden).astype(BF16)
        d_branch[part, :] = d_out
        inner = row_mean(d_out.astype(F32) * lined)
        d_gated = against(d_out, w_out()[...])
        scale = scale_ref()[part, :1]
        normed = att()[part, :].astype(F32) * scale
        dpre.buffer[part, 3 * cols :] = (d_gated * normed * dg()[part, :].astype(F32)).astype(BF16)
        d_att[part, :] = (scale * (d_gated * gu()[part, :].astype(F32) - normed * inner)).astype(BF16)
        gated[part, own] = (u_own()[part, :cols].astype(F32) * scale).astype(BF16)
        gated[part, other] = (u_other()[swap, :cols].astype(F32) * scale).astype(BF16)
    hidden_out.send()
    q, k, v, dq, dk, prior = q(), k(), v(), dq(), dk(), prior()
    heads, size = prior.shape[:2]
    carried = (scalars[2] > rows).astype(F32)
    first = pl.ds(pl.multiple_of(c * rows, rows), rows)
    second = pl.ds(pl.multiple_of((1 - c) * rows, rows), rows)
    row = lax.broadcasted_iota(jnp.int32, (rows, 1), 0)
    for h in range(heads):
        lanes = [slice(i * cols + h * size, i * cols + (h + 1) * size) for i in range(3)]
        at = lanes[0]
        mask, query_decay, key_decay = decays(rates[c * heads + h], rows)
        wide = (q[second, at].astype(F32) * query_decay).astype(BF16)
        state = (outer(wide, d_att[second, at]) * carried).astype(BF16)
        for b, part in enumerate((first, second)):
            q_b, k_b, v_b, d_o = q[part, at], k[part, at], v[part, at], d_att[part, at]
            weighted = (against(q_b, k_b) * mask).astype(BF16)
            d_scores = (against(d_o, v_b) * mask).astype(BF16)
            d_q = plain(d_scores, k_b)
            d_k = outer(d_scores, q_b)
            d_v = outer(weighted, d_o)
            if b == 1:
                d_q = d_q + against(d_o, prior[h]) * query_decay
            else:
                d_k = d_k + against(v_b, state) * key_decay
                d_v = d_v + plain(k_b, state) * key_decay
            ok = jnp.where(b * rows + row < scalars[2], 1.0, 0.0)
            dpre.buffer[part, lanes[0]] = (d_q * dq[part, at].astype(F32)).astype(BF16)
            dpre.buffer[part, lanes[1]] = (d_k * dk[part, at].astype(F32)).astype(BF16)
            dpre.buffer[part, lanes[2]] = (d_v * ok).astype(BF16)
    dpre.send()
    transposed(nin(), flat)
    transposed(gated, flat_gated)
    place(scalars, flat, placed[0], orders[0])
    lanes = x_stays.buffer.shape[1]
    product(placed[0], dpre.buffer, slice(0, lanes), x_stays, x_goes)
    place(scalars, flat, placed[1], orders[1])
    place(scalars, flat_gated, placed[2], orders[1])
    between = dpre.buffer.shape[1] - lanes
    half = flat.shape[0] // 2
    for out, first in ((y_goes, half), (y_stays, 0)):
        for row in range(0, half, 256):
            at = slice(first + row, first + row + 256)
            to = slice(row, row + 256)
            out.buffer[to, :between] = plain(placed[1][at, :], dpre.buffer[:, lanes:]).astype(BF16)
            out.buffer[to, between:] = plain(placed[2][at, :], d_branch[:, own]).astype(BF16)
        out.send()


def input_gradient(scalars, dpre, w_query, w_key, w_value, w_gate, stays, goes, total):
    rows = stays.buffer.shape[0]
    cols = w_query.buffer.shape[1]
    dpre = dpre()
    for i, w in enumerate((w_query, w_key, w_value, w_gate)):
        w = w()
        for half in (0, 1):
            part = slice(half * rows, (half + 1) * rows)
            term = against(dpre[part, i * cols : (i + 1) * cols], w[...])
            if i == 0:
                total[part, :] = term
            elif i < 3:
                total[part, :] += term
            elif half == 0:
                stays.buffer[...] = total[part, :] + term
            else:
                goes.buffer[...] = (total[part, :] + term).astype(BF16)


def finish_rows(
    scalars, tok, branch, ffn_stays, ffn_came, d_hidden, in_stays, in_came, mixed, input_grad
):
    x = tok()[...].astype(F32)
    ffn = ffn_stays()[...] + ffn_came()[...].astype(F32)
    ok = valid_rows(scalars, 0, x.shape[0])
    mixed.buffer[...] = (x + ok * (branch()[...].astype(F32) + ffn)).astype(BF16)
    mixed.send()
    scale = lax.rsqrt(row_mean(x * x) + EPSILON)
    normed = x * scale
    d_in = in_stays()[...] + in_came()[...].astype(F32)
    input_grad.buffer[...] = d_hidden()[...] + scale * (d_in - normed * row_mean(d_in * normed))


def join_columns(scalars, *refs):
    ins, outs = refs[:8], refs[8:]
    cols = outs[0].buffer.shape[1] // 2
    own = pl.multiple_of(scalars[0] * cols, cols)
    other = pl.multiple_of((1 - scalars[0]) * cols, cols)
    step = 128
    for first, side in ((own, 0), (other, 2)):
        place_at = 0
        for i in range(2):
            total = ins[side + i]()[...].astype(F32) + ins[4 + side + i]()[...].astype(F32)
            for at in range(0, total.shape[1], step):
                lanes = pl.ds(pl.multiple_of(first + place_at % cols, step), step)
                outs[place_at // cols].buffer[:, lanes] = total[:, at : at + step]
                place_at += step


ORDERS = {"D": "yxab", "L": "xbya", "R": "axyb", "X": "axyb", "Y": "yxab"}
WAITS = "RYDRXYLRDXYLDXLYX"


def on_device(
    tokens,
    seq_lens,
    decay_rate,
    w_query,
    w_key,
    w_value,
    w_gate_u,
    w_out,
    w_left,
    w_right,
    w_down,
    cotangent,
):
    n_wide = lax.axis_size("wide")
    bits = n_wide.bit_length() - 1
    tail = list(range(4, bits))
    orders = {c: ["xyab".index(d) for d in dims] + tail for c, dims in ORDERS.items()}
    ffn_orders = [orders[c] for c in "DLR"]
    attn_orders = [orders[c] for c in "XY"]
    rows, width = tokens.shape
    units = w_left.shape[1]
    heads = decay_rate.shape[0] // 2
    size = width // decay_rate.shape[0]
    cols = width // 2
    group = 2 * rows
    c = lax.axis_index("narrow")
    scalars = jnp.stack([c, lax.axis_index("wide"), seq_lens[0, 0]]).astype(jnp.int32)

    def other(v):
        return lax.ppermute(v, "narrow", [(0, 1), (1, 0)])

    def over(v, bit):
        return lax.ppermute(v, "wide", [(i, i ^ (1 << bit)) for i in range(n_wide)])

    def half_cols(s, ref):
        return ref.at[:, pl.ds(pl.multiple_of(s[0] * cols, cols), cols)]

    def half_rows(s, ref):
        return ref.at[pl.ds(pl.multiple_of(s[0] * cols, cols), cols), :]

    halves = (half_cols, (width, cols))
    small = (scalars,)
    tok_other, cot_other = other(tokens), other(cotangent)
    weights = (w_query, w_key, w_value, w_gate_u)
    *held, nin_own, q, k, v, dq, dk, gu, dg, gate = call(
        project_own,
        [here((width, cols))] * 4
        + [here((rows, width))]
        + [here((rows, cols))] * 7
        + [here((rows, cols), F32)],
        small,
        (tokens, *weights),
        parts={i: halves for i in (1, 2, 3, 4)},
        into={1: 0, 2: 1, 3: 2, 4: 3},
        window=3,
        name="project_own",
    )
    u, nin, q, k, v, dq, dk, gu, dg, att, prior, down_held, out_held, left_held = call(
        attention_forward,
        [here((group, cols + 128)), arr((group, width))]
        + [arr((group, cols))] * 8
        + [arr((heads, size, size)), here((units, width))]
        + [here((width, width)), here((width, units))],
        (scalars, decay_rate),
        (nin_own, q, k, v, dq, dk, gu, dg, gate, tok_other, *held, w_down, w_out, w_left),
        into={14: 11, 15: 12, 16: 13},
        inside=(0, 1, 2, 3, 4, 5, 6, 7, 8, 10, 11, 12, 13),
        after=(cot_other,),
        near=(9,),
        scratch=[pltpu.VMEM((group, cols), F32)],
        name="attention_forward",
    )
    u_other = other(u)
    right_held, d_joined, placed_d = call(
        functools.partial(early_products, orders["D"]),
        [here((width, units)), here((group, units), F32), here((width, group))],
        small,
        (cotangent, cot_other, down_held, w_right),
        after=(u,),
        near=(1,),
        inside=(2,),
        into={3: 0},
        scratch=[pltpu.VMEM((group, width), BF16), pltpu.VMEM((width, group), BF16)],
        window=3,
        name="early_products",
    )
    part = here((width // 2, units))
    joined, d_left, d_right, branch, scale, flat, *goes = call(
        functools.partial(feed_forward, ffn_orders),
        [here((group, units))] * 3
        + [arr((group, width)), arr((group, 128), F32), here((width, group))]
        + [part] * 3,
        small,
        (u, u_other, out_held, tokens, tok_other, left_held, right_held, d_joined, placed_d),
        inside=(0, 2, 5, 6, 7, 8),
        near=(1, 4),
        scratch=[pltpu.VMEM((group, width), BF16)] + [pltpu.VMEM((width // 2, group), BF16)] * 2,
        name="feed_forward",
    )
    (mid,) = call(
        mid_gradient,
        [here((group, width))],
        (),
        (d_left, left_held, d_right, right_held),
        inside=(0, 1, 2, 3),
        scratch=[pltpu.VMEM((group, width), F32)],
        name="mid_gradient",
    )
    mid_other = other(mid)
    attn_part = (width // 2, 5 * cols // 2)
    dpre, x_goes, x_stays, y_goes, y_stays, d_hidden = call(
        functools.partial(attention_backward, attn_orders),
        [here((group, 4 * cols))]
        + [here(attn_part)] * 4
        + [arr((rows, width), F32)],
        (scalars, decay_rate),
        (mid, mid_other, tokens, tok_other, cotangent, cot_other, branch, w_out, scale)
        + (gu, dg, att, u, u_other, q, k, v, prior, dq, dk, nin),
        parts={7: (half_rows, (cols, width))},
        inside=(0,),
        near=(1, 3, 5, 12, 13),
        window=8,
        scratch=[pltpu.VMEM((group, cols), BF16)]
        + [pltpu.VMEM((group, width), BF16)] * 2
        + [pltpu.VMEM((width, group), BF16)] * 5,
        slack=4,
        name="attention_backward",
    )
    ffn_stays, ffn_goes, *stays = call(
        functools.partial(down_and_staying, ffn_orders),
        [here((rows, width), F32), here((rows, width))] + [part] * 3,
        small,
        (down_held, placed_d, flat, joined, d_left, d_right),
        inside=range(6),
        after=(dpre,),
        scratch=[pltpu.VMEM((width // 2, group), BF16)] * 2,
        name="down_and_staying",
    )
    ffn_came = other(ffn_goes)
    in_stays, in_goes = call(
        input_gradient,
        [arr((rows, width), F32), here((rows, width))],
        small,
        (dpre, w_query, w_key, w_value, w_gate_u),
        inside=(0,),
        after=(stays[0],),
        parts={i: halves for i in (1, 2, 3, 4)},
        scratch=[pltpu.VMEM((group, width), F32)],
        name="input_gradient",
    )
    in_came = other(in_goes)

    held_parts = dict(zip("DLR", zip(stays, goes)))
    held_parts.update(X=(x_stays, x_goes), Y=(y_stays, y_goes))

    def add(chunk, came):
        stays = held_parts[chunk][0]
        total = stays.astype(F32) + came.astype(F32)
        half = total.shape[0] // 2
        held_parts[chunk] = total[:half].astype(BF16), total[half:].astype(BF16)
        return held_parts[chunk][1]

    first = [over(held_parts[c][1], orders[c][0]) for c in "RDL"]
    *first, last = lax.optimization_barrier((*first, in_stays))
    for chunk, came in zip("RDL", first):
        came, last = lax.optimization_barrier((came, last))
        last = add(chunk, came)
    mixed, input_grad = call(
        finish_rows,
        [arr((rows, width)), arr((rows, width), F32)],
        small,
        (tokens, branch, ffn_stays, ffn_came, d_hidden, in_stays, in_came),
        after=(last,),
        parts={1: (lambda s, ref: ref.at[pl.ds(0, rows), :], (rows, width))},
        near=(2, 3, 6),
        window=7,
        name="finish_rows",
    )
    last = mixed
    arrived, full = {}, {}
    done = dict(D=1, L=1, R=1, X=0, Y=0)
    for chunk in WAITS:
        first = done[chunk]
        done[chunk] += 1
        for phase in range(first, bits if first == 3 else first + 1):
            came = over(held_parts[chunk][1], orders[chunk][phase])
            came, last = lax.optimization_barrier((came, last))
            if phase == bits - 1:
                arrived[chunk] = last = came
                if chunk in "DLR":
                    last = full[chunk] = held_parts[chunk][0].astype(F32) + came.astype(F32)
            else:
                last = add(chunk, came)
    slab = width // n_wide
    stays = [held_parts[c][0] for c in "XY"]
    came = [arrived[c] for c in "XY"]
    joint = call(
        join_columns,
        [arr((slab, width), F32)] * 5,
        small,
        (*stays, *map(other, stays), *came, *map(other, came)),
        inside=range(8),
        name="join_columns",
    )
    grad_left, grad_right, grad_down = full["L"], full["R"], full["D"].T
    return (mixed, input_grad, *joint, grad_left, grad_right, grad_down)


def solution(mesh):
    placed = (
        P(("wide", "narrow"), None),
        P("wide", None),
        P(),
        P(),
        P(),
        P(),
        P(),
        P(),
        P(None, "narrow"),
        P(None, "narrow"),
        P("narrow", None),
        P(("wide", "narrow"), None),
    )
    return jax.shard_map(
        on_device,
        mesh=mesh,
        in_specs=placed,
        out_specs=(
            P(("wide", "narrow"), None),
            P(("wide", "narrow"), None),
            P("wide", None),
            P("wide", None),
            P("wide", None),
            P("wide", None),
            P("wide", None),
            P("wide", "narrow"),
            P("wide", "narrow"),
            P("narrow", "wide"),
        ),
        check_vma=False,
    )
```
